32 devices in a mesh: groups: 2 (over x), tm: 16 (over z, y, core).
Axes of the slice: x: 2, y: 2, z: 4, core: 2. Of those that a mesh axis runs over, the one named last changes fastest.
Arguments:
- latent: bfloat16 [16384, 384], P(('groups', 'tm')), parts along dimension 0, may hold values from -45 to 45
- owner: int32 [16384], P(('groups', 'tm')), parts along dimension 0, may hold values from 0 to 15, as said below
- frame_counts: int32 [16], P('groups'), parts along dimension 0, may hold values from 1 to 8, 32 in all
- norm_gain: float32 [384], replicated, may hold values from 0.1 to 1.9
- norm_shift: float32 [384], replicated, may hold values from -3 to 3
- res_kernel: bfloat16 [3, 3, 3, 384, 384], replicated, may hold values from -0.0625 to 0.0625
- res_bias: float32 [384], replicated, may hold values from -3 to 3
- time_kernel: bfloat16 [3, 384, 768], replicated, may hold values from -0.1875 to 0.1875
- time_bias: float32 [768], replicated, may hold values from -3 to 3
- up_kernel: bfloat16 [3, 3, 384, 192], replicated, may hold values from -0.109375 to 0.109375
- up_bias: float32 [192], replicated, may hold values from -3 to 3
Outputs:
- frames_out: bfloat16 [128, 32, 6144], P(('groups', 'tm')), parts along dimension 0
The draws below stay inside these ranges and needn't reach their ends.
There are 2 independent parts, one for each index of `groups`. The reference program is written for one: setup_inputs(seed, part) draws one part's arguments, and reference() takes and returns one part's arrays. A program takes and returns all parts, laid end to end along the dimension named above; an argument that names none is the same for every part. Nothing has to cross between parts.
Inputs may be any that keep to these rules, and one draw needn't show every extreme that they name: Each device's block of 512 tokens holds at most 64 tokens for any one owner, some block holds exactly 64 for one owner, and every device is the owner of exactly 512 tokens.
All inputs are finite; a program needn't handle non-finite values.
Results may differ from the reference program's by a relative error of at most 0.0057.
Values may be sent and summed in bfloat16 or wider, within the bound.
No kernel may reach another device: no remote copies, remote signals or barrier semaphores. Data moves between devices by JAX's collectives and lax.ppermute only.
A program may use at most 128 MiB of HBM per device.

```python
import math
import jax
import jax.numpy as jnp
import numpy as np
from jax import lax

C = 384
OC = 192
VIDEOS = 8
FR_DEV = 2
H = 16
W = 16
TC = 768
FRAMES = 32
N_TM = 16


def owner_table(key):
    peer_count = N_TM
    token_count = FR_DEV * H * W
    capacity = 2 * token_count // peer_count
    half_count = peer_count // 2
    first_key, second_key, third_key = jax.random.split(jax.random.fold_in(key, 11), 3)
    swings = jax.random.randint(first_key, (half_count,), -(capacity // 2), capacity // 2 + 1)
    summit = jax.random.randint(second_key, (), 0, half_count)
    swings = jnp.where(jnp.arange(half_count) == summit, capacity // 2, swings)
    distance = (jnp.arange(peer_count)[:, None] - jnp.arange(peer_count)[None, :]) % peer_count
    polarity = jnp.where(distance % 2 == 0, 1, -1)
    counts = capacity // 2 + polarity * swings[distance // 2]
    bounds = jnp.cumsum(counts, 1)
    orders = jax.vmap(lambda single: jax.random.permutation(single, token_count))(jax.random.split(third_key, peer_count))
    owners = jnp.sum((bounds[:, None, :] <= orders[:, :, None]).astype(jnp.int32), 2)
    return owners.reshape(-1).astype(jnp.int32)


def draw_owner(key, part):
    return owner_table(key)


def draw_latent(key, part):
    owners = owner_table(key)
    ranking = jnp.argsort(owners, stable=True)
    base_key, channel_key, pixel_key = jax.random.split(jax.random.fold_in(key, 23), 3)
    frame_count = FR_DEV * N_TM
    values = jax.random.truncated_normal(base_key, -3.0, 3.0, (frame_count, H * W, C), jnp.float32)
    pixel_scale = jnp.exp(jax.random.uniform(pixel_key, (frame_count, H * W, 1), jnp.float32, jnp.log(0.5), jnp.log(5.0)))
    channel_scale = jnp.exp(jax.random.uniform(channel_key, (C,), jnp.float32, jnp.log(0.5), jnp.log(5.0)))
    frame_scale = 3.0 ** (jnp.arange(frame_count, dtype=jnp.float32) / max(frame_count - 1, 1))
    values = 0.2 * values * channel_scale * pixel_scale * frame_scale[:, None, None]
    flattened = values.reshape(frame_count * H * W, C)
    return jnp.zeros_like(flattened).at[ranking].set(flattened).astype(jnp.bfloat16)


def split_up(amount, total, reach, slope):
    loads = [(1 << 20) // math.isqrt(standing ** slope) + 1 for standing in range(2, amount + 1)]
    rest, holding = total - reach - (amount - 1), [1] * (amount - 1)
    while rest > 0:
        free = [i for i in range(amount - 1) if holding[i] < reach]
        mass, budget = sum([loads[i] for i in free]), rest
        for i in free:
            extra = min(reach - holding[i], max(1, budget * loads[i] // mass), rest)
            holding[i] = holding[i] + extra
            rest = rest - extra
    return np.array([reach] + holding)


def uneven_parts(key, count, total, reach, lean):
    if count == 2:
        one = jax.random.randint(key, (), max(1, total - reach), min(reach, total - 1) + 1)
        return jnp.stack([one, total - one])
    tallies = jnp.asarray(split_up(count, total, reach, lean), jnp.int32)
    couples = (count - 1) // 2
    source_of, taker = tallies[1:1 + 2 * couples:2], tallies[2:2 + 2 * couples:2]
    room = jnp.minimum(source_of - 1, reach - taker)
    moved = jax.random.randint(jax.random.fold_in(key, 1), (couples,), 0, 1 << 20) % (room + 1)
    tallies = tallies.at[1:1 + 2 * couples:2].set(source_of - moved).at[2:2 + 2 * couples:2].set(taker + moved)
    return tallies[jax.random.permutation(jax.random.fold_in(key, 2), count)]


def noise(own_key, shape, spread, most, kind=jnp.bfloat16):
    return jnp.clip(spread * jax.random.normal(own_key, shape, jnp.float32), -most, most).astype(kind)


def setup_inputs(seed: int = 0, part: int = 0) -> dict:
    key_list = jax.random.split(jax.random.key(seed), 12)
    own_keys = jax.random.split(jax.random.fold_in(key_list[11], part), 12)
    latent = draw_latent(jax.random.fold_in(jax.random.fold_in(key_list[11], part), 71), part)
    owner = draw_owner(jax.random.fold_in(jax.random.fold_in(key_list[11], part), 71), part)
    frame_counts = uneven_parts(own_keys[2], VIDEOS, FRAMES, FRAMES // 4, 2).astype(jnp.int32)
    norm_gain = jnp.clip(1.0 + 0.18 * jax.random.normal(key_list[3], (C,), jnp.float32), 0.1, 1.9)
    norm_shift = noise(key_list[4], (C,), 0.5, 3.0, jnp.float32)
    res_kernel = noise(key_list[5], (3, 3, 3, C, C), (27 * C) ** -0.5, 0.0625)
    res_bias = noise(key_list[6], (C,), 0.5, 3.0, jnp.float32)
    time_kernel = noise(key_list[7], (3, C, TC), (3 * C) ** -0.5, 0.1875)
    time_bias = noise(key_list[8], (TC,), 0.5, 3.0, jnp.float32)
    up_kernel = noise(key_list[9], (3, 3, C, OC), (9 * C) ** -0.5, 0.109375)
    up_bias = noise(key_list[10], (OC,), 0.5, 3.0, jnp.float32)
    return {"latent": latent, "owner": owner, "frame_counts": frame_counts, "norm_gain": norm_gain, "norm_shift": norm_shift, "res_kernel": res_kernel, "res_bias": res_bias, "time_kernel": time_kernel, "time_bias": time_bias, "up_kernel": up_kernel, "up_bias": up_bias}


epsilon = 1e-06

def video_starts_of(frame_ids, frame_counts):
    video_ends = jnp.cumsum(frame_counts).astype(jnp.int32)
    video_starts = (video_ends - frame_counts).astype(jnp.int32)
    passed = lax.optimization_barrier(jnp.sum((video_ends[None, :] <= frame_ids[:, None]).astype(jnp.int32), 1)).astype(jnp.int32)
    member = jnp.minimum(passed, VIDEOS - 1)
    chosen = member[:, None] == jnp.arange(VIDEOS, dtype=jnp.int32)[None, :]
    return lax.optimization_barrier(jnp.sum(jnp.where(chosen, video_starts[None, :], 0), 1)).astype(jnp.int32)

def spatial_taps(frame_block, kernel):
    frames, height, columns, channels_in = frame_block.shape
    padded = jnp.pad(frame_block, ((0, 0), (1, 1), (1, 1), (0, 0)))
    summed = jnp.zeros((frames * height * columns, kernel.shape[-1]), jnp.float32)
    for row_tap in range(3):
        for col_tap in range(3):
            window = padded[:, row_tap:row_tap + height, col_tap:col_tap + columns, :]
            summed = summed + jnp.dot(window.reshape(-1, channels_in), kernel[row_tap, col_tap], preferred_element_type=jnp.float32)
    return summed

def causal_shift(field, starts, offset):
    frame_count = field.shape[0]
    moved = jnp.concatenate([jnp.zeros((offset,) + field.shape[1:], field.dtype), field[:frame_count - offset]], 0)
    keeping = (jnp.arange(frame_count, dtype=jnp.int32) - offset >= starts).astype(field.dtype)
    return moved * keeping.reshape((frame_count,) + (1,) * (field.ndim - 1))

def reference(latent, owner, frame_counts, norm_gain, norm_shift, res_kernel, res_bias, time_kernel, time_bias, up_kernel, up_bias):
    ranking = jnp.argsort(owner, stable=True)
    decoded = latent[ranking].reshape(FRAMES, H, W, C)
    starts = video_starts_of(jnp.arange(FRAMES, dtype=jnp.int32), frame_counts)
    values = decoded.astype(jnp.float32)
    squares = lax.optimization_barrier(jnp.mean(values * values, -1, keepdims=True))
    scaled = values * lax.rsqrt(squares + epsilon)
    activated = jax.nn.silu(scaled * norm_gain + norm_shift).astype(jnp.bfloat16)
    conv_sum = jnp.zeros((FRAMES * H * W, C), jnp.float32)
    for time_tap in range(3):
        conv_sum = conv_sum + spatial_taps(causal_shift(activated, starts, 2 - time_tap), res_kernel[time_tap])
    residual = (values.reshape(-1, C) + res_bias + conv_sum).astype(jnp.bfloat16).reshape(FRAMES, H, W, C)
    temporal = jnp.zeros((FRAMES * H * W, TC), jnp.float32)
    for time_tap in range(3):
        shifted = causal_shift(residual, starts, 2 - time_tap).reshape(-1, C)
        temporal = temporal + jnp.dot(shifted, time_kernel[time_tap], preferred_element_type=jnp.float32)
    temporal = (temporal + time_bias).astype(jnp.bfloat16)
    doubled = temporal.reshape(FRAMES, H, W, 2, C).transpose(0, 3, 1, 2, 4).reshape(2 * FRAMES, H, W, C)
    blocks = doubled.reshape(N_TM, 2 * FR_DEV, H, W, C)

    def upscale(frame_block):
        enlarged = jnp.repeat(jnp.repeat(frame_block, 2, axis=1), 2, axis=2)
        summed = spatial_taps(enlarged, up_kernel) + up_bias
        return summed.astype(jnp.bfloat16).reshape(2 * FR_DEV, 2 * H, 2 * W * OC)
    return lax.map(upscale, blocks).reshape(2 * FRAMES, 2 * H, 2 * W * OC)
```

```python
import functools

import jax
import jax.numpy as jnp
from jax import lax
from jax.experimental import pallas as pl
from jax.experimental.pallas import tpu as pltpu
from jax.sharding import PartitionSpec as P

H = 16
W = 16
MARK = 128.0
epsilon = 1e-06
MIB = 1 << 20
f32 = jnp.float32
bf16 = jnp.bfloat16


def in_vmem(value):
    return pltpu.with_memory_space_constraint(value, pltpu.VMEM)


VM = pl.BlockSpec(memory_space=pltpu.VMEM)
SM = pl.BlockSpec(memory_space=pltpu.SMEM)


def iota(shape, dim):
    return lax.broadcasted_iota(jnp.int32, shape, dim)


def mm(lhs, rhs):
    return jnp.dot(lhs, rhs, preferred_element_type=f32)


def from_behind(value, axis, by):
    size = lax.axis_size(axis)
    pairs = [(i, i + by) for i in range(size) if 0 <= i + by < size]
    return lax.ppermute(value, axis, pairs)


def pack_kernel(owner_ref, latent_ref, out_ref, *, peers, capacity):
    tokens = latent_ref.shape[0]
    owner = owner_ref[...]
    marked = iota((peers, tokens), 0) == owner
    upper = (iota((tokens, tokens), 0) <= iota((tokens, tokens), 1)).astype(bf16)
    running = mm(marked.astype(bf16), upper)
    rank = jnp.sum(jnp.where(marked, running - 1.0, 0.0), 0, keepdims=True)
    slot = owner * capacity + rank.astype(jnp.int32)
    chosen = (iota((peers * capacity, tokens), 0) == slot).astype(bf16)
    rows = mm(chosen, latent_ref[...])
    filled = mm(chosen, jnp.ones((tokens, 128), bf16))
    empty = jnp.concatenate([(1.0 - filled) * MARK] * (rows.shape[1] // 128), 1)
    out_ref[...] = (rows + empty).astype(bf16)


def unpack_kernel(
    got_ref, gain_ref, shift_ref, decoded_ref, active_ref, *, peers, capacity
):
    slots, channels = got_ref.shape
    tokens = decoded_ref.shape[0]
    present = (got_ref[:, :128] < MARK / 2).astype(bf16)
    slot_of = iota((peers, slots), 1)
    member = (slot_of // capacity == iota((peers, slots), 0)).astype(bf16)
    counts = mm(member, present)
    below = (iota((peers, peers), 1) < iota((peers, peers), 0)).astype(f32)
    before = jnp.dot(below, counts, precision=lax.Precision.HIGHEST, preferred_element_type=f32)
    member32 = member.astype(f32)
    first = jnp.sum(member32 * before[:, :1], 0, keepdims=True).astype(jnp.int32)
    held = jnp.sum(member32 * counts[:, :1], 0, keepdims=True).astype(jnp.int32)
    within = iota((1, slots), 1) % capacity
    place = jnp.where(within < held, first + within, -1)
    row = iota((tokens, slots), 0)
    pixel = row % (H * W)
    source = row - pixel + (pixel % H) * W + pixel // H
    chosen = (source == place).astype(bf16)
    values = mm(chosen, got_ref[...])
    decoded_ref[...] = values.astype(bf16)
    squares = jnp.mean(values * values, -1, keepdims=True)
    scaled = values * lax.rsqrt(squares + epsilon)
    fed = scaled * gain_ref[...] + shift_ref[...]
    active_ref[...] = (fed / (1.0 + jnp.exp(-fed))).astype(bf16)


def vertical(frame):
    wide = frame.astype(f32)
    y = iota(wide.shape, 0) % H
    up = jnp.where(y == 0, 0.0, pltpu.roll(wide, 1, 0))
    down = jnp.where(y == H - 1, 0.0, pltpu.roll(wide, wide.shape[0] - 1, 0))
    return up.astype(bf16), frame, down.astype(bf16)


def patches(frame, out_ref, first):
    pixels, channels = frame.shape
    nothing = jnp.zeros((H, channels), bf16)
    for a, shifted in enumerate(vertical(frame)):
        for b in range(3):
            if b == 0:
                moved = jnp.concatenate([nothing, shifted[: pixels - H]], 0)
            elif b == 1:
                moved = shifted
            else:
                moved = jnp.concatenate([shifted[H:], nothing], 0)
            at = (a * 3 + b) * channels
            out_ref[first : first + pixels, at : at + channels] = moved


def keeps(counts_ref, position_ref):
    first = position_ref[0] * 2
    starts = [jnp.int32(0), jnp.int32(0)]
    end = jnp.int32(0)
    for video in range(counts_ref.shape[0]):
        end = end + counts_ref[video]
        starts = [jnp.where(end <= first + f, end, starts[f]) for f in range(2)]
    return [
        [(first + f - back >= starts[f]).astype(f32) for back in range(3)] for f in range(2)
    ]


def local_conv_kernel(counts_ref, position_ref, active_ref, kernel_ref, out_ref, near):
    pixels = H * W
    keep = keeps(counts_ref, position_ref)
    for f in range(2):
        patches(active_ref[f * pixels : (f + 1) * pixels, :], near, f * pixels)
    own = mm(near[...], kernel_ref[2])
    out_ref[:pixels] = own[:pixels]
    out_ref[pixels:] = own[pixels:] + keep[1][1] * mm(near[:pixels], kernel_ref[1])


def residual_kernel(
    counts_ref, position_ref, prior_ref, kernel_ref, local_ref, decoded_ref, bias_ref, out_ref, near
):
    pixels = H * W
    keep = keeps(counts_ref, position_ref)
    for f in range(2):
        patches(prior_ref[f * pixels : (f + 1) * pixels, :], near, f * pixels)
    far = mm(near[...], kernel_ref[0])
    behind = mm(near[pixels:], kernel_ref[1])
    base = local_ref[...] + decoded_ref[...].astype(f32) + bias_ref[...]
    out_ref[:pixels] = (base[:pixels] + keep[0][2] * far[:pixels] + keep[0][1] * behind).astype(bf16)
    out_ref[pixels:] = (base[pixels:] + keep[1][2] * far[pixels:]).astype(bf16)


def local_time_kernel(counts_ref, position_ref, residual_ref, kernel_ref, bias_ref, out_ref):
    pixels = H * W
    keep = keeps(counts_ref, position_ref)
    own = mm(residual_ref[...], kernel_ref[2]) + bias_ref[...]
    out_ref[:pixels] = own[:pixels]
    out_ref[pixels:] = own[pixels:] + keep[1][1] * mm(residual_ref[:pixels], kernel_ref[1])


def up_kernel_body(
    counts_ref, position_ref, prior_ref, kernel_ref, local_ref, folded_ref, bias_ref, out_ref,
    near, rows32,
):
    pixels = H * W
    channels = prior_ref.shape[1]
    outs = bias_ref.shape[1]
    keep = keeps(counts_ref, position_ref)
    step = pl.program_id(0)

    @pl.when(step == 0)
    def _():
        far = mm(prior_ref[...], kernel_ref[0])
        behind = mm(prior_ref[pixels:], kernel_ref[1])
        first = local_ref[:pixels] + keep[0][2] * far[:pixels] + keep[0][1] * behind
        second = local_ref[pixels:] + keep[1][2] * far[pixels:]
        for f, wide in enumerate((first, second)):
            temporal = wide.astype(bf16)
            for half in range(2):
                e = 2 * f + half
                near[e, :H] = jnp.zeros((H, 3 * channels), bf16)
                near[e, H + pixels :] = jnp.zeros((H, 3 * channels), bf16)
                frame = temporal[:, half * channels : (half + 1) * channels]
                for a, shifted in enumerate(vertical(frame)):
                    near[e, H : H + pixels, a * channels : (a + 1) * channels] = shifted

    for p in range(2):
        phases = []
        for q in range(2):
            total = bias_ref[...] + jnp.zeros((pixels, outs), f32)
            for side in range(2):
                window = near[
                    step,
                    (q + side) * H : (q + side) * H + pixels,
                    p * channels : (p + 2) * channels,
                ]
                total = total + mm(window, folded_ref[q, side, p])
            phases.append(total)
        both = jnp.concatenate(phases, 1)
        blocks = 2 * outs // 128
        for x in range(W):
            for block in range(blocks):
                rows32[x * blocks + block, pl.ds(p, H, stride=2)] = both[
                    x * H : (x + 1) * H, block * 128 : (block + 1) * 128
                ]
    for block in range(rows32.shape[0]):
        out_ref[0, :, block * 128 : (block + 1) * 128] = rows32[block].astype(bf16)


def fold(up_kernel):
    taps = up_kernel.astype(f32)
    rows = jnp.stack(
        [jnp.stack([taps[0], taps[1] + taps[2]]), jnp.stack([taps[0] + taps[1], taps[2]])]
    )
    left = rows[:, :, 0], rows[:, :, 1] + rows[:, :, 2]
    right = rows[:, :, 0] + rows[:, :, 1], rows[:, :, 2]
    whole = jnp.stack([jnp.stack(left), jnp.stack(right)]).astype(bf16)
    return whole.reshape(2, 2, 2, 2 * taps.shape[2], taps.shape[3])


def on_device(
    latent,
    owner,
    frame_counts,
    norm_gain,
    norm_shift,
    res_kernel,
    res_bias,
    time_kernel,
    time_bias,
    up_kernel,
    up_bias,
):
    peers = lax.axis_size("tm")
    position = lax.axis_index("tm").astype(jnp.int32).reshape(1)
    tokens, channels = latent.shape
    capacity = 2 * tokens // peers
    pixels = H * W
    wide = time_kernel.shape[-1]
    outs = up_kernel.shape[-1]
    kernel = res_kernel.reshape(3, 9 * channels, channels)
    folded = fold(up_kernel)

    packed = pl.pallas_call(
        functools.partial(pack_kernel, peers=peers, capacity=capacity),
        out_shape=pltpu.VMEM((peers * capacity, channels), bf16),
        in_specs=[VM, VM],
        out_specs=VM,
        compiler_params=pltpu.CompilerParams(vmem_limit_bytes=16 * MIB),
        name="pack",
    )(owner.reshape(1, tokens), latent)
    received = lax.all_to_all(packed, "tm", split_axis=0, concat_axis=0, tiled=True)
    decoded, active = pl.pallas_call(
        functools.partial(unpack_kernel, peers=peers, capacity=capacity),
        out_shape=[pltpu.VMEM((tokens, channels), bf16)] * 2,
        in_specs=[VM] * 3,
        out_specs=[VM] * 2,
        compiler_params=pltpu.CompilerParams(vmem_limit_bytes=16 * MIB),
        name="unpack",
    )(in_vmem(received), norm_gain.reshape(1, channels), norm_shift.reshape(1, channels))
    prior = from_behind(active, "tm", 1)
    kernel = in_vmem(kernel)
    local = pl.pallas_call(
        local_conv_kernel,
        out_shape=pltpu.VMEM((tokens, channels), f32),
        in_specs=[SM, SM, VM, VM],
        out_specs=VM,
        scratch_shapes=[pltpu.VMEM((tokens, 9 * channels), bf16)],
        compiler_params=pltpu.CompilerParams(vmem_limit_bytes=16 * MIB),
        cost_estimate=pl.CostEstimate(
            flops=6 * pixels * 9 * channels * channels, bytes_accessed=0, transcendentals=0
        ),
        name="local_conv",
    )(frame_counts, position, in_vmem(active), kernel)
    residual = pl.pallas_call(
        residual_kernel,
        out_shape=pltpu.VMEM((tokens, channels), bf16),
        in_specs=[SM, SM] + [VM] * 5,
        out_specs=VM,
        scratch_shapes=[pltpu.VMEM((tokens, 9 * channels), bf16)],
        compiler_params=pltpu.CompilerParams(vmem_limit_bytes=16 * MIB),
        name="residual",
    )(
        frame_counts,
        position,
        in_vmem(prior),
        kernel,
        in_vmem(local),
        in_vmem(decoded),
        res_bias.reshape(1, channels),
    )
    prior_residual = from_behind(residual, "tm", 1)
    time_kernel = in_vmem(time_kernel)
    local_time = pl.pallas_call(
        local_time_kernel,
        out_shape=pltpu.VMEM((tokens, wide), f32),
        in_specs=[SM, SM] + [VM] * 3,
        out_specs=VM,
        compiler_params=pltpu.CompilerParams(vmem_limit_bytes=16 * MIB),
        cost_estimate=pl.CostEstimate(
            flops=6 * pixels * channels * wide, bytes_accessed=0, transcendentals=0
        ),
        name="local_time",
    )(frame_counts, position, in_vmem(residual), time_kernel, time_bias.reshape(1, wide))
    frames = 2 * tokens // pixels
    return pl.pallas_call(
        up_kernel_body,
        out_shape=jax.ShapeDtypeStruct((frames, 2 * H, 2 * W * outs), bf16),
        grid=(frames,),
        in_specs=[SM, SM] + [VM] * 5,
        out_specs=pl.BlockSpec((1, 2 * H, 2 * W * outs), lambda e: (e, 0, 0)),
        scratch_shapes=[
            pltpu.VMEM((frames, 2 * H + pixels, 3 * channels), bf16),
            pltpu.VMEM((2 * W * outs // 128, 2 * H, 128), f32),
        ],
        compiler_params=pltpu.CompilerParams(vmem_limit_bytes=20 * MIB),
        name="upscale",
    )(
        frame_counts,
        position,
        in_vmem(prior_residual),
        time_kernel,
        in_vmem(local_time),
        in_vmem(folded),
        up_bias.reshape(1, outs),
    )


def solution(mesh):
    placed = (
        P(("groups", "tm"), None),
        P(("groups", "tm")),
        P("groups"),
        P(),
        P(),
        P(),
        P(),
        P(),
        P(),
        P(),
        P(),
    )
    return jax.shard_map(
        on_device,
        mesh=mesh,
        in_specs=placed,
        out_specs=P(("groups", "tm"), None, None),
        check_vma=False,
    )
```

```python
import functools

import jax
import jax.numpy as jnp
from jax import lax
from jax.experimental import pallas as pl
from jax.experimental.pallas import tpu as pltpu
from jax.sharding import PartitionSpec as P

H = 16
W = 16
MARK = 128.0
epsilon = 1e-06
MIB = 1 << 20
f32 = jnp.float32
bf16 = jnp.bfloat16


def in_vmem(value):
    return pltpu.with_memory_space_constraint(value, pltpu.VMEM)


def in_hbm(value):
    return pltpu.with_memory_space_constraint(value, pltpu.HBM)


VM = pl.BlockSpec(memory_space=pltpu.VMEM)
HB = pl.BlockSpec(memory_space=pltpu.HBM)
SM = pl.BlockSpec(memory_space=pltpu.SMEM)


def iota(shape, dim):
    return lax.broadcasted_iota(jnp.int32, shape, dim)


def mm(lhs, rhs):
    return jnp.dot(lhs, rhs, preferred_element_type=f32)


def from_behind(value, axis):
    size = lax.axis_size(axis)
    return lax.ppermute(value, axis, [(i, (i + 1) % size) for i in range(size)])


def pack_kernel(
    owner_hbm, latent_hbm, out_hbm, owner_ref, wide_ref, made_ref, arrived, left, *, peers, capacity
):
    tokens, channels = latent_hbm.shape
    copies = [
        pltpu.make_async_copy(owner_hbm, owner_ref, arrived.at[0]),
        pltpu.make_async_copy(latent_hbm, wide_ref.at[:, :channels], arrived.at[1]),
    ]
    for copy in copies:
        copy.start()
    wide_ref[:, channels:] = jnp.ones((tokens, 128), bf16)
    upper = (iota((tokens, tokens), 0) <= iota((tokens, tokens), 1)).astype(bf16)
    copies[0].wait()
    owner = owner_ref[...]
    marked = iota((peers, tokens), 0) == owner
    running = mm(marked.astype(bf16), upper)
    rank = jnp.sum(jnp.where(marked, running - 1.0, 0.0), 0, keepdims=True)
    slot = owner * capacity + rank.astype(jnp.int32)
    copies[1].wait()
    pieces = left.shape[0]
    rows = peers * capacity // pieces
    sent = []
    for piece in range(pieces):
        at = pl.ds(piece * rows, rows)
        chosen = (iota((rows, tokens), 0) + piece * rows == slot).astype(bf16)
        found = mm(chosen, wide_ref[...])
        empty = (1.0 - found[:, channels:]) * MARK
        made_ref[at] = (
            found[:, :channels] + jnp.concatenate([empty] * (channels // 128), 1)
        ).astype(bf16)
        copy = pltpu.make_async_copy(made_ref.at[at], out_hbm.at[at], left.at[piece])
        copy.start()
        sent.append(copy)
    for copy in sent:
        copy.wait()


def unpack_kernel(
    got_ref, small_ref, taps_hbm, decoded_ref, active_ref, taps_ref, arrived,
    *, peers, capacity, frame,
):
    copy = pltpu.make_async_copy(
        taps_hbm.at[1, pl.ds(frame * taps_ref.shape[0], taps_ref.shape[0])], taps_ref, arrived
    )
    copy.start()
    slots, channels = got_ref.shape
    pixels = decoded_ref.shape[0]
    present = (got_ref[:, :128] < MARK / 2).astype(bf16)
    slot_of = iota((peers, slots), 1)
    member = (slot_of // capacity == iota((peers, slots), 0)).astype(bf16)
    counts = mm(member, present)
    below = (iota((peers, peers), 1) < iota((peers, peers), 0)).astype(f32)
    before = jnp.dot(below, counts, precision=lax.Precision.HIGHEST, preferred_element_type=f32)
    member32 = member.astype(f32)
    first = jnp.sum(member32 * before[:, :1], 0, keepdims=True).astype(jnp.int32)
    held = jnp.sum(member32 * counts[:, :1], 0, keepdims=True).astype(jnp.int32)
    within = iota((1, slots), 1) % capacity
    place = jnp.where(within < held, first + within, -1)
    pixel = iota((pixels, slots), 0)
    source = frame * pixels + (pixel % H) * W + pixel // H
    chosen = (source == place).astype(bf16)
    values = mm(chosen, got_ref[...])
    decoded_ref[...] = values.astype(bf16)
    squares = jnp.mean(values * values, -1, keepdims=True)
    scaled = values * lax.rsqrt(squares + epsilon)
    fed = scaled * small_ref[0:1, :channels] + small_ref[1:2, :channels]
    active_ref[...] = (fed / (1.0 + jnp.exp(-fed))).astype(bf16)
    copy.wait()


def vertical(frame):
    wide = frame.astype(f32)
    y = iota(wide.shape, 0) % H
    up = jnp.where(y == 0, 0.0, pltpu.roll(wide, 1, 0))
    down = jnp.where(y == H - 1, 0.0, pltpu.roll(wide, wide.shape[0] - 1, 0))
    return up.astype(bf16), frame, down.astype(bf16)


def patches(frame):
    pixels, channels = frame.shape
    nothing = jnp.zeros((H, channels), bf16)
    parts = []
    for shifted in vertical(frame):
        parts.append(jnp.concatenate([nothing, shifted[: pixels - H]], 0))
        parts.append(shifted)
        parts.append(jnp.concatenate([shifted[H:], nothing], 0))
    return jnp.concatenate(parts, 1)


def kept(keep_ref):
    return [[keep_ref[3 * f + back : 3 * f + back + 1, :1] for back in range(3)] for f in range(2)]


def halved(near, low_ref, high_ref):
    half = low_ref.shape[0]
    return mm(near[:, :half], low_ref[...]) + mm(near[:, half:], high_ref[...])


def local_conv_kernel(
    keep_ref, first_ref, second_ref, low_ref, high_ref, here_ref, taps_hbm, time_hbm,
    sum0_ref, sum1_ref, taps_ref, time_ref,
    near, arrived,
):
    copies = [
        pltpu.make_async_copy(taps_hbm.at[0], taps_ref, arrived.at[0]),
        pltpu.make_async_copy(time_hbm, time_ref, arrived.at[1]),
    ]
    for copy in copies:
        copy.start()
    pixels = H * W
    keep = kept(keep_ref)
    near[:pixels] = patches(first_ref[...])
    near[pixels:] = patches(second_ref[...])
    own = mm(near[...], here_ref[...])
    sum0_ref[...] = own[:pixels]
    sum1_ref[...] = own[pixels:] + keep[1][1] * halved(near[:pixels], low_ref, high_ref)
    for copy in copies:
        copy.wait()


def second_residual_kernel(
    keep_ref, small_ref, prior_ref, taps_ref, sum_ref, decoded_ref, folded_hbm,
    out_ref, near_ref, folded_ref,
    arrived,
):
    copy = pltpu.make_async_copy(folded_hbm.at[0], folded_ref, arrived)
    copy.start()
    keep = kept(keep_ref)
    near_ref[...] = patches(prior_ref[...])
    base = sum_ref[...] + decoded_ref[...].astype(f32) + small_ref[2:3, : out_ref.shape[1]]
    out_ref[...] = (base + keep[1][2] * mm(near_ref[...], taps_ref[...])).astype(bf16)
    copy.wait()


def behind_kernel(
    keep_ref, small_ref, near_ref, low_ref, high_ref, sum_ref, decoded_ref, folded_hbm,
    out_ref, folded_ref,
    arrived,
):
    copy = pltpu.make_async_copy(folded_hbm.at[1], folded_ref, arrived)
    copy.start()
    keep = kept(keep_ref)
    base = sum_ref[...] + decoded_ref[...].astype(f32) + small_ref[2:3, : out_ref.shape[1]]
    out_ref[...] = base + keep[0][1] * halved(near_ref[...], low_ref, high_ref)
    copy.wait()


def first_residual_kernel(keep_ref, prior_ref, taps_ref, sum_ref, out_ref, near):
    keep = kept(keep_ref)
    near[...] = patches(prior_ref[...])
    out_ref[...] = (sum_ref[...] + keep[0][2] * mm(near[...], taps_ref[...])).astype(bf16)


def local_time_kernel(
    keep_ref, small_ref, first_ref, second_ref, time_ref, sum0_ref, sum1_ref
):
    keep = kept(keep_ref)
    bias = small_ref[3:4, : sum0_ref.shape[1]]
    sum0_ref[...] = mm(first_ref[...], time_ref[2]) + bias
    sum1_ref[...] = (
        mm(second_ref[...], time_ref[2]) + bias + keep[1][1] * mm(first_ref[...], time_ref[1])
    )


def upscale(temporal, frame, small_ref, even_ref, odd_ref, out_hbm, near, rows32, made, left):
    pixels = H * W
    channels = near.shape[1] // 3
    outs = even_ref.shape[3]
    both = temporal.astype(bf16)
    nothing = jnp.zeros((H, 3 * channels), bf16)
    for half in range(2):
        base = H + half * (pixels + H)
        near[base - H : base] = nothing
        shown = both[:, half * channels : (half + 1) * channels]
        for a, shifted in enumerate(vertical(shown)):
            near[base : base + pixels, a * channels : (a + 1) * channels] = shifted
    near[2 * (H + pixels) :] = nothing
    span = 2 * pixels + H
    bias = small_ref[4:5, :outs]
    blocks = 2 * outs // 128
    for p in range(2):
        phases = []
        for q, taps_ref in enumerate((even_ref, odd_ref)):
            total = bias
            for side in range(2):
                first = (q + side) * H
                window = near[first : first + span, p * channels : (p + 2) * channels]
                total = total + mm(window, taps_ref[side, p])
            phases.append(total)
        pair = jnp.concatenate(phases, 1)
        for half in range(2):
            for x in range(W):
                row = half * (pixels + H) + x * H
                for block in range(blocks):
                    rows32[half, x * blocks + block, pl.ds(p, H, stride=2)] = pair[
                        row : row + H, block * 128 : (block + 1) * 128
                    ]
    sent = []
    for half in range(2):
        for block in range(W * blocks):
            made[half, :, block * 128 : (block + 1) * 128] = rows32[half, block].astype(bf16)
        copy = pltpu.make_async_copy(made.at[half], out_hbm.at[2 * frame + half], left.at[half])
        copy.start()
        sent.append(copy)
    for copy in sent:
        copy.wait()


def second_up_kernel(
    keep_ref, small_ref, prior_ref, time_ref, sum_ref, even_ref, odd_ref, out_hbm,
    near, rows32, made, left,
):
    keep = kept(keep_ref)
    temporal = sum_ref[...] + keep[1][2] * mm(prior_ref[...], time_ref[0])
    upscale(temporal, 1, small_ref, even_ref, odd_ref, out_hbm, near, rows32, made, left)


def first_up_kernel(
    keep_ref, small_ref, before_ref, prior_ref, time_ref, sum_ref, even_ref, odd_ref, made_hbm,
    out_hbm,
    near, rows32, made, left,
):
    keep = kept(keep_ref)
    far = keep[0][2] * mm(before_ref[...], time_ref[0])
    temporal = sum_ref[...] + far + keep[0][1] * mm(prior_ref[...], time_ref[1])
    upscale(temporal, 0, small_ref, even_ref, odd_ref, out_hbm, near, rows32, made, left)


def keeps(counts_ref, position_ref):
    first = position_ref[0] * 2
    starts = [jnp.int32(0), jnp.int32(0)]
    end = jnp.int32(0)
    for video in range(counts_ref.shape[0]):
        end = end + counts_ref[video]
        starts = [jnp.where(end <= first + f, end, starts[f]) for f in range(2)]
    return [
        [(first + f - back >= starts[f]).astype(f32) for back in range(3)] for f in range(2)
    ]


def halves(taps):
    return (taps[0], taps[1] + taps[2]), (taps[0] + taps[1], taps[2])


def prepare_kernel(
    counts_ref, position_ref, gain_ref, shift_ref, res_bias_ref, time_bias_ref, up_bias_ref,
    up_hbm, taps_hbm,
    folded_ref, small_ref, keep_ref, taps_ref,
    up_ref, arrived,
):
    copies = [
        pltpu.make_async_copy(up_hbm, up_ref, arrived.at[0]),
        pltpu.make_async_copy(taps_hbm.at[2], taps_ref, arrived.at[1]),
    ]
    for copy in copies:
        copy.start()
    small_ref[...] = jnp.zeros_like(small_ref)
    for i, ref in enumerate((gain_ref, shift_ref, res_bias_ref, time_bias_ref, up_bias_ref)):
        small_ref[i : i + 1, : ref.shape[1]] = ref[...]
    keep = keeps(counts_ref, position_ref)
    row = iota(keep_ref.shape, 0)
    seen = jnp.zeros(keep_ref.shape, f32)
    for f in range(2):
        for back in range(3):
            seen = jnp.where(row == 3 * f + back, keep[f][back], seen)
    keep_ref[...] = seen
    copies[0].wait()
    channels = up_ref.shape[3]
    columns = [
        halves([up_ref[a, b].astype(f32) for b in range(3)]) for a in range(3)
    ]
    for q in range(2):
        for side in range(2):
            rows = halves([columns[a][q][side] for a in range(3)])
            for p in range(2):
                for dy in range(2):
                    folded_ref[q, side, p, dy * channels : (dy + 1) * channels] = rows[p][
                        dy
                    ].T.astype(bf16)
    copies[1].wait()


def on_device(
    latent,
    owner,
    frame_counts,
    norm_gain,
    norm_shift,
    res_kernel,
    res_bias,
    time_kernel,
    time_bias,
    up_kernel,
    up_bias,
):
    peers = lax.axis_size("tm")
    position = lax.axis_index("tm").astype(jnp.int32).reshape(1)
    tokens, channels = latent.shape
    capacity = 2 * tokens // peers
    pixels = H * W
    wide = time_kernel.shape[-1]
    outs = up_kernel.shape[-1]

    packed = pl.pallas_call(
        functools.partial(pack_kernel, peers=peers, capacity=capacity),
        out_shape=jax.ShapeDtypeStruct((peers * capacity, channels), bf16),
        in_specs=[HB, HB],
        out_specs=HB,
        scratch_shapes=[
            pltpu.VMEM((1, tokens), jnp.int32),
            pltpu.VMEM((tokens, channels + 128), bf16),
            pltpu.VMEM((peers * capacity, channels), bf16),
            pltpu.SemaphoreType.DMA((2,)),
            pltpu.SemaphoreType.DMA((4,)),
        ],
        compiler_params=pltpu.CompilerParams(vmem_limit_bytes=16 * MIB),
        name="pack",
    )(in_hbm(owner.reshape(1, tokens)), in_hbm(latent))
    packed, up_kernel = lax.optimization_barrier((packed, up_kernel))
    received = lax.all_to_all(packed, "tm", split_axis=0, concat_axis=0, tiled=True)
    res_kernel = in_hbm(res_kernel.reshape(3, 9 * channels, channels))
    folded, small, keep, here = pl.pallas_call(
        prepare_kernel,
        out_shape=[
            jax.ShapeDtypeStruct((2, 2, 2, 2 * channels, outs), bf16),
            pltpu.VMEM((8, wide), f32),
            pltpu.VMEM((8, 128), f32),
            pltpu.VMEM((9 * channels, channels), bf16),
        ],
        in_specs=[SM] * 2 + [VM] * 5 + [HB] * 2,
        out_specs=[VM] * 4,
        scratch_shapes=[
            pltpu.VMEM((3, 3, outs, channels), bf16),
            pltpu.SemaphoreType.DMA((2,)),
        ],
        compiler_params=pltpu.CompilerParams(vmem_limit_bytes=16 * MIB),
        cost_estimate=pl.CostEstimate(
            flops=0, bytes_accessed=2 * res_kernel.size * 2, transcendentals=0
        ),
        name="prepare",
    )(
        frame_counts,
        position,
        norm_gain.reshape(1, channels),
        norm_shift.reshape(1, channels),
        res_bias.reshape(1, channels),
        time_bias.reshape(1, wide),
        up_bias.reshape(1, outs),
        in_hbm(jnp.swapaxes(up_kernel, 2, 3)),
        res_kernel,
    )

    def call(body, name, outputs, arguments, scratch=(), flops=0, **more):
        out_specs = more.pop("out_specs", [VM] * len(outputs))
        in_specs = more.pop("in_specs", [VM] * len(arguments))
        return pl.pallas_call(
            body,
            out_shape=outputs,
            in_specs=in_specs,
            out_specs=out_specs,
            scratch_shapes=scratch,
            compiler_params=pltpu.CompilerParams(vmem_limit_bytes=12 * MIB),
            cost_estimate=pl.CostEstimate(flops=flops, bytes_accessed=0, transcendentals=0),
            name=name,
            **more,
        )(*arguments)

    vm = in_vmem
    frame16 = pltpu.VMEM((pixels, channels), bf16)
    frame32 = pltpu.VMEM((pixels, channels), f32)
    near_shape = pltpu.VMEM((pixels, 9 * channels), bf16)
    tap = 2 * pixels * 9 * channels * channels
    sem = pltpu.SemaphoreType.DMA
    taps_shape = pltpu.VMEM((9 * channels, channels), bf16)
    small, keep, received = vm(small), vm(keep), vm(received)
    decoded, active, prior, behind = {}, {}, {}, {}
    for f in (1, 0):
        decoded[f], active[f], behind[f] = call(
            functools.partial(unpack_kernel, peers=peers, capacity=capacity, frame=f),
            "unpack",
            [frame16] * 2 + [pltpu.VMEM((9 * channels // 2, channels), bf16)],
            [received, small, res_kernel],
            [sem],
            in_specs=[VM, VM, HB],
        )
        prior[f] = from_behind(active[f], "tm")
    low, high, here = vm(behind[0]), vm(behind[1]), vm(here)
    sum0, sum1, far, times = call(
        local_conv_kernel,
        "local_conv",
        [frame32] * 2 + [taps_shape, pltpu.VMEM(time_kernel.shape, bf16)],
        [keep, vm(active[0]), vm(active[1]), low, high, here, res_kernel, in_hbm(time_kernel)],
        [pltpu.VMEM((2 * pixels, 9 * channels), bf16), sem((2,))],
        flops=3 * tap,
        in_specs=[VM] * 6 + [HB] * 2,
    )
    far, folded = vm(far), in_hbm(folded)
    half_taps = pltpu.VMEM(folded.shape[1:], bf16)
    second, near, taps0 = call(
        second_residual_kernel,
        "second_residual",
        [frame16, near_shape, half_taps],
        [keep, small, vm(prior[1]), far, vm(sum1), vm(decoded[1]), folded],
        [sem],
        flops=tap,
        in_specs=[VM] * 6 + [HB],
    )
    prior_second = from_behind(second, "tm")
    sum0, taps1 = call(
        behind_kernel,
        "behind",
        [frame32, half_taps],
        [keep, small, vm(near), low, high, vm(sum0), vm(decoded[0]), folded],
        [sem],
        flops=tap,
        in_specs=[VM] * 7 + [HB],
    )
    (first,) = call(
        first_residual_kernel,
        "first_residual",
        [frame16],
        [keep, vm(prior[0]), far, vm(sum0)],
        [near_shape],
        flops=tap,
    )
    prior_first = from_behind(first, "tm")
    times = vm(times)
    time0, time1 = call(
        local_time_kernel,
        "local_time",
        [pltpu.VMEM((pixels, wide), f32)] * 2,
        [keep, small, vm(first), vm(second), times],
        flops=6 * pixels * channels * wide,
    )
    frames = 2 * tokens // pixels
    out = jax.ShapeDtypeStruct((frames, 2 * H, 2 * W * outs), bf16)
    up_scratch = [
        pltpu.VMEM((2 * pixels + 3 * H, 3 * channels), bf16),
        pltpu.VMEM((2, 2 * W * outs // 128, 2 * H, 128), f32),
        pltpu.VMEM((2, 2 * H, 2 * W * outs), bf16),
        sem((2,)),
    ]
    taps0, taps1, prior_second = vm(taps0), vm(taps1), vm(prior_second)
    (made,) = call(
        second_up_kernel,
        "second_up",
        [out],
        [keep, small, prior_second, times, vm(time1), taps0, taps1],
        up_scratch,
        flops=8 * tap,
        out_specs=[HB],
    )
    (made,) = call(
        first_up_kernel,
        "first_up",
        [out],
        [keep, small, vm(prior_first), prior_second, times, vm(time0), taps0, taps1, made],
        up_scratch,
        flops=8 * tap,
        in_specs=[VM] * 8 + [pl.BlockSpec(memory_space=pl.ANY)],
        out_specs=[HB],
        input_output_aliases={8: 0},
    )
    return made


def solution(mesh):
    placed = (
        P(("groups", "tm"), None),
        P(("groups", "tm")),
        P("groups"),
        P(),
        P(),
        P(),
        P(),
        P(),
        P(),
        P(),
        P(),
    )
    return jax.shard_map(
        on_device,
        mesh=mesh,
        in_specs=placed,
        out_specs=P(("groups", "tm"), None, None),
        check_vma=False,
    )
```

```python
import functools

import jax
import jax.numpy as jnp
from jax import lax
from jax.experimental import pallas as pl
from jax.experimental.pallas import tpu as pltpu
from jax.sharding import PartitionSpec as P

H = 16
W = 16
MARK = 128.0
epsilon = 1e-06
MIB = 1 << 20
f32 = jnp.float32
bf16 = jnp.bfloat16


def in_vmem(value):
    return pltpu.with_memory_space_constraint(value, pltpu.VMEM)


def in_hbm(value):
    return pltpu.with_memory_space_constraint(value, pltpu.HBM)


VM = pl.BlockSpec(memory_space=pltpu.VMEM)
HB = pl.BlockSpec(memory_space=pltpu.HBM)
SM = pl.BlockSpec(memory_space=pltpu.SMEM)


def iota(shape, dim):
    return lax.broadcasted_iota(jnp.int32, shape, dim)


def mm(lhs, rhs):
    return jnp.dot(lhs, rhs, preferred_element_type=f32)


def alone(keep_ref, f):
    row = 3 * f + 1 + f
    return jnp.max(keep_ref[row : row + 1]) == 0.0


def convolve(near, taps):
    return lax.dot_general(taps, near, (((0,), (1,)), ((), ())), preferred_element_type=f32).T


def from_behind(value, axis):
    size = lax.axis_size(axis)
    return lax.ppermute(value, axis, [(i, (i + 1) % size) for i in range(size)])


def pack_kernel(
    owner_hbm, latent_hbm, out_hbm, owner_ref, wide_ref, made_ref, arrived, left, *, peers, capacity
):
    tokens, channels = latent_hbm.shape
    copies = [
        pltpu.make_async_copy(owner_hbm, owner_ref, arrived.at[0]),
        pltpu.make_async_copy(latent_hbm, wide_ref.at[:, :channels], arrived.at[1]),
    ]
    for copy in copies:
        copy.start()
    wide_ref[:, channels:] = jnp.ones((tokens, 128), bf16)
    upper = (iota((tokens, tokens), 0) <= iota((tokens, tokens), 1)).astype(bf16)
    copies[0].wait()
    owner = owner_ref[...]
    marked = iota((peers, tokens), 0) == owner
    running = mm(marked.astype(bf16), upper)
    rank = jnp.sum(jnp.where(marked, running - 1.0, 0.0), 0, keepdims=True)
    slot = owner * capacity + rank.astype(jnp.int32)
    copies[1].wait()
    pieces = left.shape[0]
    rows = peers * capacity // pieces
    sent = []
    for piece in range(pieces):
        at = pl.ds(piece * rows, rows)
        chosen = (iota((rows, tokens), 0) + piece * rows == slot).astype(bf16)
        found = mm(chosen, wide_ref[...])
        empty = (1.0 - found[:, channels:]) * MARK
        made_ref[at] = (
            found[:, :channels] + jnp.concatenate([empty] * (channels // 128), 1)
        ).astype(bf16)
        copy = pltpu.make_async_copy(made_ref.at[at], out_hbm.at[at], left.at[piece])
        copy.start()
        sent.append(copy)
    for copy in sent:
        copy.wait()


def places(got_ref, peers, capacity):
    slots = got_ref.shape[0]
    present = (got_ref[:, :128] < MARK / 2).astype(bf16)
    sender = iota((peers, slots), 1) // capacity
    member = (sender == iota((peers, slots), 0)).astype(f32)
    below = (sender < iota((peers, slots), 0)).astype(f32)
    tallies = mm(jnp.concatenate([member, below], 0).astype(bf16), present)
    held = jnp.sum(member * tallies[:peers, :1], 0, keepdims=True).astype(jnp.int32)
    first = jnp.sum(member * tallies[peers:, :1], 0, keepdims=True).astype(jnp.int32)
    within = iota((1, slots), 1) % capacity
    return jnp.where(within < held, first + within, -1)


def unpack(place, got_ref, small_ref, decoded_ref, active_ref, frame):
    slots, channels = got_ref.shape
    pixels = decoded_ref.shape[0]
    pixel = iota((pixels, slots), 0)
    source = frame * pixels + (pixel % H) * W + pixel // H
    chosen = (source == place).astype(bf16)
    values = mm(chosen, got_ref[...])
    decoded_ref[...] = values.astype(bf16)
    squares = jnp.mean(values * values, -1, keepdims=True)
    scaled = values * lax.rsqrt(squares + epsilon)
    fed = scaled * small_ref[0:1, :channels] + small_ref[1:2, :channels]
    active_ref[...] = (fed / (1.0 + jnp.exp(-fed))).astype(bf16)


def unpack_second_kernel(
    got_ref, small_ref, decoded_ref, active_ref, place_ref, *, peers, capacity
):
    place = places(got_ref, peers, capacity)
    place_ref[...] = place
    unpack(place, got_ref, small_ref, decoded_ref, active_ref, 1)


def unpack_first_kernel(got_ref, small_ref, place_ref, decoded_ref, active_ref):
    unpack(place_ref[...], got_ref, small_ref, decoded_ref, active_ref, 0)


def vertical(frame):
    wide = frame.astype(f32)
    y = iota(wide.shape, 0) % H
    up = jnp.where(y == 0, 0.0, pltpu.roll(wide, 1, 0))
    down = jnp.where(y == H - 1, 0.0, pltpu.roll(wide, wide.shape[0] - 1, 0))
    return up.astype(bf16), frame, down.astype(bf16)


def patches(frame):
    pixels, channels = frame.shape
    nothing = jnp.zeros((H, channels), bf16)
    parts = []
    for shifted in vertical(frame):
        parts.append(jnp.concatenate([nothing, shifted[: pixels - H]], 0))
        parts.append(shifted)
        parts.append(jnp.concatenate([shifted[H:], nothing], 0))
    return jnp.concatenate(parts, 1)


def kept(keep_ref):
    return [[keep_ref[3 * f + back : 3 * f + back + 1, :1] for back in range(3)] for f in range(2)]


def local_conv_kernel(
    keep_ref, first_ref, second_ref, here_ref, behind_ref, sum0_ref, sum1_ref
):
    keep = kept(keep_ref)
    channels = sum0_ref.shape[1]
    sum1 = convolve(patches(second_ref[...]), here_ref[...])
    both = mm(
        patches(first_ref[...]), jnp.concatenate([here_ref[...], behind_ref[...]], 1)
    )
    sum0_ref[...] = both[:, :channels]
    sum1_ref[...] = sum1 + keep[1][1] * both[:, channels:]


def second_residual_kernel(
    keep_ref, small_ref, prior_ref, far_ref, sum_ref, decoded_ref, out_ref, near_ref
):
    base = sum_ref[...] + decoded_ref[...].astype(f32) + small_ref[2:3, : out_ref.shape[1]]

    near = patches(prior_ref[...])
    near_ref[...] = near
    far = kept(keep_ref)[1][2] * convolve(near, far_ref[...])
    out_ref[...] = (base + far).astype(bf16)


def behind_kernel(
    keep_ref, small_ref, near_ref, behind_ref, sum_ref, decoded_ref, out_ref
):
    base = sum_ref[...] + decoded_ref[...].astype(f32) + small_ref[2:3, : out_ref.shape[1]]
    out_ref[...] = base + kept(keep_ref)[0][1] * convolve(near_ref[...], behind_ref[...])


def first_residual_kernel(keep_ref, prior_ref, far_ref, sum_ref, out_ref):
    far = kept(keep_ref)[0][2] * convolve(patches(prior_ref[...]), far_ref[...])
    out_ref[...] = (sum_ref[...] + far).astype(bf16)


def local_time_kernel(
    keep_ref, small_ref, first_ref, second_ref, time_ref, sum0_ref, sum1_ref
):
    keep = kept(keep_ref)
    bias = small_ref[3:4, : sum0_ref.shape[1]]
    sum0_ref[...] = mm(first_ref[...], time_ref[2]) + bias
    sum1_ref[...] = (
        mm(second_ref[...], time_ref[2]) + bias + keep[1][1] * mm(first_ref[...], time_ref[1])
    )


def upscale(temporal, frame, small_ref, folded_ref, made_ref, near, rows32):
    pixels = H * W
    channels = near.shape[1] // 3
    outs = folded_ref.shape[3]
    both = temporal.astype(bf16)
    nothing = jnp.zeros((H, 3 * channels), bf16)
    for half in range(2):
        base = H + half * (pixels + H)
        near[base - H : base] = nothing
        shown = both[:, half * channels : (half + 1) * channels]
        for a, shifted in enumerate(vertical(shown)):
            near[base : base + pixels, a * channels : (a + 1) * channels] = shifted
    near[2 * (H + pixels) :] = nothing
    span = 2 * pixels + H
    bias = small_ref[4:5, :outs]
    blocks = 2 * outs // 128
    for p in range(2):
        phases = []
        for q in range(2):
            windows = [
                near[
                    (q + side) * H : (q + side) * H + span, p * channels : (p + 2) * channels
                ]
                for side in range(2)
            ]
            phases.append(mm(jnp.concatenate(windows, 1), folded_ref[q, p]) + bias)
        pair = jnp.concatenate(phases, 1)
        for half in range(2):
            for x in range(W):
                row = half * (pixels + H) + x * H
                for block in range(blocks):
                    rows32[half, x * blocks + block, pl.ds(p, H, stride=2)] = pair[
                        row : row + H, block * 128 : (block + 1) * 128
                    ]
    for half in range(2):
        for block in range(W * blocks):
            made_ref[2 * frame + half, :, block * 128 : (block + 1) * 128] = rows32[
                half, block
            ].astype(bf16)


def early_up_kernel(
    keep_ref, small_ref, sum0_ref, sum1_ref, folded_ref, made_ref, near, rows32
):
    @pl.when(alone(keep_ref, 1))
    def _():
        upscale(sum1_ref[...], 1, small_ref, folded_ref, made_ref, near, rows32)

    @pl.when(alone(keep_ref, 0))
    def _():
        upscale(sum0_ref[...], 0, small_ref, folded_ref, made_ref, near, rows32)


def second_up_kernel(
    keep_ref, small_ref, prior_ref, time_ref, sum_ref, folded_ref, early_ref, made_ref,
    near, rows32,
):
    @pl.when(jnp.logical_not(alone(keep_ref, 1)))
    def _():
        temporal = sum_ref[...] + mm(prior_ref[...], time_ref[0])
        upscale(temporal, 1, small_ref, folded_ref, made_ref, near, rows32)


def first_up_kernel(
    keep_ref, small_ref, before_ref, prior_ref, time_ref, sum_ref, folded_ref, later_ref,
    out_hbm,
    made_ref, near, rows32, left,
):
    later = pltpu.make_async_copy(later_ref.at[2:4], out_hbm.at[2:4], left.at[0])
    later.start()
    lonely = alone(keep_ref, 0)

    @pl.when(lonely)
    def _():
        copy = pltpu.make_async_copy(later_ref.at[0:2], out_hbm.at[0:2], left.at[1])
        copy.start()
        copy.wait()

    @pl.when(jnp.logical_not(lonely))
    def _():
        seen = keep_ref[2:3, :1].astype(bf16)
        pair = jnp.concatenate([before_ref[...] * seen, prior_ref[...]], 1)
        both = time_ref[:2].reshape(pair.shape[1], time_ref.shape[2])
        temporal = sum_ref[...] + mm(pair, both)
        upscale(temporal, 0, small_ref, folded_ref, made_ref, near, rows32)
        copy = pltpu.make_async_copy(made_ref, out_hbm.at[0:2], left.at[1])
        copy.start()
        copy.wait()

    later.wait()


def keeps(counts_ref, position_ref):
    first = position_ref[0] * 2
    starts = [jnp.int32(0), jnp.int32(0)]
    end = jnp.int32(0)
    for video in range(counts_ref.shape[0]):
        end = end + counts_ref[video]
        starts = [jnp.where(end <= first + f, end, starts[f]) for f in range(2)]
    return [
        [(first + f - back >= starts[f]).astype(f32) for back in range(3)] for f in range(2)
    ]


def halves(taps):
    return (taps[0], taps[1] + taps[2]), (taps[0] + taps[1], taps[2])


def prepare_kernel(
    counts_ref, position_ref, gain_ref, shift_ref, res_bias_ref, time_bias_ref, up_bias_ref,
    up_hbm, taps_hbm,
    folded_ref, small_ref, keep_ref, here_ref, behind_hbm, far_hbm,
    up_ref, behind_ref, far_ref, arrived, left,
):
    copies = [
        pltpu.make_async_copy(up_hbm, up_ref, arrived.at[0]),
        pltpu.make_async_copy(taps_hbm.at[2], here_ref, arrived.at[1]),
        pltpu.make_async_copy(taps_hbm.at[1], behind_ref, arrived.at[2]),
        pltpu.make_async_copy(taps_hbm.at[0], far_ref, arrived.at[3]),
    ]
    for copy in copies:
        copy.start()
    small_ref[...] = jnp.zeros_like(small_ref)
    for i, ref in enumerate((gain_ref, shift_ref, res_bias_ref, time_bias_ref, up_bias_ref)):
        small_ref[i : i + 1, : ref.shape[1]] = ref[...]
    keep = keeps(counts_ref, position_ref)
    row = iota(keep_ref.shape, 0)
    seen = jnp.zeros(keep_ref.shape, f32)
    for f in range(2):
        for back in range(3):
            seen = jnp.where(row == 3 * f + back, keep[f][back], seen)
    keep_ref[...] = seen
    copies[0].wait()
    channels = up_ref.shape[3]
    columns = [
        halves([up_ref[a, b].astype(f32) for b in range(3)]) for a in range(3)
    ]
    for q in range(2):
        for side in range(2):
            rows = halves([columns[a][q][side] for a in range(3)])
            for p in range(2):
                for dy in range(2):
                    at = (2 * side + dy) * channels
                    folded_ref[q, p, at : at + channels] = rows[p][dy].T.astype(bf16)
    for copy in copies[1:]:
        copy.wait()
    sent = [
        pltpu.make_async_copy(behind_ref, behind_hbm, left.at[0]),
        pltpu.make_async_copy(far_ref, far_hbm, left.at[1]),
    ]
    for copy in sent:
        copy.start()
    for copy in sent:
        copy.wait()


def on_device(
    latent,
    owner,
    frame_counts,
    norm_gain,
    norm_shift,
    res_kernel,
    res_bias,
    time_kernel,
    time_bias,
    up_kernel,
    up_bias,
):
    peers = lax.axis_size("tm")
    position = lax.axis_index("tm").astype(jnp.int32).reshape(1)
    tokens, channels = latent.shape
    capacity = 2 * tokens // peers
    pixels = H * W
    wide = time_kernel.shape[-1]
    outs = up_kernel.shape[-1]

    packed = pl.pallas_call(
        functools.partial(pack_kernel, peers=peers, capacity=capacity),
        out_shape=jax.ShapeDtypeStruct((peers * capacity, channels), bf16),
        in_specs=[HB, HB],
        out_specs=HB,
        scratch_shapes=[
            pltpu.VMEM((1, tokens), jnp.int32),
            pltpu.VMEM((tokens, channels + 128), bf16),
            pltpu.VMEM((peers * capacity, channels), bf16),
            pltpu.SemaphoreType.DMA((2,)),
            pltpu.SemaphoreType.DMA((4,)),
        ],
        compiler_params=pltpu.CompilerParams(vmem_limit_bytes=16 * MIB),
        name="pack",
    )(in_hbm(owner.reshape(1, tokens)), in_hbm(latent))
    packed, up_kernel = lax.optimization_barrier((packed, up_kernel))
    received = lax.all_to_all(packed, "tm", split_axis=0, concat_axis=0, tiled=True)
    res_kernel = res_kernel.reshape(3, 9 * channels, channels)
    one_tap = (9 * channels, channels)
    res_kernel = in_hbm(res_kernel)
    folded, small, keep, here, behind, far = pl.pallas_call(
        prepare_kernel,
        out_shape=[
            jax.ShapeDtypeStruct((2, 2, 4 * channels, outs), bf16),
            pltpu.VMEM((8, wide), f32),
            pltpu.VMEM((8, 128), f32),
            pltpu.VMEM(one_tap, bf16),
            pltpu.HBM(one_tap, bf16),
            pltpu.HBM(one_tap, bf16),
        ],
        in_specs=[SM] * 2 + [VM] * 5 + [HB] * 2,
        out_specs=[VM] * 4 + [HB] * 2,
        scratch_shapes=[
            pltpu.VMEM((3, 3, outs, channels), bf16),
            pltpu.VMEM(one_tap, bf16),
            pltpu.VMEM(one_tap, bf16),
            pltpu.SemaphoreType.DMA((4,)),
            pltpu.SemaphoreType.DMA((2,)),
        ],
        compiler_params=pltpu.CompilerParams(vmem_limit_bytes=20 * MIB),
        cost_estimate=pl.CostEstimate(
            flops=0, bytes_accessed=2 * res_kernel.size * 2, transcendentals=0
        ),
        name="prepare",
    )(
        frame_counts,
        position,
        norm_gain.reshape(1, channels),
        norm_shift.reshape(1, channels),
        res_bias.reshape(1, channels),
        time_bias.reshape(1, wide),
        up_bias.reshape(1, outs),
        in_hbm(jnp.swapaxes(up_kernel, 2, 3)),
        res_kernel,
    )

    def call(body, name, outputs, arguments, scratch=(), share=1.0, **more):
        out_specs = more.pop("out_specs", [VM] * len(outputs))
        in_specs = more.pop("in_specs", [VM] * len(arguments))
        return pl.pallas_call(
            body,
            out_shape=outputs,
            in_specs=in_specs,
            out_specs=out_specs,
            scratch_shapes=scratch,
            compiler_params=pltpu.CompilerParams(vmem_limit_bytes=12 * MIB),
            cost_estimate=pl.CostEstimate(
                flops=int(share * tap), bytes_accessed=0, transcendentals=0
            ),
            name=name,
            **more,
        )(*arguments)

    vm = in_vmem
    frame16 = pltpu.VMEM((pixels, channels), bf16)
    frame32 = pltpu.VMEM((pixels, channels), f32)
    near_shape = pltpu.VMEM((pixels, 9 * channels), bf16)
    tap = 2 * pixels * 9 * channels * channels
    sem = pltpu.SemaphoreType.DMA
    small, keep, received = vm(small), vm(keep), vm(received)
    decoded1, active1, place = call(
        functools.partial(unpack_second_kernel, peers=peers, capacity=capacity),
        "unpack_second",
        [frame16] * 2 + [pltpu.VMEM((1, peers * capacity), jnp.int32)],
        [received, small],
        share=3,
    )
    prior1 = from_behind(active1, "tm")
    decoded0, active0 = call(
        unpack_first_kernel, "unpack_first", [frame16] * 2, [received, small, vm(place)], share=0
    )
    prior0 = from_behind(active0, "tm")
    behind, far = vm(behind), vm(far)
    sum0, sum1 = call(
        local_conv_kernel,
        "local_conv",
        [frame32] * 2,
        [keep, vm(active0), vm(active1), vm(here), behind],
        share=3,
    )
    second, near = call(
        second_residual_kernel,
        "second_residual",
        [frame16, near_shape],
        [keep, small, vm(prior1), far, vm(sum1), vm(decoded1)],
        share=1,
    )
    prior_second = from_behind(second, "tm")
    (sum0,) = call(
        behind_kernel,
        "behind",
        [frame32],
        [keep, small, vm(near), behind, vm(sum0), vm(decoded0)],
        share=1,
    )
    (first,) = call(
        first_residual_kernel,
        "first_residual",
        [frame16],
        [keep, vm(prior0), far, vm(sum0)],
        share=1,
    )
    prior_first = from_behind(first, "tm")
    times = vm(time_kernel)
    time0, time1 = call(
        local_time_kernel,
        "local_time",
        [pltpu.VMEM((pixels, wide), f32)] * 2,
        [keep, small, vm(first), vm(second), times],
        share=0.4,
    )
    frames = 2 * tokens // pixels
    shape = (frames, 2 * H, 2 * W * outs)
    up_scratch = [
        pltpu.VMEM((2 * pixels + 3 * H, 3 * channels), bf16),
        pltpu.VMEM((2, 2 * W * outs // 128, 2 * H, 128), f32),
    ]
    folded, prior_second = vm(folded), vm(prior_second)
    time0, time1 = vm(time0), vm(time1)
    (early,) = call(
        early_up_kernel,
        "early_up",
        [pltpu.VMEM(shape, bf16)],
        [keep, small, time0, time1, folded],
        up_scratch,
        share=2,
    )
    (later,) = call(
        second_up_kernel,
        "second_up",
        [pltpu.VMEM(shape, bf16)],
        [keep, small, prior_second, times, time1, folded, vm(early)],
        up_scratch,
        share=6,
        input_output_aliases={6: 0},
    )
    (made,) = call(
        first_up_kernel,
        "first_up",
        [jax.ShapeDtypeStruct(shape, bf16)],
        [keep, small, vm(prior_first), prior_second, times, time0, folded, vm(later)],
        [pltpu.VMEM((frames // 2,) + shape[1:], bf16)] + up_scratch + [sem((2,))],
        share=6,
        out_specs=[HB],
    )
    return made


def solution(mesh):
    placed = (
        P(("groups", "tm"), None),
        P(("groups", "tm")),
        P("groups"),
        P(),
        P(),
        P(),
        P(),
        P(),
        P(),
        P(),
        P(),
    )
    return jax.shard_map(
        on_device,
        mesh=mesh,
        in_specs=placed,
        out_specs=P(("groups", "tm"), None, None),
        check_vma=False,
    )
```

```python
import functools

import jax
import jax.numpy as jnp
from jax import lax
from jax.experimental import pallas as pl
from jax.experimental.pallas import tpu as pltpu
from jax.sharding import PartitionSpec as P

H = 16
W = 16
MARK = 128.0
epsilon = 1e-06
MIB = 1 << 20
f32 = jnp.float32
bf16 = jnp.bfloat16


def in_vmem(value):
    return pltpu.with_memory_space_constraint(value, pltpu.VMEM)


def in_hbm(value):
    return pltpu.with_memory_space_constraint(value, pltpu.HBM)


VM = pl.BlockSpec(memory_space=pltpu.VMEM)
HB = pl.BlockSpec(memory_space=pltpu.HBM)
SM = pl.BlockSpec(memory_space=pltpu.SMEM)


def iota(shape, dim):
    return lax.broadcasted_iota(jnp.int32, shape, dim)


def mm(lhs, rhs):
    return jnp.dot(lhs, rhs, preferred_element_type=f32)


def convolve(near, taps):
    return lax.dot_general(taps, near, (((0,), (1,)), ((), ())), preferred_element_type=f32).T


def from_behind(value, axis):
    size = lax.axis_size(axis)
    return lax.ppermute(value, axis, [(i, (i + 1) % size) for i in range(size)])


def pack_kernel(
    owner_hbm, latent_hbm, out_hbm, owner_ref, wide_ref, made_ref, arrived, left, *, peers, capacity
):
    tokens, channels = latent_hbm.shape
    copies = [
        pltpu.make_async_copy(owner_hbm, owner_ref, arrived.at[0]),
        pltpu.make_async_copy(latent_hbm, wide_ref.at[:, :channels], arrived.at[1]),
    ]
    for copy in copies:
        copy.start()
    wide_ref[:, channels:] = jnp.ones((tokens, 128), bf16)
    upper = (iota((tokens, tokens), 0) <= iota((tokens, tokens), 1)).astype(bf16)
    copies[0].wait()
    owner = owner_ref[...]
    marked = iota((peers, tokens), 0) == owner
    running = mm(marked.astype(bf16), upper)
    rank = jnp.sum(jnp.where(marked, running - 1.0, 0.0), 0, keepdims=True)
    slot = owner * capacity + rank.astype(jnp.int32)
    copies[1].wait()
    pieces = left.shape[0]
    rows = peers * capacity // pieces
    sent = []
    for piece in range(pieces):
        at = pl.ds(piece * rows, rows)
        chosen = (iota((rows, tokens), 0) + piece * rows == slot).astype(bf16)
        found = mm(chosen, wide_ref[...])
        empty = (1.0 - found[:, channels:]) * MARK
        made_ref[at] = (
            found[:, :channels] + jnp.concatenate([empty] * (channels // 128), 1)
        ).astype(bf16)
        copy = pltpu.make_async_copy(made_ref.at[at], out_hbm.at[at], left.at[piece])
        copy.start()
        sent.append(copy)
    for copy in sent:
        copy.wait()


def places(got_ref, peers, capacity):
    slots = got_ref.shape[0]
    present = (got_ref[:, :128] < MARK / 2).astype(bf16)
    sender = iota((peers, slots), 1) // capacity
    member = (sender == iota((peers, slots), 0)).astype(f32)
    below = (sender < iota((peers, slots), 0)).astype(f32)
    tallies = mm(jnp.concatenate([member, below], 0).astype(bf16), present)
    held = jnp.sum(member * tallies[:peers, :1], 0, keepdims=True).astype(jnp.int32)
    first = jnp.sum(member * tallies[peers:, :1], 0, keepdims=True).astype(jnp.int32)
    within = iota((1, slots), 1) % capacity
    return jnp.where(within < held, first + within, -1)


def unpack(place, got_ref, small_ref, decoded_ref, active_ref, frame):
    slots, channels = got_ref.shape
    pixels = decoded_ref.shape[0]
    pixel = iota((pixels, slots), 0)
    source = frame * pixels + (pixel % H) * W + pixel // H
    chosen = (source == place).astype(bf16)
    values = mm(chosen, got_ref[...])
    decoded_ref[...] = values.astype(bf16)
    squares = jnp.mean(values * values, -1, keepdims=True)
    scaled = values * lax.rsqrt(squares + epsilon)
    fed = scaled * small_ref[0:1, :channels] + small_ref[1:2, :channels]
    active_ref[...] = (fed / (1.0 + jnp.exp(-fed))).astype(bf16)


def unpack_second_kernel(
    got_ref, small_ref, decoded_ref, active_ref, place_ref, *, peers, capacity
):
    place = places(got_ref, peers, capacity)
    place_ref[...] = place
    unpack(place, got_ref, small_ref, decoded_ref, active_ref, 1)


def unpack_first_kernel(got_ref, small_ref, place_ref, decoded_ref, active_ref):
    unpack(place_ref[...], got_ref, small_ref, decoded_ref, active_ref, 0)


def vertical(frame):
    wide = frame.astype(f32)
    y = iota(wide.shape, 0) % H
    up = jnp.where(y == 0, 0.0, pltpu.roll(wide, 1, 0))
    down = jnp.where(y == H - 1, 0.0, pltpu.roll(wide, wide.shape[0] - 1, 0))
    return up.astype(bf16), frame, down.astype(bf16)


def patches(frame):
    pixels, channels = frame.shape
    nothing = jnp.zeros((H, channels), bf16)
    parts = []
    for shifted in vertical(frame):
        parts.append(jnp.concatenate([nothing, shifted[: pixels - H]], 0))
        parts.append(shifted)
        parts.append(jnp.concatenate([shifted[H:], nothing], 0))
    return jnp.concatenate(parts, 1)


def kept(keep_ref):
    return [[keep_ref[3 * f + back : 3 * f + back + 1, :1] for back in range(3)] for f in range(2)]


def local_conv_kernel(
    keep_ref, first_ref, second_ref, here_ref, behind_ref, sum0_ref, sum1_ref
):
    keep = kept(keep_ref)
    channels = sum0_ref.shape[1]
    sum1 = convolve(patches(second_ref[...]), here_ref[...])
    both = mm(
        patches(first_ref[...]), jnp.concatenate([here_ref[...], behind_ref[...]], 1)
    )
    sum0_ref[...] = both[:, :channels]
    sum1_ref[...] = sum1 + keep[1][1] * both[:, channels:]


def second_residual_kernel(
    solo_ref, keep_ref, small_ref, prior_ref, far_ref, sum_ref, decoded_ref, out_ref, near_ref
):
    base = sum_ref[...] + decoded_ref[...].astype(f32) + small_ref[2:3, : out_ref.shape[1]]


    @pl.when(solo_ref[0] == 1)
    def _():
        out_ref[...] = base.astype(bf16)

    @pl.when(solo_ref[0] == 0)
    def _():
        near = patches(prior_ref[...])
        near_ref[...] = near
        far = kept(keep_ref)[1][2] * convolve(near, far_ref[...])
        out_ref[...] = (base + far).astype(bf16)


def behind_kernel(
    solo_ref, keep_ref, small_ref, near_ref, behind_ref, sum_ref, decoded_ref, out_ref
):
    base = sum_ref[...] + decoded_ref[...].astype(f32) + small_ref[2:3, : out_ref.shape[1]]

    @pl.when(solo_ref[0] == 1)
    def _():
        out_ref[...] = base

    @pl.when(solo_ref[0] == 0)
    def _():
        out_ref[...] = base + kept(keep_ref)[0][1] * convolve(near_ref[...], behind_ref[...])


def first_residual_kernel(solo_ref, keep_ref, prior_ref, far_ref, sum_ref, out_ref):

    @pl.when(solo_ref[0] == 1)
    def _():
        out_ref[...] = sum_ref[...].astype(bf16)

    @pl.when(solo_ref[0] == 0)
    def _():
        far = kept(keep_ref)[0][2] * convolve(patches(prior_ref[...]), far_ref[...])
        out_ref[...] = (sum_ref[...] + far).astype(bf16)


def local_time_kernel(
    keep_ref, small_ref, first_ref, second_ref, time_ref, sum0_ref, sum1_ref
):
    keep = kept(keep_ref)
    bias = small_ref[3:4, : sum0_ref.shape[1]]
    sum0_ref[...] = mm(first_ref[...], time_ref[2]) + bias
    sum1_ref[...] = (
        mm(second_ref[...], time_ref[2]) + bias + keep[1][1] * mm(first_ref[...], time_ref[1])
    )


def upscale(temporal, frame, small_ref, folded_ref, made_ref, near, rows32):
    pixels = H * W
    channels = near.shape[1] // 3
    outs = folded_ref.shape[3]
    both = temporal.astype(bf16)
    nothing = jnp.zeros((H, 3 * channels), bf16)
    for half in range(2):
        base = H + half * (pixels + H)
        near[base - H : base] = nothing
        shown = both[:, half * channels : (half + 1) * channels]
        for a, shifted in enumerate(vertical(shown)):
            near[base : base + pixels, a * channels : (a + 1) * channels] = shifted
    near[2 * (H + pixels) :] = nothing
    span = 2 * pixels + H
    bias = small_ref[4:5, :outs]
    blocks = 2 * outs // 128
    for p in range(2):
        phases = []
        for q in range(2):
            windows = [
                near[
                    (q + side) * H : (q + side) * H + span, p * channels : (p + 2) * channels
                ]
                for side in range(2)
            ]
            phases.append(mm(jnp.concatenate(windows, 1), folded_ref[q, p]) + bias)
        pair = jnp.concatenate(phases, 1)
        for half in range(2):
            for x in range(W):
                row = half * (pixels + H) + x * H
                for block in range(blocks):
                    rows32[half, x * blocks + block, pl.ds(p, H, stride=2)] = pair[
                        row : row + H, block * 128 : (block + 1) * 128
                    ]
    for half in range(2):
        for block in range(W * blocks):
            made_ref[2 * frame + half, :, block * 128 : (block + 1) * 128] = rows32[
                half, block
            ].astype(bf16)


def early_up_kernel(
    solo_ref, small_ref, sum0_ref, sum1_ref, folded_ref, out_hbm, made_ref, near, rows32, left
):
    @pl.when(solo_ref[0] == 1)
    def _():
        copies = [
            pltpu.make_async_copy(
                made_ref.at[2 * f : 2 * f + 2], out_hbm.at[2 * f : 2 * f + 2], left.at[f]
            )
            for f in range(2)
        ]
        for f, sum_ref in ((1, sum1_ref), (0, sum0_ref)):
            upscale(sum_ref[...], f, small_ref, folded_ref, made_ref, near, rows32)
            copies[f].start()
        for copy in copies:
            copy.wait()


def second_up_kernel(
    solo_ref, keep_ref, small_ref, prior_ref, time_ref, sum_ref, folded_ref, made_ref, near, rows32
):
    @pl.when(solo_ref[0] == 0)
    def _():
        temporal = sum_ref[...] + kept(keep_ref)[1][2] * mm(prior_ref[...], time_ref[0])
        upscale(temporal, 0, small_ref, folded_ref, made_ref, near, rows32)


def first_up_kernel(
    solo_ref, keep_ref, small_ref, before_ref, prior_ref, time_ref, sum_ref, folded_ref,
    later_ref, early_hbm, out_hbm,
    made_ref, near, rows32, left,
):
    @pl.when(solo_ref[0] == 0)
    def _():
        later = pltpu.make_async_copy(later_ref, out_hbm.at[2:4], left.at[0])
        later.start()
        seen = [keep_ref[row : row + 1, :1].astype(bf16) for row in (2, 1)]
        pair = jnp.concatenate([before_ref[...] * seen[0], prior_ref[...] * seen[1]], 1)
        both = time_ref[:2].reshape(pair.shape[1], time_ref.shape[2])
        temporal = sum_ref[...] + mm(pair, both)
        upscale(temporal, 0, small_ref, folded_ref, made_ref, near, rows32)
        copy = pltpu.make_async_copy(made_ref, out_hbm.at[0:2], left.at[1])
        copy.start()
        copy.wait()
        later.wait()


def keeps(counts_ref, position_ref):
    first = position_ref[0] * 2
    starts = [jnp.int32(0), jnp.int32(0)]
    end = jnp.int32(0)
    for video in range(counts_ref.shape[0]):
        end = end + counts_ref[video]
        starts = [jnp.where(end <= first + f, end, starts[f]) for f in range(2)]
    return [
        [(first + f - back >= starts[f]).astype(f32) for back in range(3)] for f in range(2)
    ]


def halves(taps):
    return (taps[0], taps[1] + taps[2]), (taps[0] + taps[1], taps[2])


def prepare_kernel(
    counts_ref, position_ref, gain_ref, shift_ref, res_bias_ref, time_bias_ref, up_bias_ref,
    up_hbm, taps_hbm,
    folded_hbm, small_ref, keep_ref, here_ref, behind_hbm, far_hbm, solo_ref,
    up_ref, folded_ref, behind_ref, far_ref, arrived, left,
):
    copies = [
        pltpu.make_async_copy(up_hbm, up_ref, arrived.at[0]),
        pltpu.make_async_copy(taps_hbm.at[2], here_ref, arrived.at[1]),
        pltpu.make_async_copy(taps_hbm.at[1], behind_ref, arrived.at[2]),
        pltpu.make_async_copy(taps_hbm.at[0], far_ref, arrived.at[3]),
    ]
    for copy in copies:
        copy.start()
    small_ref[...] = jnp.zeros_like(small_ref)
    for i, ref in enumerate((gain_ref, shift_ref, res_bias_ref, time_bias_ref, up_bias_ref)):
        small_ref[i : i + 1, : ref.shape[1]] = ref[...]
    keep = keeps(counts_ref, position_ref)
    solo_ref[0] = (keep[0][1] == 0.0).astype(jnp.int32)
    row = iota(keep_ref.shape, 0)
    seen = jnp.zeros(keep_ref.shape, f32)
    for f in range(2):
        for back in range(3):
            seen = jnp.where(row == 3 * f + back, keep[f][back], seen)
    keep_ref[...] = seen
    copies[0].wait()
    channels = up_ref.shape[3]
    columns = [
        halves([up_ref[a, b].astype(f32) for b in range(3)]) for a in range(3)
    ]
    for q in range(2):
        for side in range(2):
            rows = halves([columns[a][q][side] for a in range(3)])
            for p in range(2):
                for dy in range(2):
                    at = (2 * side + dy) * channels
                    folded_ref[q, p, at : at + channels] = rows[p][dy].T.astype(bf16)
    for copy in copies[1:]:
        copy.wait()
    sent = [
        pltpu.make_async_copy(behind_ref, behind_hbm, left.at[0]),
        pltpu.make_async_copy(far_ref, far_hbm, left.at[1]),
        pltpu.make_async_copy(folded_ref, folded_hbm, left.at[2]),
    ]
    for copy in sent:
        copy.start()
    for copy in sent:
        copy.wait()


def on_device(
    latent,
    owner,
    frame_counts,
    norm_gain,
    norm_shift,
    res_kernel,
    res_bias,
    time_kernel,
    time_bias,
    up_kernel,
    up_bias,
):
    peers = lax.axis_size("tm")
    position = lax.axis_index("tm").astype(jnp.int32).reshape(1)
    tokens, channels = latent.shape
    capacity = 2 * tokens // peers
    pixels = H * W
    wide = time_kernel.shape[-1]
    outs = up_kernel.shape[-1]

    packed = pl.pallas_call(
        functools.partial(pack_kernel, peers=peers, capacity=capacity),
        out_shape=jax.ShapeDtypeStruct((peers * capacity, channels), bf16),
        in_specs=[HB, HB],
        out_specs=HB,
        scratch_shapes=[
            pltpu.VMEM((1, tokens), jnp.int32),
            pltpu.VMEM((tokens, channels + 128), bf16),
            pltpu.VMEM((peers * capacity, channels), bf16),
            pltpu.SemaphoreType.DMA((2,)),
            pltpu.SemaphoreType.DMA((4,)),
        ],
        compiler_params=pltpu.CompilerParams(vmem_limit_bytes=16 * MIB),
        name="pack",
    )(in_hbm(owner.reshape(1, tokens)), in_hbm(latent))
    packed, up_kernel = lax.optimization_barrier((packed, up_kernel))
    received = lax.all_to_all(packed, "tm", split_axis=0, concat_axis=0, tiled=True)
    res_kernel = res_kernel.reshape(3, 9 * channels, channels)
    one_tap = (9 * channels, channels)
    res_kernel = in_hbm(res_kernel)
    folded, small, keep, here, behind, far, solo = pl.pallas_call(
        prepare_kernel,
        out_shape=[
            pltpu.HBM((2, 2, 4 * channels, outs), bf16),
            pltpu.VMEM((8, wide), f32),
            pltpu.VMEM((8, 128), f32),
            pltpu.VMEM(one_tap, bf16),
            pltpu.HBM(one_tap, bf16),
            pltpu.HBM(one_tap, bf16),
            pltpu.SMEM((1,), jnp.int32),
        ],
        in_specs=[SM] * 2 + [VM] * 5 + [HB] * 2,
        out_specs=[HB] + [VM] * 3 + [HB] * 2 + [SM],
        scratch_shapes=[
            pltpu.VMEM((3, 3, outs, channels), bf16),
            pltpu.VMEM((2, 2, 4 * channels, outs), bf16),
            pltpu.VMEM(one_tap, bf16),
            pltpu.VMEM(one_tap, bf16),
            pltpu.SemaphoreType.DMA((4,)),
            pltpu.SemaphoreType.DMA((3,)),
        ],
        compiler_params=pltpu.CompilerParams(vmem_limit_bytes=20 * MIB),
        cost_estimate=pl.CostEstimate(
            flops=0, bytes_accessed=2 * res_kernel.size * 2, transcendentals=0
        ),
        name="prepare",
    )(
        frame_counts,
        position,
        norm_gain.reshape(1, channels),
        norm_shift.reshape(1, channels),
        res_bias.reshape(1, channels),
        time_bias.reshape(1, wide),
        up_bias.reshape(1, outs),
        in_hbm(jnp.swapaxes(up_kernel, 2, 3)),
        res_kernel,
    )

    def call(body, name, outputs, arguments, scratch=(), share=1.0, **more):
        out_specs = more.pop("out_specs", [VM] * len(outputs))
        in_specs = more.pop("in_specs", [VM] * len(arguments))
        return pl.pallas_call(
            body,
            out_shape=outputs,
            in_specs=in_specs,
            out_specs=out_specs,
            scratch_shapes=scratch,
            compiler_params=pltpu.CompilerParams(vmem_limit_bytes=12 * MIB),
            cost_estimate=pl.CostEstimate(
                flops=int(share * tap), bytes_accessed=0, transcendentals=0
            ),
            name=name,
            **more,
        )(*arguments)

    vm = in_vmem
    frame16 = pltpu.VMEM((pixels, channels), bf16)
    frame32 = pltpu.VMEM((pixels, channels), f32)
    near_shape = pltpu.VMEM((pixels, 9 * channels), bf16)
    tap = 2 * pixels * 9 * channels * channels
    sem = pltpu.SemaphoreType.DMA
    small, keep, received = vm(small), vm(keep), vm(received)
    decoded1, active1, place = call(
        functools.partial(unpack_second_kernel, peers=peers, capacity=capacity),
        "unpack_second",
        [frame16] * 2 + [pltpu.VMEM((1, peers * capacity), jnp.int32)],
        [received, small],
        share=3,
    )
    prior1 = from_behind(active1, "tm")
    decoded0, active0 = call(
        unpack_first_kernel, "unpack_first", [frame16] * 2, [received, small, vm(place)], share=0
    )
    prior0 = from_behind(active0, "tm")
    behind, far = vm(behind), vm(far)
    sum0, sum1 = call(
        local_conv_kernel,
        "local_conv",
        [frame32] * 2,
        [keep, vm(active0), vm(active1), vm(here), behind],
        share=3,
    )
    second, near = call(
        second_residual_kernel,
        "second_residual",
        [frame16, near_shape],
        [solo, keep, small, vm(prior1), far, vm(sum1), vm(decoded1)],
        in_specs=[SM] + [VM] * 6,
        share=1,
    )
    prior_second = from_behind(second, "tm")
    (sum0,) = call(
        behind_kernel,
        "behind",
        [frame32],
        [solo, keep, small, vm(near), behind, vm(sum0), vm(decoded0)],
        in_specs=[SM] + [VM] * 6,
        share=1,
    )
    (first,) = call(
        first_residual_kernel,
        "first_residual",
        [frame16],
        [solo, keep, vm(prior0), far, vm(sum0)],
        in_specs=[SM] + [VM] * 4,
        share=1,
    )
    prior_first = from_behind(first, "tm")
    times = vm(time_kernel)
    time0, time1 = call(
        local_time_kernel,
        "local_time",
        [pltpu.VMEM((pixels, wide), f32)] * 2,
        [keep, small, vm(first), vm(second), times],
        share=0.4,
    )
    frames = 2 * tokens // pixels
    shape = (frames, 2 * H, 2 * W * outs)
    up_scratch = [
        pltpu.VMEM((2 * pixels + 3 * H, 3 * channels), bf16),
        pltpu.VMEM((2, 2 * W * outs // 128, 2 * H, 128), f32),
    ]
    folded, prior_second = vm(folded), vm(prior_second)
    time0, time1 = vm(time0), vm(time1)
    half_shape = (frames // 2,) + shape[1:]
    (early,) = call(
        early_up_kernel,
        "early_up",
        [jax.ShapeDtypeStruct(shape, bf16)],
        [solo, small, time0, time1, folded],
        [pltpu.VMEM(shape, bf16)] + up_scratch + [sem((2,))],
        share=2,
        in_specs=[SM] + [VM] * 4,
        out_specs=[HB],
    )
    (later,) = call(
        second_up_kernel,
        "second_up",
        [pltpu.VMEM(half_shape, bf16)],
        [solo, keep, small, prior_second, times, time1, folded],
        up_scratch,
        share=6,
        in_specs=[SM] + [VM] * 6,
    )
    (made,) = call(
        first_up_kernel,
        "first_up",
        [jax.ShapeDtypeStruct(shape, bf16)],
        [
            solo, keep, small, vm(prior_first), prior_second, times, time0, folded, vm(later),
            early,
        ],
        [pltpu.VMEM(half_shape, bf16)] + up_scratch + [sem((2,))],
        share=6,
        in_specs=[SM] + [VM] * 8 + [pl.BlockSpec(memory_space=pl.ANY)],
        out_specs=[HB],
        input_output_aliases={9: 0},
    )
    return made


def solution(mesh):
    placed = (
        P(("groups", "tm"), None),
        P(("groups", "tm")),
        P("groups"),
        P(),
        P(),
        P(),
        P(),
        P(),
        P(),
        P(),
        P(),
    )
    return jax.shard_map(
        on_device,
        mesh=mesh,
        in_specs=placed,
        out_specs=P(("groups", "tm"), None, None),
        check_vma=False,
    )
```

```python
import functools

import jax
import jax.numpy as jnp
from jax import lax
from jax.experimental import pallas as pl
from jax.experimental.pallas import tpu as pltpu
from jax.sharding import PartitionSpec as P

H = 16
W = 16
MARK = 128.0
epsilon = 1e-06
MIB = 1 << 20
f32 = jnp.float32
bf16 = jnp.bfloat16


def in_vmem(value):
    return pltpu.with_memory_space_constraint(value, pltpu.VMEM)


def in_hbm(value):
    return pltpu.with_memory_space_constraint(value, pltpu.HBM)


VM = pl.BlockSpec(memory_space=pltpu.VMEM)
HB = pl.BlockSpec(memory_space=pltpu.HBM)
SM = pl.BlockSpec(memory_space=pltpu.SMEM)


def iota(shape, dim):
    return lax.broadcasted_iota(jnp.int32, shape, dim)


def mm(lhs, rhs):
    return jnp.dot(lhs, rhs, preferred_element_type=f32)


def convolve(near, taps):
    return lax.dot_general(taps, near, (((0,), (1,)), ((), ())), preferred_element_type=f32).T


def from_behind(value, axis):
    size = lax.axis_size(axis)
    return lax.ppermute(value, axis, [(i, (i + 1) % size) for i in range(size)])


def pack_kernel(
    owner_hbm, latent_hbm, out_hbm, owner_ref, wide_ref, made_ref, arrived, left, *, peers, capacity
):
    tokens, channels = latent_hbm.shape
    copies = [
        pltpu.make_async_copy(owner_hbm, owner_ref, arrived.at[0]),
        pltpu.make_async_copy(latent_hbm, wide_ref.at[:, :channels], arrived.at[1]),
    ]
    for copy in copies:
        copy.start()
    wide_ref[:, channels:] = jnp.ones((tokens, 128), bf16)
    upper = (iota((tokens, tokens), 0) <= iota((tokens, tokens), 1)).astype(bf16)
    copies[0].wait()
    owner = owner_ref[...]
    marked = iota((peers, tokens), 0) == owner
    running = mm(marked.astype(bf16), upper)
    rank = jnp.sum(jnp.where(marked, running - 1.0, 0.0), 0, keepdims=True)
    slot = owner * capacity + rank.astype(jnp.int32)
    copies[1].wait()
    pieces = left.shape[0]
    rows = peers * capacity // pieces
    sent = []
    for piece in range(pieces):
        at = pl.ds(piece * rows, rows)
        chosen = (iota((rows, tokens), 0) + piece * rows == slot).astype(bf16)
        found = mm(chosen, wide_ref[...])
        empty = (1.0 - found[:, channels:]) * MARK
        made_ref[at] = (
            found[:, :channels] + jnp.concatenate([empty] * (channels // 128), 1)
        ).astype(bf16)
        copy = pltpu.make_async_copy(made_ref.at[at], out_hbm.at[at], left.at[piece])
        copy.start()
        sent.append(copy)
    for copy in sent:
        copy.wait()


def places(got_ref, peers, capacity):
    slots = got_ref.shape[0]
    present = (got_ref[:, :128] < MARK / 2).astype(bf16)
    sender = iota((peers, slots), 1) // capacity
    member = (sender == iota((peers, slots), 0)).astype(f32)
    below = (sender < iota((peers, slots), 0)).astype(f32)
    tallies = mm(jnp.concatenate([member, below], 0).astype(bf16), present)
    held = jnp.sum(member * tallies[:peers, :1], 0, keepdims=True).astype(jnp.int32)
    first = jnp.sum(member * tallies[peers:, :1], 0, keepdims=True).astype(jnp.int32)
    within = iota((1, slots), 1) % capacity
    return jnp.where(within < held, first + within, -1)


def unpack(place, got_ref, small_ref, decoded_ref, active_ref, frame):
    slots, channels = got_ref.shape
    pixels = decoded_ref.shape[0]
    pixel = iota((pixels, slots), 0)
    source = frame * pixels + (pixel % H) * W + pixel // H
    chosen = (source == place).astype(bf16)
    values = mm(chosen, got_ref[...])
    decoded_ref[...] = values.astype(bf16)
    squares = jnp.mean(values * values, -1, keepdims=True)
    scaled = values * lax.rsqrt(squares + epsilon)
    fed = scaled * small_ref[0:1, :channels] + small_ref[1:2, :channels]
    active_ref[...] = (fed / (1.0 + jnp.exp(-fed))).astype(bf16)


def unpack_second_kernel(
    got_ref, small_ref, decoded_ref, active_ref, place_ref, *, peers, capacity
):
    place = places(got_ref, peers, capacity)
    place_ref[...] = place
    unpack(place, got_ref, small_ref, decoded_ref, active_ref, 1)


def unpack_first_kernel(got_ref, small_ref, place_ref, decoded_ref, active_ref):
    unpack(place_ref[...], got_ref, small_ref, decoded_ref, active_ref, 0)


def vertical(frame):
    wide = frame.astype(f32)
    y = iota(wide.shape, 0) % H
    up = jnp.where(y == 0, 0.0, pltpu.roll(wide, 1, 0))
    down = jnp.where(y == H - 1, 0.0, pltpu.roll(wide, wide.shape[0] - 1, 0))
    return up.astype(bf16), frame, down.astype(bf16)


def steps(frame):
    wide = frame.astype(f32)
    up, here, down = vertical(frame)
    return (up.astype(f32) - wide).astype(bf16), here, (down.astype(f32) - wide).astype(bf16)


def patches(frame):
    pixels, channels = frame.shape
    nothing = jnp.zeros((H, channels), bf16)
    parts = []
    for shifted in vertical(frame):
        parts.append(jnp.concatenate([nothing, shifted[: pixels - H]], 0))
        parts.append(shifted)
        parts.append(jnp.concatenate([shifted[H:], nothing], 0))
    return jnp.concatenate(parts, 1)


def kept(keep_ref):
    return [[keep_ref[3 * f + back : 3 * f + back + 1, :1] for back in range(3)] for f in range(2)]


def local_conv_kernel(
    keep_ref, first_ref, second_ref, here_ref, behind_ref, sum0_ref, sum1_ref
):
    keep = kept(keep_ref)
    channels = sum0_ref.shape[1]
    sum1 = convolve(patches(second_ref[...]), here_ref[...])
    both = mm(
        patches(first_ref[...]), jnp.concatenate([here_ref[...], behind_ref[...]], 1)
    )
    sum0_ref[...] = both[:, :channels]
    sum1_ref[...] = sum1 + keep[1][1] * both[:, channels:]


def second_residual_kernel(
    solo_ref, keep_ref, small_ref, prior_ref, far_ref, sum_ref, decoded_ref, out_ref, near_ref
):
    base = sum_ref[...] + decoded_ref[...].astype(f32) + small_ref[2:3, : out_ref.shape[1]]


    @pl.when(solo_ref[0] == 1)
    def _():
        out_ref[...] = base.astype(bf16)

    @pl.when(solo_ref[0] == 0)
    def _():
        near = patches(prior_ref[...])
        near_ref[...] = near
        far = kept(keep_ref)[1][2] * convolve(near, far_ref[...])
        out_ref[...] = (base + far).astype(bf16)


def behind_kernel(
    solo_ref, keep_ref, small_ref, near_ref, behind_ref, sum_ref, decoded_ref, out_ref
):
    base = sum_ref[...] + decoded_ref[...].astype(f32) + small_ref[2:3, : out_ref.shape[1]]

    @pl.when(solo_ref[0] == 1)
    def _():
        out_ref[...] = base

    @pl.when(solo_ref[0] == 0)
    def _():
        out_ref[...] = base + kept(keep_ref)[0][1] * convolve(near_ref[...], behind_ref[...])


def first_residual_kernel(solo_ref, keep_ref, prior_ref, far_ref, sum_ref, out_ref):

    @pl.when(solo_ref[0] == 1)
    def _():
        out_ref[...] = sum_ref[...].astype(bf16)

    @pl.when(solo_ref[0] == 0)
    def _():
        far = kept(keep_ref)[0][2] * convolve(patches(prior_ref[...]), far_ref[...])
        out_ref[...] = (sum_ref[...] + far).astype(bf16)


def local_time_kernel(
    keep_ref, small_ref, first_ref, second_ref, time_ref, sum0_ref, sum1_ref
):
    keep = kept(keep_ref)
    bias = small_ref[3:4, : sum0_ref.shape[1]]
    sum0_ref[...] = mm(first_ref[...], time_ref[2]) + bias
    sum1_ref[...] = (
        mm(second_ref[...], time_ref[2]) + bias + keep[1][1] * mm(first_ref[...], time_ref[1])
    )


def upscale(temporal, frame, small_ref, folded_ref, made_ref, near, rows32, ready=()):
    pixels = H * W
    channels = near.shape[1] // 3
    outs = folded_ref.shape[3]
    both = temporal.astype(bf16)
    nothing = jnp.zeros((H, 3 * channels), bf16)
    for half in range(2):
        base = H + half * (pixels + H)
        near[base - H : base] = nothing
        shown = both[:, half * channels : (half + 1) * channels]
        for t, part in enumerate(steps(shown)):
            near[base : base + pixels, t * channels : (t + 1) * channels] = part
    near[2 * (H + pixels) :] = nothing
    span = 2 * pixels + H
    bias = small_ref[4:5, :outs]
    blocks = 2 * outs // 128
    products = []
    for q in range(2):
        for t in range(3):
            windows = [
                near[(q + side) * H : (q + side) * H + span, t * channels : (t + 1) * channels]
                for side in range(2)
            ]
            products.append(mm(jnp.concatenate(windows, 1), folded_ref[q, t]))
    for p in range(2):
        pair = jnp.concatenate(
            [products[3 * q + 1] + bias + products[3 * q + 2 * p] for q in range(2)], 1
        )
        for half in range(2):
            for x in range(W):
                row = half * (pixels + H) + x * H
                for block in range(blocks):
                    rows32[half, x * blocks + block, pl.ds(p, H, stride=2)] = pair[
                        row : row + H, block * 128 : (block + 1) * 128
                    ]
    for half in range(2):
        for block in range(W * blocks):
            made_ref[2 * frame + half, :, block * 128 : (block + 1) * 128] = rows32[
                half, block
            ].astype(bf16)
        for copy in ready[half : half + 1]:
            copy.start()


def early_up_kernel(
    solo_ref, small_ref, sum0_ref, sum1_ref, folded_ref, out_hbm, made_ref, near, rows32, left
):
    @pl.when(solo_ref[0] == 1)
    def _():
        copies = [
            pltpu.make_async_copy(made_ref.at[e], out_hbm.at[e], left.at[e]) for e in range(4)
        ]
        for f, sum_ref in ((1, sum1_ref), (0, sum0_ref)):
            ready = copies[2 * f : 2 * f + 2]
            upscale(sum_ref[...], f, small_ref, folded_ref, made_ref, near, rows32, ready)
        for copy in copies:
            copy.wait()


def second_up_kernel(
    solo_ref, keep_ref, small_ref, prior_ref, time_ref, sum_ref, folded_ref, made_ref, near, rows32
):
    @pl.when(solo_ref[0] == 0)
    def _():
        temporal = sum_ref[...] + kept(keep_ref)[1][2] * mm(prior_ref[...], time_ref[0])
        upscale(temporal, 0, small_ref, folded_ref, made_ref, near, rows32)


def first_up_kernel(
    solo_ref, keep_ref, small_ref, before_ref, prior_ref, time_ref, sum_ref, folded_ref,
    later_ref, early_hbm, out_hbm,
    made_ref, near, rows32, left,
):
    @pl.when(solo_ref[0] == 0)
    def _():
        later = pltpu.make_async_copy(later_ref, out_hbm.at[2:4], left.at[0])
        later.start()
        seen = [keep_ref[row : row + 1, :1].astype(bf16) for row in (2, 1)]
        pair = jnp.concatenate([before_ref[...] * seen[0], prior_ref[...] * seen[1]], 1)
        both = time_ref[:2].reshape(pair.shape[1], time_ref.shape[2])
        temporal = sum_ref[...] + mm(pair, both)
        copies = [
            pltpu.make_async_copy(made_ref.at[e], out_hbm.at[e], left.at[1 + e]) for e in range(2)
        ]
        upscale(temporal, 0, small_ref, folded_ref, made_ref, near, rows32, copies)
        for copy in copies:
            copy.wait()
        later.wait()


def keeps(counts_ref, position_ref):
    first = position_ref[0] * 2
    starts = [jnp.int32(0), jnp.int32(0)]
    end = jnp.int32(0)
    for video in range(counts_ref.shape[0]):
        end = end + counts_ref[video]
        starts = [jnp.where(end <= first + f, end, starts[f]) for f in range(2)]
    return [
        [(first + f - back >= starts[f]).astype(f32) for back in range(3)] for f in range(2)
    ]


def halves(taps):
    return (taps[0], taps[1] + taps[2]), (taps[0] + taps[1], taps[2])


def prepare_kernel(
    counts_ref, position_ref, gain_ref, shift_ref, res_bias_ref, time_bias_ref, up_bias_ref,
    up_hbm, taps_hbm,
    folded_hbm, small_ref, keep_ref, here_ref, behind_hbm, far_hbm, solo_ref,
    up_ref, folded_ref, behind_ref, far_ref, arrived, left,
):
    copies = [
        pltpu.make_async_copy(up_hbm, up_ref, arrived.at[0]),
        pltpu.make_async_copy(taps_hbm.at[2], here_ref, arrived.at[1]),
        pltpu.make_async_copy(taps_hbm.at[1], behind_ref, arrived.at[2]),
        pltpu.make_async_copy(taps_hbm.at[0], far_ref, arrived.at[3]),
    ]
    for copy in copies:
        copy.start()
    small_ref[...] = jnp.zeros_like(small_ref)
    for i, ref in enumerate((gain_ref, shift_ref, res_bias_ref, time_bias_ref, up_bias_ref)):
        small_ref[i : i + 1, : ref.shape[1]] = ref[...]
    keep = keeps(counts_ref, position_ref)
    solo_ref[0] = (keep[0][1] == 0.0).astype(jnp.int32)
    row = iota(keep_ref.shape, 0)
    seen = jnp.zeros(keep_ref.shape, f32)
    for f in range(2):
        for back in range(3):
            seen = jnp.where(row == 3 * f + back, keep[f][back], seen)
    keep_ref[...] = seen
    copies[0].wait()
    channels = up_ref.shape[3]
    rows = [[up_ref[a, b].astype(f32) for b in range(3)] for a in range(3)]
    rows[1] = [rows[0][b] + rows[1][b] + rows[2][b] for b in range(3)]
    for t in range(3):
        columns = halves(rows[t])
        for q in range(2):
            for side in range(2):
                folded_ref[q, t, side * channels : (side + 1) * channels] = columns[q][
                    side
                ].T.astype(bf16)
    for copy in copies[1:]:
        copy.wait()
    sent = [
        pltpu.make_async_copy(behind_ref, behind_hbm, left.at[0]),
        pltpu.make_async_copy(far_ref, far_hbm, left.at[1]),
        pltpu.make_async_copy(folded_ref, folded_hbm, left.at[2]),
    ]
    for copy in sent:
        copy.start()
    for copy in sent:
        copy.wait()


def on_device(
    latent,
    owner,
    frame_counts,
    norm_gain,
    norm_shift,
    res_kernel,
    res_bias,
    time_kernel,
    time_bias,
    up_kernel,
    up_bias,
):
    peers = lax.axis_size("tm")
    position = lax.axis_index("tm").astype(jnp.int32).reshape(1)
    tokens, channels = latent.shape
    capacity = 2 * tokens // peers
    pixels = H * W
    wide = time_kernel.shape[-1]
    outs = up_kernel.shape[-1]

    packed = pl.pallas_call(
        functools.partial(pack_kernel, peers=peers, capacity=capacity),
        out_shape=jax.ShapeDtypeStruct((peers * capacity, channels), bf16),
        in_specs=[HB, HB],
        out_specs=HB,
        scratch_shapes=[
            pltpu.VMEM((1, tokens), jnp.int32),
            pltpu.VMEM((tokens, channels + 128), bf16),
            pltpu.VMEM((peers * capacity, channels), bf16),
            pltpu.SemaphoreType.DMA((2,)),
            pltpu.SemaphoreType.DMA((4,)),
        ],
        compiler_params=pltpu.CompilerParams(vmem_limit_bytes=16 * MIB),
        name="pack",
    )(in_hbm(owner.reshape(1, tokens)), in_hbm(latent))
    packed, up_kernel = lax.optimization_barrier((packed, up_kernel))
    received = lax.all_to_all(packed, "tm", split_axis=0, concat_axis=0, tiled=True)
    res_kernel = res_kernel.reshape(3, 9 * channels, channels)
    one_tap = (9 * channels, channels)
    res_kernel = in_hbm(res_kernel)
    folded, small, keep, here, behind, far, solo = pl.pallas_call(
        prepare_kernel,
        out_shape=[
            pltpu.HBM((2, 3, 2 * channels, outs), bf16),
            pltpu.VMEM((8, wide), f32),
            pltpu.VMEM((8, 128), f32),
            pltpu.VMEM(one_tap, bf16),
            pltpu.HBM(one_tap, bf16),
            pltpu.HBM(one_tap, bf16),
            pltpu.SMEM((1,), jnp.int32),
        ],
        in_specs=[SM] * 2 + [VM] * 5 + [HB] * 2,
        out_specs=[HB] + [VM] * 3 + [HB] * 2 + [SM],
        scratch_shapes=[
            pltpu.VMEM((3, 3, outs, channels), bf16),
            pltpu.VMEM((2, 3, 2 * channels, outs), bf16),
            pltpu.VMEM(one_tap, bf16),
            pltpu.VMEM(one_tap, bf16),
            pltpu.SemaphoreType.DMA((4,)),
            pltpu.SemaphoreType.DMA((3,)),
        ],
        compiler_params=pltpu.CompilerParams(vmem_limit_bytes=20 * MIB),
        cost_estimate=pl.CostEstimate(
            flops=0, bytes_accessed=2 * res_kernel.size * 2, transcendentals=0
        ),
        name="prepare",
    )(
        frame_counts,
        position,
        norm_gain.reshape(1, channels),
        norm_shift.reshape(1, channels),
        res_bias.reshape(1, channels),
        time_bias.reshape(1, wide),
        up_bias.reshape(1, outs),
        in_hbm(jnp.swapaxes(up_kernel, 2, 3)),
        res_kernel,
    )

    def call(body, name, outputs, arguments, scratch=(), share=1.0, **more):
        out_specs = more.pop("out_specs", [VM] * len(outputs))
        in_specs = more.pop("in_specs", [VM] * len(arguments))
        return pl.pallas_call(
            body,
            out_shape=outputs,
            in_specs=in_specs,
            out_specs=out_specs,
            scratch_shapes=scratch,
            compiler_params=pltpu.CompilerParams(vmem_limit_bytes=12 * MIB),
            cost_estimate=pl.CostEstimate(
                flops=int(share * tap), bytes_accessed=0, transcendentals=0
            ),
            name=name,
            **more,
        )(*arguments)

    vm = in_vmem
    frame16 = pltpu.VMEM((pixels, channels), bf16)
    frame32 = pltpu.VMEM((pixels, channels), f32)
    near_shape = pltpu.VMEM((pixels, 9 * channels), bf16)
    tap = 2 * pixels * 9 * channels * channels
    sem = pltpu.SemaphoreType.DMA
    small, keep, received = vm(small), vm(keep), vm(received)
    decoded1, active1, place = call(
        functools.partial(unpack_second_kernel, peers=peers, capacity=capacity),
        "unpack_second",
        [frame16] * 2 + [pltpu.VMEM((1, peers * capacity), jnp.int32)],
        [received, small],
        share=3,
    )
    prior1 = from_behind(active1, "tm")
    decoded0, active0 = call(
        unpack_first_kernel, "unpack_first", [frame16] * 2, [received, small, vm(place)], share=0
    )
    prior0 = from_behind(active0, "tm")
    behind, far = vm(behind), vm(far)
    sum0, sum1 = call(
        local_conv_kernel,
        "local_conv",
        [frame32] * 2,
        [keep, vm(active0), vm(active1), vm(here), behind],
        share=3,
    )
    second, near = call(
        second_residual_kernel,
        "second_residual",
        [frame16, near_shape],
        [solo, keep, small, vm(prior1), far, vm(sum1), vm(decoded1)],
        in_specs=[SM] + [VM] * 6,
        share=1,
    )
    prior_second = from_behind(second, "tm")
    (sum0,) = call(
        behind_kernel,
        "behind",
        [frame32],
        [solo, keep, small, vm(near), behind, vm(sum0), vm(decoded0)],
        in_specs=[SM] + [VM] * 6,
        share=1,
    )
    (first,) = call(
        first_residual_kernel,
        "first_residual",
        [frame16],
        [solo, keep, vm(prior0), far, vm(sum0)],
        in_specs=[SM] + [VM] * 4,
        share=1,
    )
    prior_first = from_behind(first, "tm")
    times = vm(time_kernel)
    time0, time1 = call(
        local_time_kernel,
        "local_time",
        [pltpu.VMEM((pixels, wide), f32)] * 2,
        [keep, small, vm(first), vm(second), times],
        share=0.4,
    )
    frames = 2 * tokens // pixels
    shape = (frames, 2 * H, 2 * W * outs)
    up_scratch = [
        pltpu.VMEM((2 * pixels + 3 * H, 3 * channels), bf16),
        pltpu.VMEM((2, 2 * W * outs // 128, 2 * H, 128), f32),
    ]
    folded, prior_second = vm(folded), vm(prior_second)
    time0, time1 = vm(time0), vm(time1)
    half_shape = (frames // 2,) + shape[1:]
    (early,) = call(
        early_up_kernel,
        "early_up",
        [jax.ShapeDtypeStruct(shape, bf16)],
        [solo, small, time0, time1, folded],
        [pltpu.VMEM(shape, bf16)] + up_scratch + [sem((4,))],
        share=2,
        in_specs=[SM] + [VM] * 4,
        out_specs=[HB],
    )
    (later,) = call(
        second_up_kernel,
        "second_up",
        [pltpu.VMEM(half_shape, bf16)],
        [solo, keep, small, prior_second, times, time1, folded],
        up_scratch,
        share=6,
        in_specs=[SM] + [VM] * 6,
    )
    (made,) = call(
        first_up_kernel,
        "first_up",
        [jax.ShapeDtypeStruct(shape, bf16)],
        [
            solo, keep, small, vm(prior_first), prior_second, times, time0, folded, vm(later),
            early,
        ],
        [pltpu.VMEM(half_shape, bf16)] + up_scratch + [sem((3,))],
        share=6,
        in_specs=[SM] + [VM] * 8 + [pl.BlockSpec(memory_space=pl.ANY)],
        out_specs=[HB],
        input_output_aliases={9: 0},
    )
    return made


def solution(mesh):
    placed = (
        P(("groups", "tm"), None),
        P(("groups", "tm")),
        P("groups"),
        P(),
        P(),
        P(),
        P(),
        P(),
        P(),
        P(),
        P(),
    )
    return jax.shard_map(
        on_device,
        mesh=mesh,
        in_specs=placed,
        out_specs=P(("groups", "tm"), None, None),
        check_vma=False,
    )
```

```python
import functools

import jax
import jax.numpy as jnp
from jax import lax
from jax.experimental import pallas as pl
from jax.experimental.pallas import tpu as pltpu
from jax.sharding import PartitionSpec as P

H = 16
W = 16
MARK = 128.0
epsilon = 1e-06
MIB = 1 << 20
f32 = jnp.float32
bf16 = jnp.bfloat16


def in_vmem(value):
    return pltpu.with_memory_space_constraint(value, pltpu.VMEM)


def in_hbm(value):
    return pltpu.with_memory_space_constraint(value, pltpu.HBM)


VM = pl.BlockSpec(memory_space=pltpu.VMEM)
HB = pl.BlockSpec(memory_space=pltpu.HBM)
SM = pl.BlockSpec(memory_space=pltpu.SMEM)


def iota(shape, dim):
    return lax.broadcasted_iota(jnp.int32, shape, dim)


def mm(lhs, rhs):
    return jnp.dot(lhs, rhs, preferred_element_type=f32)


def convolve(near, taps):
    return lax.dot_general(taps, near, (((0,), (1,)), ((), ())), preferred_element_type=f32).T


def from_behind(value, axis):
    size = lax.axis_size(axis)
    return lax.ppermute(value, axis, [(i, (i + 1) % size) for i in range(size)])


def pack_kernel(
    owner_hbm, latent_hbm, out_hbm, owner_ref, wide_ref, made_ref, arrived, left, *, peers, capacity
):
    tokens, channels = latent_hbm.shape
    copies = [
        pltpu.make_async_copy(owner_hbm, owner_ref, arrived.at[0]),
        pltpu.make_async_copy(latent_hbm, wide_ref.at[:, :channels], arrived.at[1]),
    ]
    for copy in copies:
        copy.start()
    wide_ref[:, channels:] = jnp.ones((tokens, 128), bf16)
    upper = (iota((tokens, tokens), 0) <= iota((tokens, tokens), 1)).astype(bf16)
    copies[0].wait()
    owner = owner_ref[...]
    marked = iota((peers, tokens), 0) == owner
    running = mm(marked.astype(bf16), upper)
    rank = jnp.sum(jnp.where(marked, running - 1.0, 0.0), 0, keepdims=True)
    slot = owner * capacity + rank.astype(jnp.int32)
    copies[1].wait()
    pieces = left.shape[0]
    rows = peers * capacity // pieces
    sent = []
    for piece in range(pieces):
        at = pl.ds(piece * rows, rows)
        chosen = (iota((rows, tokens), 0) + piece * rows == slot).astype(bf16)
        found = mm(chosen, wide_ref[...])
        empty = (1.0 - found[:, channels:]) * MARK
        made_ref[at] = (
            found[:, :channels] + jnp.concatenate([empty] * (channels // 128), 1)
        ).astype(bf16)
        copy = pltpu.make_async_copy(made_ref.at[at], out_hbm.at[at], left.at[piece])
        copy.start()
        sent.append(copy)
    for copy in sent:
        copy.wait()


def places(got_ref, peers, capacity):
    slots = got_ref.shape[0]
    present = (got_ref[:, :128] < MARK / 2).astype(bf16)
    sender = iota((peers, slots), 1) // capacity
    member = (sender == iota((peers, slots), 0)).astype(f32)
    below = (sender < iota((peers, slots), 0)).astype(f32)
    tallies = mm(jnp.concatenate([member, below], 0).astype(bf16), present)
    held = jnp.sum(member * tallies[:peers, :1], 0, keepdims=True).astype(jnp.int32)
    first = jnp.sum(member * tallies[peers:, :1], 0, keepdims=True).astype(jnp.int32)
    within = iota((1, slots), 1) % capacity
    return jnp.where(within < held, first + within, -1)


def unpack(place, got_ref, small_ref, decoded_ref, active_ref, frame):
    slots, channels = got_ref.shape
    pixels = decoded_ref.shape[0]
    pixel = iota((pixels, slots), 0)
    source = frame * pixels + (pixel % H) * W + pixel // H
    chosen = (source == place).astype(bf16)
    values = mm(chosen, got_ref[...])
    decoded_ref[...] = values.astype(bf16)
    squares = jnp.mean(values * values, -1, keepdims=True)
    scaled = values * lax.rsqrt(squares + epsilon)
    fed = scaled * small_ref[0:1, :channels] + small_ref[1:2, :channels]
    active_ref[...] = (fed / (1.0 + jnp.exp(-fed))).astype(bf16)


def unpack_second_kernel(
    got_ref, small_ref, decoded_ref, active_ref, place_ref, *, peers, capacity
):
    place = places(got_ref, peers, capacity)
    place_ref[...] = place
    unpack(place, got_ref, small_ref, decoded_ref, active_ref, 1)


def unpack_first_kernel(got_ref, small_ref, place_ref, decoded_ref, active_ref):
    unpack(place_ref[...], got_ref, small_ref, decoded_ref, active_ref, 0)


def vertical(frame):
    wide = frame.astype(f32)
    y = iota(wide.shape, 0) % H
    up = jnp.where(y == 0, 0.0, pltpu.roll(wide, 1, 0))
    down = jnp.where(y == H - 1, 0.0, pltpu.roll(wide, wide.shape[0] - 1, 0))
    return up.astype(bf16), frame, down.astype(bf16)


def steps(frame):
    wide = frame.astype(f32)
    up, here, down = vertical(frame)
    return (up.astype(f32) - wide).astype(bf16), here, (down.astype(f32) - wide).astype(bf16)


def patches(frame):
    pixels, channels = frame.shape
    nothing = jnp.zeros((H, channels), bf16)
    parts = []
    for shifted in vertical(frame):
        parts.append(jnp.concatenate([nothing, shifted[: pixels - H]], 0))
        parts.append(shifted)
        parts.append(jnp.concatenate([shifted[H:], nothing], 0))
    return jnp.concatenate(parts, 1)


def kept(keep_ref):
    return [[keep_ref[3 * f + back : 3 * f + back + 1, :1] for back in range(3)] for f in range(2)]


def local_conv_kernel(
    keep_ref, small_ref, first_ref, second_ref, decoded0_ref, decoded1_ref, here_ref, behind_ref,
    sum0_ref, sum1_ref,
):
    keep = kept(keep_ref)
    channels = sum0_ref.shape[1]
    sum1 = convolve(patches(second_ref[...]), here_ref[...])
    both = mm(
        patches(first_ref[...]), jnp.concatenate([here_ref[...], behind_ref[...]], 1)
    )
    bias = small_ref[2:3, :channels]
    sum0_ref[...] = both[:, :channels] + decoded0_ref[...].astype(f32) + bias
    base = decoded1_ref[...].astype(f32) + bias
    sum1_ref[...] = sum1 + base + keep[1][1] * both[:, channels:]


def second_residual_kernel(
    solo_ref, keep_ref, prior_ref, far_ref, sum_ref, out_ref, near_ref
):
    @pl.when(solo_ref[0] == 1)
    def _():
        out_ref[...] = sum_ref[...].astype(bf16)

    @pl.when(solo_ref[0] == 0)
    def _():
        near = patches(prior_ref[...])
        near_ref[...] = near
        far = kept(keep_ref)[1][2] * convolve(near, far_ref[...])
        out_ref[...] = (sum_ref[...] + far).astype(bf16)


def behind_kernel(solo_ref, keep_ref, near_ref, behind_ref, sum_ref, out_ref):
    @pl.when(solo_ref[0] == 1)
    def _():
        out_ref[...] = sum_ref[...]

    @pl.when(solo_ref[0] == 0)
    def _():
        behind = convolve(near_ref[...], behind_ref[...])
        out_ref[...] = sum_ref[...] + kept(keep_ref)[0][1] * behind


def first_residual_kernel(solo_ref, keep_ref, prior_ref, far_ref, sum_ref, out_ref):

    @pl.when(solo_ref[0] == 1)
    def _():
        out_ref[...] = sum_ref[...].astype(bf16)

    @pl.when(solo_ref[0] == 0)
    def _():
        far = kept(keep_ref)[0][2] * convolve(patches(prior_ref[...]), far_ref[...])
        out_ref[...] = (sum_ref[...] + far).astype(bf16)


def local_time_kernel(
    keep_ref, small_ref, first_ref, second_ref, time_ref, sum0_ref, sum1_ref
):
    keep = kept(keep_ref)
    bias = small_ref[3:4, : sum0_ref.shape[1]]
    sum0_ref[...] = mm(first_ref[...], time_ref[2]) + bias
    sum1_ref[...] = (
        mm(second_ref[...], time_ref[2]) + bias + keep[1][1] * mm(first_ref[...], time_ref[1])
    )


def upscale(temporal, frame, small_ref, folded_ref, made_ref, near, rows32, ready=()):
    pixels = H * W
    channels = near.shape[1] // 3
    outs = folded_ref.shape[3]
    both = temporal.astype(bf16)
    nothing = jnp.zeros((H, 3 * channels), bf16)
    bias = small_ref[4:5, :outs]
    blocks = 2 * outs // 128
    stride = pixels + 2 * H
    for half in range(2):
        base = H + half * stride
        near[base - H : base] = nothing
        near[base + pixels : base + pixels + H] = nothing
        shown = both[:, half * channels : (half + 1) * channels]
        for t, part in enumerate(steps(shown)):
            near[base : base + pixels, t * channels : (t + 1) * channels] = part
    for half in range(2):
        products = []
        for q in range(2):
            for t in range(3):
                windows = [
                    near[
                        half * stride + (q + side) * H : half * stride + (q + side) * H + pixels,
                        t * channels : (t + 1) * channels,
                    ]
                    for side in range(2)
                ]
                products.append(mm(jnp.concatenate(windows, 1), folded_ref[q, t]))
        for p in range(2):
            pair = jnp.concatenate(
                [products[3 * q + 1] + bias + products[3 * q + 2 * p] for q in range(2)], 1
            )
            for x in range(W):
                for block in range(blocks):
                    rows32[half, x * blocks + block, pl.ds(p, H, stride=2)] = pair[
                        x * H : (x + 1) * H, block * 128 : (block + 1) * 128
                    ]
        for block in range(W * blocks):
            made_ref[2 * frame + half, :, block * 128 : (block + 1) * 128] = rows32[
                half, block
            ].astype(bf16)
        for copy in ready[half : half + 1]:
            copy.start()


def early_up_kernel(
    solo_ref, small_ref, sum0_ref, sum1_ref, folded_ref, out_hbm, made_ref, near, rows32, left
):
    @pl.when(solo_ref[0] == 1)
    def _():
        copies = [
            pltpu.make_async_copy(made_ref.at[e], out_hbm.at[e], left.at[e]) for e in range(4)
        ]
        for f, sum_ref in ((1, sum1_ref), (0, sum0_ref)):
            ready = copies[2 * f : 2 * f + 2]
            upscale(sum_ref[...], f, small_ref, folded_ref, made_ref, near, rows32, ready)
        for copy in copies:
            copy.wait()


def second_up_kernel(
    solo_ref, keep_ref, small_ref, prior_ref, time_ref, sum_ref, folded_ref, made_ref, near, rows32
):
    @pl.when(solo_ref[0] == 0)
    def _():
        temporal = sum_ref[...] + kept(keep_ref)[1][2] * mm(prior_ref[...], time_ref[0])
        upscale(temporal, 0, small_ref, folded_ref, made_ref, near, rows32)


def first_up_kernel(
    solo_ref, keep_ref, small_ref, before_ref, prior_ref, time_ref, sum_ref, folded_ref,
    later_ref, early_hbm, out_hbm,
    made_ref, near, rows32, left,
):
    @pl.when(solo_ref[0] == 0)
    def _():
        later = pltpu.make_async_copy(later_ref, out_hbm.at[2:4], left.at[0])
        later.start()
        seen = [keep_ref[row : row + 1, :1].astype(bf16) for row in (2, 1)]
        pair = jnp.concatenate([before_ref[...] * seen[0], prior_ref[...] * seen[1]], 1)
        both = time_ref[:2].reshape(pair.shape[1], time_ref.shape[2])
        temporal = sum_ref[...] + mm(pair, both)
        copies = [
            pltpu.make_async_copy(made_ref.at[e], out_hbm.at[e], left.at[1 + e]) for e in range(2)
        ]
        upscale(temporal, 0, small_ref, folded_ref, made_ref, near, rows32, copies)
        for copy in copies:
            copy.wait()
        later.wait()


def keeps(counts_ref, position_ref):
    first = position_ref[0] * 2
    starts = [jnp.int32(0), jnp.int32(0)]
    end = jnp.int32(0)
    for video in range(counts_ref.shape[0]):
        end = end + counts_ref[video]
        starts = [jnp.where(end <= first + f, end, starts[f]) for f in range(2)]
    return [
        [(first + f - back >= starts[f]).astype(f32) for back in range(3)] for f in range(2)
    ]


def halves(taps):
    return (taps[0], taps[1] + taps[2]), (taps[0] + taps[1], taps[2])


def prepare_kernel(
    counts_ref, position_ref, gain_ref, shift_ref, res_bias_ref, time_bias_ref, up_bias_ref,
    up_hbm, taps_hbm,
    folded_hbm, small_ref, keep_ref, here_ref, behind_hbm, far_hbm, solo_ref,
    up_ref, folded_ref, behind_ref, far_ref, arrived, left,
):
    copies = [
        pltpu.make_async_copy(up_hbm, up_ref, arrived.at[0]),
        pltpu.make_async_copy(taps_hbm.at[2], here_ref, arrived.at[1]),
        pltpu.make_async_copy(taps_hbm.at[1], behind_ref, arrived.at[2]),
        pltpu.make_async_copy(taps_hbm.at[0], far_ref, arrived.at[3]),
    ]
    for copy in copies:
        copy.start()
    small_ref[...] = jnp.zeros_like(small_ref)
    for i, ref in enumerate((gain_ref, shift_ref, res_bias_ref, time_bias_ref, up_bias_ref)):
        small_ref[i : i + 1, : ref.shape[1]] = ref[...]
    keep = keeps(counts_ref, position_ref)
    solo_ref[0] = (keep[0][1] == 0.0).astype(jnp.int32)
    row = iota(keep_ref.shape, 0)
    seen = jnp.zeros(keep_ref.shape, f32)
    for f in range(2):
        for back in range(3):
            seen = jnp.where(row == 3 * f + back, keep[f][back], seen)
    keep_ref[...] = seen
    copies[0].wait()
    channels = up_ref.shape[3]
    rows = [[up_ref[a, b].astype(f32) for b in range(3)] for a in range(3)]
    rows[1] = [rows[0][b] + rows[1][b] + rows[2][b] for b in range(3)]
    for t in range(3):
        columns = halves(rows[t])
        for q in range(2):
            for side in range(2):
                folded_ref[q, t, side * channels : (side + 1) * channels] = columns[q][
                    side
                ].T.astype(bf16)
    for copy in copies[1:]:
        copy.wait()
    sent = [
        pltpu.make_async_copy(behind_ref, behind_hbm, left.at[0]),
        pltpu.make_async_copy(far_ref, far_hbm, left.at[1]),
        pltpu.make_async_copy(folded_ref, folded_hbm, left.at[2]),
    ]
    for copy in sent:
        copy.start()
    for copy in sent:
        copy.wait()


def on_device(
    latent,
    owner,
    frame_counts,
    norm_gain,
    norm_shift,
    res_kernel,
    res_bias,
    time_kernel,
    time_bias,
    up_kernel,
    up_bias,
):
    peers = lax.axis_size("tm")
    position = lax.axis_index("tm").astype(jnp.int32).reshape(1)
    tokens, channels = latent.shape
    capacity = 2 * tokens // peers
    pixels = H * W
    wide = time_kernel.shape[-1]
    outs = up_kernel.shape[-1]

    packed = pl.pallas_call(
        functools.partial(pack_kernel, peers=peers, capacity=capacity),
        out_shape=jax.ShapeDtypeStruct((peers * capacity, channels), bf16),
        in_specs=[HB, HB],
        out_specs=HB,
        scratch_shapes=[
            pltpu.VMEM((1, tokens), jnp.int32),
            pltpu.VMEM((tokens, channels + 128), bf16),
            pltpu.VMEM((peers * capacity, channels), bf16),
            pltpu.SemaphoreType.DMA((2,)),
            pltpu.SemaphoreType.DMA((4,)),
        ],
        compiler_params=pltpu.CompilerParams(vmem_limit_bytes=16 * MIB),
        name="pack",
    )(in_hbm(owner.reshape(1, tokens)), in_hbm(latent))
    packed, up_kernel = lax.optimization_barrier((packed, up_kernel))
    received = lax.all_to_all(packed, "tm", split_axis=0, concat_axis=0, tiled=True)
    res_kernel = res_kernel.reshape(3, 9 * channels, channels)
    one_tap = (9 * channels, channels)
    res_kernel = in_hbm(res_kernel)
    folded, small, keep, here, behind, far, solo = pl.pallas_call(
        prepare_kernel,
        out_shape=[
            pltpu.HBM((2, 3, 2 * channels, outs), bf16),
            pltpu.VMEM((8, wide), f32),
            pltpu.VMEM((8, 128), f32),
            pltpu.VMEM(one_tap, bf16),
            pltpu.HBM(one_tap, bf16),
            pltpu.HBM(one_tap, bf16),
            pltpu.SMEM((1,), jnp.int32),
        ],
        in_specs=[SM] * 2 + [VM] * 5 + [HB] * 2,
        out_specs=[HB] + [VM] * 3 + [HB] * 2 + [SM],
        scratch_shapes=[
            pltpu.VMEM((3, 3, outs, channels), bf16),
            pltpu.VMEM((2, 3, 2 * channels, outs), bf16),
            pltpu.VMEM(one_tap, bf16),
            pltpu.VMEM(one_tap, bf16),
            pltpu.SemaphoreType.DMA((4,)),
            pltpu.SemaphoreType.DMA((3,)),
        ],
        compiler_params=pltpu.CompilerParams(vmem_limit_bytes=20 * MIB),
        cost_estimate=pl.CostEstimate(
            flops=0, bytes_accessed=2 * res_kernel.size * 2, transcendentals=0
        ),
        name="prepare",
    )(
        frame_counts,
        position,
        norm_gain.reshape(1, channels),
        norm_shift.reshape(1, channels),
        res_bias.reshape(1, channels),
        time_bias.reshape(1, wide),
        up_bias.reshape(1, outs),
        in_hbm(jnp.swapaxes(up_kernel, 2, 3)),
        res_kernel,
    )

    def call(body, name, outputs, arguments, scratch=(), share=1.0, **more):
        out_specs = more.pop("out_specs", [VM] * len(outputs))
        in_specs = more.pop("in_specs", [VM] * len(arguments))
        return pl.pallas_call(
            body,
            out_shape=outputs,
            in_specs=in_specs,
            out_specs=out_specs,
            scratch_shapes=scratch,
            compiler_params=pltpu.CompilerParams(vmem_limit_bytes=12 * MIB),
            cost_estimate=pl.CostEstimate(
                flops=int(share * tap), bytes_accessed=0, transcendentals=0
            ),
            name=name,
            **more,
        )(*arguments)

    vm = in_vmem
    frame16 = pltpu.VMEM((pixels, channels), bf16)
    frame32 = pltpu.VMEM((pixels, channels), f32)
    near_shape = pltpu.VMEM((pixels, 9 * channels), bf16)
    tap = 2 * pixels * 9 * channels * channels
    sem = pltpu.SemaphoreType.DMA
    small, keep, received = vm(small), vm(keep), vm(received)
    decoded1, active1, place = call(
        functools.partial(unpack_second_kernel, peers=peers, capacity=capacity),
        "unpack_second",
        [frame16] * 2 + [pltpu.VMEM((1, peers * capacity), jnp.int32)],
        [received, small],
        share=3,
    )
    prior1 = from_behind(active1, "tm")
    decoded0, active0 = call(
        unpack_first_kernel, "unpack_first", [frame16] * 2, [received, small, vm(place)], share=0
    )
    prior0 = from_behind(active0, "tm")
    behind, far = vm(behind), vm(far)
    sum0, sum1 = call(
        local_conv_kernel,
        "local_conv",
        [frame32] * 2,
        [
            keep, small, vm(active0), vm(active1), vm(decoded0), vm(decoded1), vm(here), behind,
        ],
        share=3,
    )
    second, near = call(
        second_residual_kernel,
        "second_residual",
        [frame16, near_shape],
        [solo, keep, vm(prior1), far, vm(sum1)],
        in_specs=[SM] + [VM] * 4,
        share=1,
    )
    prior_second = from_behind(second, "tm")
    (sum0,) = call(
        behind_kernel,
        "behind",
        [frame32],
        [solo, keep, vm(near), behind, vm(sum0)],
        in_specs=[SM] + [VM] * 4,
        share=1,
    )
    (first,) = call(
        first_residual_kernel,
        "first_residual",
        [frame16],
        [solo, keep, vm(prior0), far, vm(sum0)],
        in_specs=[SM] + [VM] * 4,
        share=1,
    )
    prior_first = from_behind(first, "tm")
    times = vm(time_kernel)
    time0, time1 = call(
        local_time_kernel,
        "local_time",
        [pltpu.VMEM((pixels, wide), f32)] * 2,
        [keep, small, vm(first), vm(second), times],
        share=0.4,
    )
    frames = 2 * tokens // pixels
    shape = (frames, 2 * H, 2 * W * outs)
    up_scratch = [
        pltpu.VMEM((2 * pixels + 4 * H, 3 * channels), bf16),
        pltpu.VMEM((2, 2 * W * outs // 128, 2 * H, 128), f32),
    ]
    folded, prior_second = vm(folded), vm(prior_second)
    time0, time1 = vm(time0), vm(time1)
    half_shape = (frames // 2,) + shape[1:]
    (early,) = call(
        early_up_kernel,
        "early_up",
        [jax.ShapeDtypeStruct(shape, bf16)],
        [solo, small, time0, time1, folded],
        [pltpu.VMEM(shape, bf16)] + up_scratch + [sem((4,))],
        share=2,
        in_specs=[SM] + [VM] * 4,
        out_specs=[HB],
    )
    (later,) = call(
        second_up_kernel,
        "second_up",
        [pltpu.VMEM(half_shape, bf16)],
        [solo, keep, small, prior_second, times, time1, folded],
        up_scratch,
        share=6,
        in_specs=[SM] + [VM] * 6,
    )
    (made,) = call(
        first_up_kernel,
        "first_up",
        [jax.ShapeDtypeStruct(shape, bf16)],
        [
            solo, keep, small, vm(prior_first), prior_second, times, time0, folded, vm(later),
            early,
        ],
        [pltpu.VMEM(half_shape, bf16)] + up_scratch + [sem((3,))],
        share=6,
        in_specs=[SM] + [VM] * 8 + [pl.BlockSpec(memory_space=pl.ANY)],
        out_specs=[HB],
        input_output_aliases={9: 0},
    )
    return made


def solution(mesh):
    placed = (
        P(("groups", "tm"), None),
        P(("groups", "tm")),
        P("groups"),
        P(),
        P(),
        P(),
        P(),
        P(),
        P(),
        P(),
        P(),
    )
    return jax.shard_map(
        on_device,
        mesh=mesh,
        in_specs=placed,
        out_specs=P(("groups", "tm"), None, None),
        check_vma=False,
    )
```

```python
import functools

import jax
import jax.numpy as jnp
from jax import lax
from jax.experimental import pallas as pl
from jax.experimental.pallas import tpu as pltpu
from jax.sharding import PartitionSpec as P

H = 16
W = 16
MARK = 128.0
epsilon = 1e-06
MIB = 1 << 20
f32 = jnp.float32
bf16 = jnp.bfloat16


def in_vmem(value):
    return pltpu.with_memory_space_constraint(value, pltpu.VMEM)


def in_hbm(value):
    return pltpu.with_memory_space_constraint(value, pltpu.HBM)


VM = pl.BlockSpec(memory_space=pltpu.VMEM)
HB = pl.BlockSpec(memory_space=pltpu.HBM)
SM = pl.BlockSpec(memory_space=pltpu.SMEM)


def iota(shape, dim):
    return lax.broadcasted_iota(jnp.int32, shape, dim)


def mm(lhs, rhs):
    return jnp.dot(lhs, rhs, preferred_element_type=f32)


def convolve(near, taps):
    return lax.dot_general(taps, near, (((0,), (1,)), ((), ())), preferred_element_type=f32).T


def from_behind(value, axis):
    size = lax.axis_size(axis)
    return lax.ppermute(value, axis, [(i, (i + 1) % size) for i in range(size)])


def pack_kernel(
    owner_hbm, latent_hbm, out_hbm, owner_ref, wide_ref, made_ref, arrived, left, *, peers, capacity
):
    tokens, channels = latent_hbm.shape
    copies = [
        pltpu.make_async_copy(owner_hbm, owner_ref, arrived.at[0]),
        pltpu.make_async_copy(latent_hbm, wide_ref.at[:, :channels], arrived.at[1]),
    ]
    for copy in copies:
        copy.start()
    wide_ref[:, channels:] = jnp.ones((tokens, 128), bf16)
    upper = (iota((tokens, tokens), 0) <= iota((tokens, tokens), 1)).astype(bf16)
    copies[0].wait()
    owner = owner_ref[...]
    marked = iota((peers, tokens), 0) == owner
    running = mm(marked.astype(bf16), upper)
    rank = jnp.sum(jnp.where(marked, running - 1.0, 0.0), 0, keepdims=True)
    slot = owner * capacity + rank.astype(jnp.int32)
    copies[1].wait()
    pieces = left.shape[0]
    rows = peers * capacity // pieces
    sent = []
    for piece in range(pieces):
        at = pl.ds(piece * rows, rows)
        chosen = (iota((rows, tokens), 0) + piece * rows == slot).astype(bf16)
        found = mm(chosen, wide_ref[...])
        empty = (1.0 - found[:, channels:]) * MARK
        made_ref[at] = (
            found[:, :channels] + jnp.concatenate([empty] * (channels // 128), 1)
        ).astype(bf16)
        copy = pltpu.make_async_copy(made_ref.at[at], out_hbm.at[at], left.at[piece])
        copy.start()
        sent.append(copy)
    for copy in sent:
        copy.wait()


def places(got_ref, peers, capacity):
    slots = got_ref.shape[0]
    present = (got_ref[:, :128] < MARK / 2).astype(bf16)
    sender = iota((peers, slots), 1) // capacity
    member = (sender == iota((peers, slots), 0)).astype(f32)
    below = (sender < iota((peers, slots), 0)).astype(f32)
    tallies = mm(jnp.concatenate([member, below], 0).astype(bf16), present)
    held = jnp.sum(member * tallies[:peers, :1], 0, keepdims=True).astype(jnp.int32)
    first = jnp.sum(member * tallies[peers:, :1], 0, keepdims=True).astype(jnp.int32)
    within = iota((1, slots), 1) % capacity
    return jnp.where(within < held, first + within, -1)


def unpack(place, got_ref, small_ref, decoded_ref, active_ref, frame):
    slots, channels = got_ref.shape
    pixels = decoded_ref.shape[0]
    pixel = iota((pixels, slots), 0)
    source = frame * pixels + (pixel % H) * W + pixel // H
    chosen = (source == place).astype(bf16)
    values = mm(chosen, got_ref[...])
    decoded_ref[...] = values.astype(bf16)
    squares = jnp.mean(values * values, -1, keepdims=True)
    scaled = values * lax.rsqrt(squares + epsilon)
    fed = scaled * small_ref[0:1, :channels] + small_ref[1:2, :channels]
    active_ref[...] = (fed * jax.nn.sigmoid(fed)).astype(bf16)


def unpack_second_kernel(
    got_ref, small_ref, decoded_ref, active_ref, place_ref, *, peers, capacity
):
    place = places(got_ref, peers, capacity)
    place_ref[...] = place
    unpack(place, got_ref, small_ref, decoded_ref, active_ref, 1)


def unpack_first_kernel(got_ref, small_ref, place_ref, decoded_ref, active_ref):
    unpack(place_ref[...], got_ref, small_ref, decoded_ref, active_ref, 0)


def vertical(frame):
    wide = frame.astype(f32)
    y = iota(wide.shape, 0) % H
    up = jnp.where(y == 0, 0.0, pltpu.roll(wide, 1, 0))
    down = jnp.where(y == H - 1, 0.0, pltpu.roll(wide, wide.shape[0] - 1, 0))
    return up.astype(bf16), frame, down.astype(bf16)


def steps(frame):
    wide = frame.astype(f32)
    up, here, down = vertical(frame)
    return (up.astype(f32) - wide).astype(bf16), here, (down.astype(f32) - wide).astype(bf16)


def patches(frame):
    pixels, channels = frame.shape
    nothing = jnp.zeros((H, channels), bf16)
    parts = []
    for shifted in vertical(frame):
        parts.append(jnp.concatenate([nothing, shifted[: pixels - H]], 0))
        parts.append(shifted)
        parts.append(jnp.concatenate([shifted[H:], nothing], 0))
    return jnp.concatenate(parts, 1)


def kept(keep_ref):
    return [[keep_ref[3 * f + back : 3 * f + back + 1, :1] for back in range(3)] for f in range(2)]


def local_conv_kernel(
    keep_ref, small_ref, first_ref, second_ref, decoded0_ref, decoded1_ref, here_ref, behind_ref,
    sum0_ref, sum1_ref,
):
    keep = kept(keep_ref)
    channels = sum0_ref.shape[1]
    sum1 = convolve(patches(second_ref[...]), here_ref[...])
    both = mm(
        patches(first_ref[...]), jnp.concatenate([here_ref[...], behind_ref[...]], 1)
    )
    bias = small_ref[2:3, :channels]
    sum0_ref[...] = both[:, :channels] + decoded0_ref[...].astype(f32) + bias
    base = decoded1_ref[...].astype(f32) + bias
    sum1_ref[...] = sum1 + base + keep[1][1] * both[:, channels:]


def second_residual_kernel(
    solo_ref, keep_ref, prior_ref, far_ref, sum_ref, out_ref, near_ref
):
    @pl.when(solo_ref[0] == 1)
    def _():
        out_ref[...] = sum_ref[...].astype(bf16)

    @pl.when(solo_ref[0] == 0)
    def _():
        near = patches(prior_ref[...])
        near_ref[...] = near
        far = kept(keep_ref)[1][2] * convolve(near, far_ref[...])
        out_ref[...] = (sum_ref[...] + far).astype(bf16)


def behind_kernel(solo_ref, keep_ref, near_ref, behind_ref, sum_ref, out_ref):
    @pl.when(solo_ref[0] == 1)
    def _():
        out_ref[...] = sum_ref[...]

    @pl.when(solo_ref[0] == 0)
    def _():
        behind = convolve(near_ref[...], behind_ref[...])
        out_ref[...] = sum_ref[...] + kept(keep_ref)[0][1] * behind


def first_residual_kernel(solo_ref, keep_ref, prior_ref, far_ref, sum_ref, out_ref):

    @pl.when(solo_ref[0] == 1)
    def _():
        out_ref[...] = sum_ref[...].astype(bf16)

    @pl.when(solo_ref[0] == 0)
    def _():
        far = kept(keep_ref)[0][2] * convolve(patches(prior_ref[...]), far_ref[...])
        out_ref[...] = (sum_ref[...] + far).astype(bf16)


def local_time_kernel(
    keep_ref, small_ref, first_ref, second_ref, time_ref, sum0_ref, sum1_ref
):
    keep = kept(keep_ref)
    bias = small_ref[3:4, : sum0_ref.shape[1]]
    sum0_ref[...] = mm(first_ref[...], time_ref[2]) + bias
    sum1_ref[...] = (
        mm(second_ref[...], time_ref[2]) + bias + keep[1][1] * mm(first_ref[...], time_ref[1])
    )


def upscale(temporal, frame, small_ref, folded_ref, made_ref, near, rows32, ready=()):
    pixels = H * W
    channels = near.shape[1] // 3
    outs = folded_ref.shape[3]
    both = temporal.astype(bf16)
    nothing = jnp.zeros((H, 3 * channels), bf16)
    bias = small_ref[4:5, :outs]
    blocks = 2 * outs // 128
    stride = pixels + 2 * H
    for half in range(2):
        base = H + half * stride
        near[base - H : base] = nothing
        near[base + pixels : base + pixels + H] = nothing
        shown = both[:, half * channels : (half + 1) * channels]
        for t, part in enumerate(steps(shown)):
            near[base : base + pixels, t * channels : (t + 1) * channels] = part
    for half in range(2):
        products = []
        for q in range(2):
            for t in range(3):
                windows = [
                    near[
                        half * stride + (q + side) * H : half * stride + (q + side) * H + pixels,
                        t * channels : (t + 1) * channels,
                    ]
                    for side in range(2)
                ]
                products.append(mm(jnp.concatenate(windows, 1), folded_ref[q, t]))
        for p in range(2):
            pair = jnp.concatenate(
                [products[3 * q + 1] + bias + products[3 * q + 2 * p] for q in range(2)], 1
            )
            for x in range(W):
                for block in range(blocks):
                    rows32[half, x * blocks + block, pl.ds(p, H, stride=2)] = pair[
                        x * H : (x + 1) * H, block * 128 : (block + 1) * 128
                    ]
        for block in range(W * blocks):
            made_ref[2 * frame + half, :, block * 128 : (block + 1) * 128] = rows32[
                half, block
            ].astype(bf16)
        for copy in ready[half : half + 1]:
            copy.start()


def early_up_kernel(
    solo_ref, small_ref, sum0_ref, sum1_ref, folded_ref, out_hbm, made_ref, near, rows32, left
):
    @pl.when(solo_ref[0] == 1)
    def _():
        copies = [
            pltpu.make_async_copy(made_ref.at[e], out_hbm.at[e], left.at[e]) for e in range(4)
        ]
        for f, sum_ref in ((1, sum1_ref), (0, sum0_ref)):
            ready = copies[2 * f : 2 * f + 2]
            upscale(sum_ref[...], f, small_ref, folded_ref, made_ref, near, rows32, ready)
        for copy in copies:
            copy.wait()


def second_up_kernel(
    solo_ref, keep_ref, small_ref, prior_ref, time_ref, sum_ref, folded_ref, made_ref, near, rows32
):
    @pl.when(solo_ref[0] == 0)
    def _():
        temporal = sum_ref[...] + kept(keep_ref)[1][2] * mm(prior_ref[...], time_ref[0])
        upscale(temporal, 0, small_ref, folded_ref, made_ref, near, rows32)


def first_up_kernel(
    solo_ref, keep_ref, small_ref, before_ref, prior_ref, time_ref, sum_ref, folded_ref,
    later_ref, early_hbm, out_hbm,
    made_ref, near, rows32, left,
):
    @pl.when(solo_ref[0] == 0)
    def _():
        later = pltpu.make_async_copy(later_ref, out_hbm.at[2:4], left.at[0])
        later.start()
        seen = [keep_ref[row : row + 1, :1].astype(bf16) for row in (2, 1)]
        pair = jnp.concatenate([before_ref[...] * seen[0], prior_ref[...] * seen[1]], 1)
        both = time_ref[:2].reshape(pair.shape[1], time_ref.shape[2])
        temporal = sum_ref[...] + mm(pair, both)
        copies = [
            pltpu.make_async_copy(made_ref.at[e], out_hbm.at[e], left.at[1 + e]) for e in range(2)
        ]
        upscale(temporal, 0, small_ref, folded_ref, made_ref, near, rows32, copies)
        for copy in copies:
            copy.wait()
        later.wait()


def keeps(counts_ref, position_ref):
    first = position_ref[0] * 2
    starts = [jnp.int32(0), jnp.int32(0)]
    end = jnp.int32(0)
    for video in range(counts_ref.shape[0]):
        end = end + counts_ref[video]
        starts = [jnp.where(end <= first + f, end, starts[f]) for f in range(2)]
    return [
        [(first + f - back >= starts[f]).astype(f32) for back in range(3)] for f in range(2)
    ]


def halves(taps):
    return (taps[0], taps[1] + taps[2]), (taps[0] + taps[1], taps[2])


def prepare_kernel(
    counts_ref, position_ref, gain_ref, shift_ref, res_bias_ref, time_bias_ref, up_bias_ref,
    up_hbm, taps_hbm,
    folded_hbm, small_ref, keep_ref, here_ref, behind_hbm, far_hbm, solo_ref,
    up_ref, folded_ref, behind_ref, far_ref, arrived, left,
):
    copies = [
        pltpu.make_async_copy(up_hbm, up_ref, arrived.at[0]),
        pltpu.make_async_copy(taps_hbm.at[2], here_ref, arrived.at[1]),
        pltpu.make_async_copy(taps_hbm.at[1], behind_ref, arrived.at[2]),
        pltpu.make_async_copy(taps_hbm.at[0], far_ref, arrived.at[3]),
    ]
    for copy in copies:
        copy.start()
    small_ref[...] = jnp.zeros_like(small_ref)
    for i, ref in enumerate((gain_ref, shift_ref, res_bias_ref, time_bias_ref, up_bias_ref)):
        small_ref[i : i + 1, : ref.shape[1]] = ref[...]
    keep = keeps(counts_ref, position_ref)
    solo_ref[0] = (keep[0][1] == 0.0).astype(jnp.int32)
    row = iota(keep_ref.shape, 0)
    seen = jnp.zeros(keep_ref.shape, f32)
    for f in range(2):
        for back in range(3):
            seen = jnp.where(row == 3 * f + back, keep[f][back], seen)
    keep_ref[...] = seen
    copies[0].wait()
    channels = up_ref.shape[3]
    rows = [[up_ref[a, b].astype(f32) for b in range(3)] for a in range(3)]
    rows[1] = [rows[0][b] + rows[1][b] + rows[2][b] for b in range(3)]
    for t in range(3):
        columns = halves(rows[t])
        for q in range(2):
            for side in range(2):
                folded_ref[q, t, side * channels : (side + 1) * channels] = columns[q][
                    side
                ].T.astype(bf16)
    for copy in copies[1:]:
        copy.wait()
    sent = [
        pltpu.make_async_copy(behind_ref, behind_hbm, left.at[0]),
        pltpu.make_async_copy(far_ref, far_hbm, left.at[1]),
        pltpu.make_async_copy(folded_ref, folded_hbm, left.at[2]),
    ]
    for copy in sent:
        copy.start()
    for copy in sent:
        copy.wait()


def on_device(
    latent,
    owner,
    frame_counts,
    norm_gain,
    norm_shift,
    res_kernel,
    res_bias,
    time_kernel,
    time_bias,
    up_kernel,
    up_bias,
):
    peers = lax.axis_size("tm")
    position = lax.axis_index("tm").astype(jnp.int32).reshape(1)
    tokens, channels = latent.shape
    capacity = 2 * tokens // peers
    pixels = H * W
    wide = time_kernel.shape[-1]
    outs = up_kernel.shape[-1]

    packed = pl.pallas_call(
        functools.partial(pack_kernel, peers=peers, capacity=capacity),
        out_shape=jax.ShapeDtypeStruct((peers * capacity, channels), bf16),
        in_specs=[HB, HB],
        out_specs=HB,
        scratch_shapes=[
            pltpu.VMEM((1, tokens), jnp.int32),
            pltpu.VMEM((tokens, channels + 128), bf16),
            pltpu.VMEM((peers * capacity, channels), bf16),
            pltpu.SemaphoreType.DMA((2,)),
            pltpu.SemaphoreType.DMA((4,)),
        ],
        compiler_params=pltpu.CompilerParams(vmem_limit_bytes=16 * MIB),
        name="pack",
    )(in_hbm(owner.reshape(1, tokens)), in_hbm(latent))
    packed, up_kernel = lax.optimization_barrier((packed, up_kernel))
    received = lax.all_to_all(packed, "tm", split_axis=0, concat_axis=0, tiled=True)
    res_kernel = res_kernel.reshape(3, 9 * channels, channels)
    one_tap = (9 * channels, channels)
    res_kernel = in_hbm(res_kernel)
    folded, small, keep, here, behind, far, solo = pl.pallas_call(
        prepare_kernel,
        out_shape=[
            pltpu.HBM((2, 3, 2 * channels, outs), bf16),
            pltpu.VMEM((8, wide), f32),
            pltpu.VMEM((8, 128), f32),
            pltpu.VMEM(one_tap, bf16),
            pltpu.HBM(one_tap, bf16),
            pltpu.HBM(one_tap, bf16),
            pltpu.SMEM((1,), jnp.int32),
        ],
        in_specs=[SM] * 2 + [VM] * 5 + [HB] * 2,
        out_specs=[HB] + [VM] * 3 + [HB] * 2 + [SM],
        scratch_shapes=[
            pltpu.VMEM((3, 3, outs, channels), bf16),
            pltpu.VMEM((2, 3, 2 * channels, outs), bf16),
            pltpu.VMEM(one_tap, bf16),
            pltpu.VMEM(one_tap, bf16),
            pltpu.SemaphoreType.DMA((4,)),
            pltpu.SemaphoreType.DMA((3,)),
        ],
        compiler_params=pltpu.CompilerParams(vmem_limit_bytes=20 * MIB),
        cost_estimate=pl.CostEstimate(
            flops=0, bytes_accessed=2 * res_kernel.size * 2, transcendentals=0
        ),
        name="prepare",
    )(
        frame_counts,
        position,
        norm_gain.reshape(1, channels),
        norm_shift.reshape(1, channels),
        res_bias.reshape(1, channels),
        time_bias.reshape(1, wide),
        up_bias.reshape(1, outs),
        in_hbm(jnp.swapaxes(up_kernel, 2, 3)),
        res_kernel,
    )

    def call(body, name, outputs, arguments, scratch=(), share=1.0, **more):
        out_specs = more.pop("out_specs", [VM] * len(outputs))
        in_specs = more.pop("in_specs", [VM] * len(arguments))
        return pl.pallas_call(
            body,
            out_shape=outputs,
            in_specs=in_specs,
            out_specs=out_specs,
            scratch_shapes=scratch,
            compiler_params=pltpu.CompilerParams(vmem_limit_bytes=12 * MIB),
            cost_estimate=pl.CostEstimate(
                flops=int(share * tap), bytes_accessed=0, transcendentals=0
            ),
            name=name,
            **more,
        )(*arguments)

    vm = in_vmem
    frame16 = pltpu.VMEM((pixels, channels), bf16)
    frame32 = pltpu.VMEM((pixels, channels), f32)
    near_shape = pltpu.VMEM((pixels, 9 * channels), bf16)
    tap = 2 * pixels * 9 * channels * channels
    sem = pltpu.SemaphoreType.DMA
    small, keep, received = vm(small), vm(keep), vm(received)
    decoded1, active1, place = call(
        functools.partial(unpack_second_kernel, peers=peers, capacity=capacity),
        "unpack_second",
        [frame16] * 2 + [pltpu.VMEM((1, peers * capacity), jnp.int32)],
        [received, small],
        share=3,
    )
    prior1 = from_behind(active1, "tm")
    decoded0, active0 = call(
        unpack_first_kernel, "unpack_first", [frame16] * 2, [received, small, vm(place)], share=0
    )
    prior0 = from_behind(active0, "tm")
    behind, far = vm(behind), vm(far)
    sum0, sum1 = call(
        local_conv_kernel,
        "local_conv",
        [frame32] * 2,
        [
            keep, small, vm(active0), vm(active1), vm(decoded0), vm(decoded1), vm(here), behind,
        ],
        share=3,
    )
    second, near = call(
        second_residual_kernel,
        "second_residual",
        [frame16, near_shape],
        [solo, keep, vm(prior1), far, vm(sum1)],
        in_specs=[SM] + [VM] * 4,
        share=1,
    )
    prior_second = from_behind(second, "tm")
    (sum0,) = call(
        behind_kernel,
        "behind",
        [frame32],
        [solo, keep, vm(near), behind, vm(sum0)],
        in_specs=[SM] + [VM] * 4,
        share=1,
    )
    (first,) = call(
        first_residual_kernel,
        "first_residual",
        [frame16],
        [solo, keep, vm(prior0), far, vm(sum0)],
        in_specs=[SM] + [VM] * 4,
        share=1,
    )
    prior_first = from_behind(first, "tm")
    times = vm(time_kernel)
    time0, time1 = call(
        local_time_kernel,
        "local_time",
        [pltpu.VMEM((pixels, wide), f32)] * 2,
        [keep, small, vm(first), vm(second), times],
        share=0.4,
    )
    frames = 2 * tokens // pixels
    shape = (frames, 2 * H, 2 * W * outs)
    up_scratch = [
        pltpu.VMEM((2 * pixels + 4 * H, 3 * channels), bf16),
        pltpu.VMEM((2, 2 * W * outs // 128, 2 * H, 128), f32),
    ]
    folded, prior_second = vm(folded), vm(prior_second)
    time0, time1 = vm(time0), vm(time1)
    half_shape = (frames // 2,) + shape[1:]
    (early,) = call(
        early_up_kernel,
        "early_up",
        [jax.ShapeDtypeStruct(shape, bf16)],
        [solo, small, time0, time1, folded],
        [pltpu.VMEM(shape, bf16)] + up_scratch + [sem((4,))],
        share=2,
        in_specs=[SM] + [VM] * 4,
        out_specs=[HB],
    )
    (later,) = call(
        second_up_kernel,
        "second_up",
        [pltpu.VMEM(half_shape, bf16)],
        [solo, keep, small, prior_second, times, time1, folded],
        up_scratch,
        share=6,
        in_specs=[SM] + [VM] * 6,
    )
    (made,) = call(
        first_up_kernel,
        "first_up",
        [jax.ShapeDtypeStruct(shape, bf16)],
        [
            solo, keep, small, vm(prior_first), prior_second, times, time0, folded, vm(later),
            early,
        ],
        [pltpu.VMEM(half_shape, bf16)] + up_scratch + [sem((3,))],
        share=6,
        in_specs=[SM] + [VM] * 8 + [pl.BlockSpec(memory_space=pl.ANY)],
        out_specs=[HB],
        input_output_aliases={9: 0},
    )
    return made


def solution(mesh):
    placed = (
        P(("groups", "tm"), None),
        P(("groups", "tm")),
        P("groups"),
        P(),
        P(),
        P(),
        P(),
        P(),
        P(),
        P(),
        P(),
    )
    return jax.shard_map(
        on_device,
        mesh=mesh,
        in_specs=placed,
        out_specs=P(("groups", "tm"), None, None),
        check_vma=False,
    )
```

```python
import functools

import jax
import jax.numpy as jnp
from jax import lax
from jax.experimental import pallas as pl
from jax.experimental.pallas import tpu as pltpu
from jax.sharding import PartitionSpec as P

H = 16
W = 16
MARK = 128.0
epsilon = 1e-06
MIB = 1 << 20
f32 = jnp.float32
bf16 = jnp.bfloat16


def in_vmem(value):
    return pltpu.with_memory_space_constraint(value, pltpu.VMEM)


def in_hbm(value):
    return pltpu.with_memory_space_constraint(value, pltpu.HBM)


VM = pl.BlockSpec(memory_space=pltpu.VMEM)
HB = pl.BlockSpec(memory_space=pltpu.HBM)
SM = pl.BlockSpec(memory_space=pltpu.SMEM)


def iota(shape, dim):
    return lax.broadcasted_iota(jnp.int32, shape, dim)


def mm(lhs, rhs):
    return jnp.dot(lhs, rhs, preferred_element_type=f32)


def convolve(near, taps):
    return lax.dot_general(taps, near, (((0,), (1,)), ((), ())), preferred_element_type=f32).T


def from_behind(value, axis):
    size = lax.axis_size(axis)
    return lax.ppermute(value, axis, [(i, (i + 1) % size) for i in range(size)])


def pack_kernel(
    owner_hbm, latent_hbm, out_hbm, owner_ref, wide_ref, made_ref, arrived, left, *, peers, capacity
):
    tokens, channels = latent_hbm.shape
    copies = [
        pltpu.make_async_copy(owner_hbm, owner_ref, arrived.at[0]),
        pltpu.make_async_copy(latent_hbm, wide_ref.at[:, :channels], arrived.at[1]),
    ]
    for copy in copies:
        copy.start()
    wide_ref[:, channels:] = jnp.ones((tokens, 128), bf16)
    upper = (iota((tokens, tokens), 0) <= iota((tokens, tokens), 1)).astype(bf16)
    copies[0].wait()
    owner = owner_ref[...]
    marked = iota((peers, tokens), 0) == owner
    running = mm(marked.astype(bf16), upper)
    rank = jnp.sum(jnp.where(marked, running - 1.0, 0.0), 0, keepdims=True)
    slot = owner * capacity + rank.astype(jnp.int32)
    copies[1].wait()
    pieces = left.shape[0]
    rows = peers * capacity // pieces
    sent = []
    for piece in range(pieces):
        at = pl.ds(piece * rows, rows)
        chosen = (iota((rows, tokens), 0) + piece * rows == slot).astype(bf16)
        found = mm(chosen, wide_ref[...])
        empty = (1.0 - found[:, channels:]) * MARK
        made_ref[at] = (
            found[:, :channels] + jnp.concatenate([empty] * (channels // 128), 1)
        ).astype(bf16)
        copy = pltpu.make_async_copy(made_ref.at[at], out_hbm.at[at], left.at[piece])
        copy.start()
        sent.append(copy)
    for copy in sent:
        copy.wait()


def places(got_ref, peers, capacity):
    slots = got_ref.shape[0]
    present = (got_ref[:, :128] < MARK / 2).astype(bf16)
    sender = iota((peers, slots), 1) // capacity
    member = (sender == iota((peers, slots), 0)).astype(f32)
    below = (sender < iota((peers, slots), 0)).astype(f32)
    tallies = mm(jnp.concatenate([member, below], 0).astype(bf16), present)
    held = jnp.sum(member * tallies[:peers, :1], 0, keepdims=True).astype(jnp.int32)
    first = jnp.sum(member * tallies[peers:, :1], 0, keepdims=True).astype(jnp.int32)
    within = iota((1, slots), 1) % capacity
    return jnp.where(within < held, first + within, -1)


def unpack(place, got_ref, small_ref, decoded_ref, active_ref, frame):
    slots, channels = got_ref.shape
    pixels = decoded_ref.shape[0]
    pixel = iota((pixels, slots), 0)
    source = frame * pixels + (pixel % H) * W + pixel // H
    chosen = (source == place).astype(bf16)
    values = mm(chosen, got_ref[...])
    decoded_ref[...] = values.astype(bf16)
    squares = jnp.mean(values * values, -1, keepdims=True)
    scaled = values * lax.rsqrt(squares + epsilon)
    fed = scaled * small_ref[0:1, :channels] + small_ref[1:2, :channels]
    active_ref[...] = (fed * jax.nn.sigmoid(fed)).astype(bf16)


def unpack_second_kernel(
    got_ref, small_ref, decoded_ref, active_ref, place_ref, *, peers, capacity
):
    place = places(got_ref, peers, capacity)
    place_ref[...] = place
    unpack(place, got_ref, small_ref, decoded_ref, active_ref, 1)


def unpack_first_kernel(got_ref, small_ref, place_ref, decoded_ref, active_ref):
    unpack(place_ref[...], got_ref, small_ref, decoded_ref, active_ref, 0)


def vertical(frame):
    wide = frame.astype(f32)
    y = iota(wide.shape, 0) % H
    up = jnp.where(y == 0, 0.0, pltpu.roll(wide, 1, 0))
    down = jnp.where(y == H - 1, 0.0, pltpu.roll(wide, wide.shape[0] - 1, 0))
    return up.astype(bf16), frame, down.astype(bf16)


def steps(frame):
    wide = frame.astype(f32)
    up, here, down = vertical(frame)
    return (up.astype(f32) - wide).astype(bf16), here, (down.astype(f32) - wide).astype(bf16)


def patches(frame):
    pixels, channels = frame.shape
    nothing = jnp.zeros((H, channels), bf16)
    parts = []
    for shifted in vertical(frame):
        parts.append(jnp.concatenate([nothing, shifted[: pixels - H]], 0))
        parts.append(shifted)
        parts.append(jnp.concatenate([shifted[H:], nothing], 0))
    return jnp.concatenate(parts, 1)


def kept(keep_ref):
    return [[keep_ref[3 * f + back : 3 * f + back + 1, :1] for back in range(3)] for f in range(2)]


def local_conv_kernel(
    keep_ref, small_ref, first_ref, second_ref, decoded0_ref, decoded1_ref, here_ref, behind_ref,
    sum0_ref, sum1_ref,
):
    keep = kept(keep_ref)
    channels = sum0_ref.shape[1]
    sum1 = convolve(patches(second_ref[...]), here_ref[...])
    both = mm(
        patches(first_ref[...]), jnp.concatenate([here_ref[...], behind_ref[...]], 1)
    )
    bias = small_ref[2:3, :channels]
    sum0_ref[...] = both[:, :channels] + decoded0_ref[...].astype(f32) + bias
    base = decoded1_ref[...].astype(f32) + bias
    sum1_ref[...] = sum1 + base + keep[1][1] * both[:, channels:]


def second_residual_kernel(solo_ref, keep_ref, prior_ref, far_ref, sum_ref, out_ref):
    @pl.when(solo_ref[0] == 1)
    def _():
        out_ref[...] = sum_ref[...].astype(bf16)

    @pl.when(solo_ref[0] == 0)
    def _():
        far = kept(keep_ref)[1][2] * convolve(patches(prior_ref[...]), far_ref[...])
        out_ref[...] = (sum_ref[...] + far).astype(bf16)


def behind_kernel(solo_ref, keep_ref, prior_ref, behind_ref, sum_ref, out_ref):
    @pl.when(solo_ref[0] == 1)
    def _():
        out_ref[...] = sum_ref[...]

    @pl.when(solo_ref[0] == 0)
    def _():
        behind = convolve(patches(prior_ref[...]), behind_ref[...])
        out_ref[...] = sum_ref[...] + kept(keep_ref)[0][1] * behind


def first_residual_kernel(solo_ref, keep_ref, prior_ref, far_ref, sum_ref, out_ref):

    @pl.when(solo_ref[0] == 1)
    def _():
        out_ref[...] = sum_ref[...].astype(bf16)

    @pl.when(solo_ref[0] == 0)
    def _():
        far = kept(keep_ref)[0][2] * convolve(patches(prior_ref[...]), far_ref[...])
        out_ref[...] = (sum_ref[...] + far).astype(bf16)


def local_time_kernel(
    keep_ref, small_ref, first_ref, second_ref, time_ref, sum0_ref, sum1_ref
):
    keep = kept(keep_ref)
    bias = small_ref[3:4, : sum0_ref.shape[1]]
    sum0_ref[...] = mm(first_ref[...], time_ref[2]) + bias
    sum1_ref[...] = (
        mm(second_ref[...], time_ref[2]) + bias + keep[1][1] * mm(first_ref[...], time_ref[1])
    )


def upscale(temporal, frame, small_ref, folded_ref, made_ref, near, rows32, ready=()):
    pixels = H * W
    channels = near.shape[1] // 3
    outs = folded_ref.shape[3]
    both = temporal.astype(bf16)
    nothing = jnp.zeros((H, 3 * channels), bf16)
    bias = small_ref[4:5, :outs]
    blocks = 2 * outs // 128
    stride = pixels + 2 * H
    for half in range(2):
        base = H + half * stride
        near[base - H : base] = nothing
        near[base + pixels : base + pixels + H] = nothing
        shown = both[:, half * channels : (half + 1) * channels]
        for t, part in enumerate(steps(shown)):
            near[base : base + pixels, t * channels : (t + 1) * channels] = part
    for half in range(2):
        products = []
        for q in range(2):
            for t in range(3):
                windows = [
                    near[
                        half * stride + (q + side) * H : half * stride + (q + side) * H + pixels,
                        t * channels : (t + 1) * channels,
                    ]
                    for side in range(2)
                ]
                products.append(mm(jnp.concatenate(windows, 1), folded_ref[q, t]))
        for p in range(2):
            pair = jnp.concatenate(
                [products[3 * q + 1] + bias + products[3 * q + 2 * p] for q in range(2)], 1
            )
            for x in range(W):
                for block in range(blocks):
                    rows32[half, x * blocks + block, pl.ds(p, H, stride=2)] = pair[
                        x * H : (x + 1) * H, block * 128 : (block + 1) * 128
                    ]
        for block in range(W * blocks):
            made_ref[2 * frame + half, :, block * 128 : (block + 1) * 128] = rows32[
                half, block
            ].astype(bf16)
        for copy in ready[half : half + 1]:
            copy.start()


def early_up_kernel(
    solo_ref, small_ref, sum0_ref, sum1_ref, folded_ref, out_hbm, made_ref, near, rows32, left
):
    @pl.when(solo_ref[0] == 1)
    def _():
        copies = [
            pltpu.make_async_copy(made_ref.at[e], out_hbm.at[e], left.at[e]) for e in range(4)
        ]
        for f, sum_ref in ((1, sum1_ref), (0, sum0_ref)):
            ready = copies[2 * f : 2 * f + 2]
            upscale(sum_ref[...], f, small_ref, folded_ref, made_ref, near, rows32, ready)
        for copy in copies:
            copy.wait()


def second_up_kernel(
    solo_ref, keep_ref, small_ref, prior_ref, time_ref, sum_ref, folded_ref, made_ref, near, rows32
):
    @pl.when(solo_ref[0] == 0)
    def _():
        temporal = sum_ref[...] + kept(keep_ref)[1][2] * mm(prior_ref[...], time_ref[0])
        upscale(temporal, 0, small_ref, folded_ref, made_ref, near, rows32)


def first_up_kernel(
    solo_ref, keep_ref, small_ref, before_ref, prior_ref, time_ref, sum_ref, folded_ref,
    later_ref, early_hbm, out_hbm,
    made_ref, near, rows32, left,
):
    @pl.when(solo_ref[0] == 0)
    def _():
        later = pltpu.make_async_copy(later_ref, out_hbm.at[2:4], left.at[0])
        later.start()
        seen = [keep_ref[row : row + 1, :1].astype(bf16) for row in (2, 1)]
        pair = jnp.concatenate([before_ref[...] * seen[0], prior_ref[...] * seen[1]], 1)
        both = time_ref[:2].reshape(pair.shape[1], time_ref.shape[2])
        temporal = sum_ref[...] + mm(pair, both)
        copies = [
            pltpu.make_async_copy(made_ref.at[e], out_hbm.at[e], left.at[1 + e]) for e in range(2)
        ]
        upscale(temporal, 0, small_ref, folded_ref, made_ref, near, rows32, copies)
        for copy in copies:
            copy.wait()
        later.wait()


def keeps(counts_ref, position_ref):
    first = position_ref[0] * 2
    starts = [jnp.int32(0), jnp.int32(0)]
    end = jnp.int32(0)
    for video in range(counts_ref.shape[0]):
        end = end + counts_ref[video]
        starts = [jnp.where(end <= first + f, end, starts[f]) for f in range(2)]
    return [
        [(first + f - back >= starts[f]).astype(f32) for back in range(3)] for f in range(2)
    ]


def halves(taps):
    return (taps[0], taps[1] + taps[2]), (taps[0] + taps[1], taps[2])


def prepare_kernel(
    counts_ref, position_ref, gain_ref, shift_ref, res_bias_ref, time_bias_ref, up_bias_ref,
    up_hbm, taps_hbm,
    folded_hbm, small_ref, keep_ref, here_ref, behind_hbm, far_hbm, solo_ref,
    up_ref, folded_ref, behind_ref, far_ref, arrived, left,
):
    copies = [
        pltpu.make_async_copy(up_hbm, up_ref, arrived.at[0]),
        pltpu.make_async_copy(taps_hbm.at[2], here_ref, arrived.at[1]),
        pltpu.make_async_copy(taps_hbm.at[1], behind_ref, arrived.at[2]),
        pltpu.make_async_copy(taps_hbm.at[0], far_ref, arrived.at[3]),
    ]
    for copy in copies:
        copy.start()
    small_ref[...] = jnp.zeros_like(small_ref)
    for i, ref in enumerate((gain_ref, shift_ref, res_bias_ref, time_bias_ref, up_bias_ref)):
        small_ref[i : i + 1, : ref.shape[1]] = ref[...]
    keep = keeps(counts_ref, position_ref)
    solo_ref[0] = (keep[0][1] == 0.0).astype(jnp.int32)
    row = iota(keep_ref.shape, 0)
    seen = jnp.zeros(keep_ref.shape, f32)
    for f in range(2):
        for back in range(3):
            seen = jnp.where(row == 3 * f + back, keep[f][back], seen)
    keep_ref[...] = seen
    copies[0].wait()
    channels = up_ref.shape[3]
    rows = [[up_ref[a, b].astype(f32) for b in range(3)] for a in range(3)]
    rows[1] = [rows[0][b] + rows[1][b] + rows[2][b] for b in range(3)]
    for t in range(3):
        columns = halves(rows[t])
        for q in range(2):
            for side in range(2):
                folded_ref[q, t, side * channels : (side + 1) * channels] = columns[q][
                    side
                ].T.astype(bf16)
    for copy in copies[1:]:
        copy.wait()
    sent = [
        pltpu.make_async_copy(behind_ref, behind_hbm, left.at[0]),
        pltpu.make_async_copy(far_ref, far_hbm, left.at[1]),
        pltpu.make_async_copy(folded_ref, folded_hbm, left.at[2]),
    ]
    for copy in sent:
        copy.start()
    for copy in sent:
        copy.wait()


def on_device(
    latent,
    owner,
    frame_counts,
    norm_gain,
    norm_shift,
    res_kernel,
    res_bias,
    time_kernel,
    time_bias,
    up_kernel,
    up_bias,
):
    peers = lax.axis_size("tm")
    position = lax.axis_index("tm").astype(jnp.int32).reshape(1)
    tokens, channels = latent.shape
    capacity = 2 * tokens // peers
    pixels = H * W
    wide = time_kernel.shape[-1]
    outs = up_kernel.shape[-1]

    packed = pl.pallas_call(
        functools.partial(pack_kernel, peers=peers, capacity=capacity),
        out_shape=jax.ShapeDtypeStruct((peers * capacity, channels), bf16),
        in_specs=[HB, HB],
        out_specs=HB,
        scratch_shapes=[
            pltpu.VMEM((1, tokens), jnp.int32),
            pltpu.VMEM((tokens, channels + 128), bf16),
            pltpu.VMEM((peers * capacity, channels), bf16),
            pltpu.SemaphoreType.DMA((2,)),
            pltpu.SemaphoreType.DMA((4,)),
        ],
        compiler_params=pltpu.CompilerParams(vmem_limit_bytes=16 * MIB),
        name="pack",
    )(in_hbm(owner.reshape(1, tokens)), in_hbm(latent))
    packed, up_kernel = lax.optimization_barrier((packed, up_kernel))
    received = lax.all_to_all(packed, "tm", split_axis=0, concat_axis=0, tiled=True)
    res_kernel = res_kernel.reshape(3, 9 * channels, channels)
    one_tap = (9 * channels, channels)
    res_kernel = in_hbm(res_kernel)
    folded, small, keep, here, behind, far, solo = pl.pallas_call(
        prepare_kernel,
        out_shape=[
            pltpu.HBM((2, 3, 2 * channels, outs), bf16),
            pltpu.VMEM((8, wide), f32),
            pltpu.VMEM((8, 128), f32),
            pltpu.VMEM(one_tap, bf16),
            pltpu.HBM(one_tap, bf16),
            pltpu.HBM(one_tap, bf16),
            pltpu.SMEM((1,), jnp.int32),
        ],
        in_specs=[SM] * 2 + [VM] * 5 + [HB] * 2,
        out_specs=[HB] + [VM] * 3 + [HB] * 2 + [SM],
        scratch_shapes=[
            pltpu.VMEM((3, 3, outs, channels), bf16),
            pltpu.VMEM((2, 3, 2 * channels, outs), bf16),
            pltpu.VMEM(one_tap, bf16),
            pltpu.VMEM(one_tap, bf16),
            pltpu.SemaphoreType.DMA((4,)),
            pltpu.SemaphoreType.DMA((3,)),
        ],
        compiler_params=pltpu.CompilerParams(vmem_limit_bytes=20 * MIB),
        cost_estimate=pl.CostEstimate(
            flops=0, bytes_accessed=2 * res_kernel.size * 2, transcendentals=0
        ),
        name="prepare",
    )(
        frame_counts,
        position,
        norm_gain.reshape(1, channels),
        norm_shift.reshape(1, channels),
        res_bias.reshape(1, channels),
        time_bias.reshape(1, wide),
        up_bias.reshape(1, outs),
        in_hbm(jnp.swapaxes(up_kernel, 2, 3)),
        res_kernel,
    )

    def call(body, name, outputs, arguments, scratch=(), share=1.0, **more):
        out_specs = more.pop("out_specs", [VM] * len(outputs))
        in_specs = more.pop("in_specs", [VM] * len(arguments))
        return pl.pallas_call(
            body,
            out_shape=outputs,
            in_specs=in_specs,
            out_specs=out_specs,
            scratch_shapes=scratch,
            compiler_params=pltpu.CompilerParams(vmem_limit_bytes=12 * MIB),
            cost_estimate=pl.CostEstimate(
                flops=int(share * tap), bytes_accessed=0, transcendentals=0
            ),
            name=name,
            **more,
        )(*arguments)

    vm = in_vmem
    frame16 = pltpu.VMEM((pixels, channels), bf16)
    frame32 = pltpu.VMEM((pixels, channels), f32)
    tap = 2 * pixels * 9 * channels * channels
    sem = pltpu.SemaphoreType.DMA
    small, keep, received = vm(small), vm(keep), vm(received)
    decoded1, active1, place = call(
        functools.partial(unpack_second_kernel, peers=peers, capacity=capacity),
        "unpack_second",
        [frame16] * 2 + [pltpu.VMEM((1, peers * capacity), jnp.int32)],
        [received, small],
        share=3,
    )
    prior1 = from_behind(active1, "tm")
    decoded0, active0 = call(
        unpack_first_kernel, "unpack_first", [frame16] * 2, [received, small, vm(place)], share=0
    )
    prior0 = from_behind(active0, "tm")
    behind, far = vm(behind), vm(far)
    sum0, sum1 = call(
        local_conv_kernel,
        "local_conv",
        [frame32] * 2,
        [
            keep, small, vm(active0), vm(active1), vm(decoded0), vm(decoded1), vm(here), behind,
        ],
        share=3,
    )
    prior1 = vm(prior1)
    (second,) = call(
        second_residual_kernel,
        "second_residual",
        [frame16],
        [solo, keep, prior1, far, vm(sum1)],
        in_specs=[SM] + [VM] * 4,
        share=1,
    )
    prior_second = from_behind(second, "tm")
    (sum0,) = call(
        behind_kernel,
        "behind",
        [frame32],
        [solo, keep, prior1, behind, vm(sum0)],
        in_specs=[SM] + [VM] * 4,
        share=1,
    )
    (first,) = call(
        first_residual_kernel,
        "first_residual",
        [frame16],
        [solo, keep, vm(prior0), far, vm(sum0)],
        in_specs=[SM] + [VM] * 4,
        share=1,
    )
    prior_first = from_behind(first, "tm")
    times = vm(time_kernel)
    time0, time1 = call(
        local_time_kernel,
        "local_time",
        [pltpu.VMEM((pixels, wide), f32)] * 2,
        [keep, small, vm(first), vm(second), times],
        share=0.4,
    )
    frames = 2 * tokens // pixels
    shape = (frames, 2 * H, 2 * W * outs)
    up_scratch = [
        pltpu.VMEM((2 * pixels + 4 * H, 3 * channels), bf16),
        pltpu.VMEM((2, 2 * W * outs // 128, 2 * H, 128), f32),
    ]
    folded, prior_second = vm(folded), vm(prior_second)
    time0, time1 = vm(time0), vm(time1)
    half_shape = (frames // 2,) + shape[1:]
    (early,) = call(
        early_up_kernel,
        "early_up",
        [jax.ShapeDtypeStruct(shape, bf16)],
        [solo, small, time0, time1, folded],
        [pltpu.VMEM(shape, bf16)] + up_scratch + [sem((4,))],
        share=2,
        in_specs=[SM] + [VM] * 4,
        out_specs=[HB],
    )
    (later,) = call(
        second_up_kernel,
        "second_up",
        [pltpu.VMEM(half_shape, bf16)],
        [solo, keep, small, prior_second, times, time1, folded],
        up_scratch,
        share=6,
        in_specs=[SM] + [VM] * 6,
    )
    (made,) = call(
        first_up_kernel,
        "first_up",
        [jax.ShapeDtypeStruct(shape, bf16)],
        [
            solo, keep, small, vm(prior_first), prior_second, times, time0, folded, vm(later),
            early,
        ],
        [pltpu.VMEM(half_shape, bf16)] + up_scratch + [sem((3,))],
        share=6,
        in_specs=[SM] + [VM] * 8 + [pl.BlockSpec(memory_space=pl.ANY)],
        out_specs=[HB],
        input_output_aliases={9: 0},
    )
    return made


def solution(mesh):
    placed = (
        P(("groups", "tm"), None),
        P(("groups", "tm")),
        P("groups"),
        P(),
        P(),
        P(),
        P(),
        P(),
        P(),
        P(),
        P(),
    )
    return jax.shard_map(
        on_device,
        mesh=mesh,
        in_specs=placed,
        out_specs=P(("groups", "tm"), None, None),
        check_vma=False,
    )
```

```python
import functools

import jax
import jax.numpy as jnp
from jax import lax
from jax.experimental import pallas as pl
from jax.experimental.pallas import tpu as pltpu
from jax.sharding import PartitionSpec as P

H = 16
W = 16
MARK = 128.0
epsilon = 1e-06
MIB = 1 << 20
f32 = jnp.float32
bf16 = jnp.bfloat16


def in_vmem(value):
    return pltpu.with_memory_space_constraint(value, pltpu.VMEM)


def in_hbm(value):
    return pltpu.with_memory_space_constraint(value, pltpu.HBM)


VM = pl.BlockSpec(memory_space=pltpu.VMEM)
HB = pl.BlockSpec(memory_space=pltpu.HBM)
SM = pl.BlockSpec(memory_space=pltpu.SMEM)


def iota(shape, dim):
    return lax.broadcasted_iota(jnp.int32, shape, dim)


def mm(lhs, rhs):
    return jnp.dot(lhs, rhs, preferred_element_type=f32)


def convolve(near, taps):
    return lax.dot_general(taps, near, (((0,), (1,)), ((), ())), preferred_element_type=f32).T


def from_behind(value, axis):
    size = lax.axis_size(axis)
    return lax.ppermute(value, axis, [(i, (i + 1) % size) for i in range(size)])


def pack_kernel(
    owner_hbm, latent_hbm, out_hbm, owner_ref, wide_ref, made_ref, arrived, left, *, peers, capacity
):
    tokens, channels = latent_hbm.shape
    copies = [
        pltpu.make_async_copy(owner_hbm, owner_ref, arrived.at[0]),
        pltpu.make_async_copy(latent_hbm, wide_ref.at[:, :channels], arrived.at[1]),
    ]
    for copy in copies:
        copy.start()
    wide_ref[:, channels:] = jnp.ones((tokens, 128), bf16)
    upper = (iota((tokens, tokens), 0) <= iota((tokens, tokens), 1)).astype(bf16)
    copies[0].wait()
    owner = owner_ref[...]
    marked = iota((peers, tokens), 0) == owner
    running = mm(marked.astype(bf16), upper)
    rank = jnp.sum(jnp.where(marked, running - 1.0, 0.0), 0, keepdims=True)
    slot = owner * capacity + rank.astype(jnp.int32)
    copies[1].wait()
    pieces = left.shape[0]
    rows = peers * capacity // pieces
    sent = []
    for piece in range(pieces):
        at = pl.ds(piece * rows, rows)
        chosen = (iota((rows, tokens), 0) + piece * rows == slot).astype(bf16)
        found = mm(chosen, wide_ref[...])
        empty = (1.0 - found[:, channels:]) * MARK
        made_ref[at] = (
            found[:, :channels] + jnp.concatenate([empty] * (channels // 128), 1)
        ).astype(bf16)
        copy = pltpu.make_async_copy(made_ref.at[at], out_hbm.at[at], left.at[piece])
        copy.start()
        sent.append(copy)
    for copy in sent:
        copy.wait()


def places(got_ref, peers, capacity):
    slots = got_ref.shape[0]
    present = (got_ref[:, :128] < MARK / 2).astype(bf16)
    sender = iota((peers, slots), 1) // capacity
    member = (sender == iota((peers, slots), 0)).astype(f32)
    below = (sender < iota((peers, slots), 0)).astype(f32)
    tallies = mm(jnp.concatenate([member, below], 0).astype(bf16), present)
    held = jnp.sum(member * tallies[:peers, :1], 0, keepdims=True).astype(jnp.int32)
    first = jnp.sum(member * tallies[peers:, :1], 0, keepdims=True).astype(jnp.int32)
    within = iota((1, slots), 1) % capacity
    return jnp.where(within < held, first + within, -1)


def unpack(place, got_ref, small_ref, decoded_ref, active_ref, frame):
    slots, channels = got_ref.shape
    pixels = decoded_ref.shape[0]
    part = pixels // 2
    for rows in (slice(0, part), slice(part, pixels)):
        pixel = iota((part, slots), 0) + rows.start
        source = frame * pixels + (pixel % H) * W + pixel // H
        values = mm((source == place).astype(bf16), got_ref[...])
        decoded_ref[rows] = values.astype(bf16)
        squares = jnp.mean(values * values, -1, keepdims=True)
        scaled = values * lax.rsqrt(squares + epsilon)
        fed = scaled * small_ref[0:1, :channels] + small_ref[1:2, :channels]
        active_ref[rows] = (fed * jax.nn.sigmoid(fed)).astype(bf16)


def unpack_second_kernel(
    got_ref, small_ref, decoded_ref, active_ref, place_ref, *, peers, capacity
):
    place = places(got_ref, peers, capacity)
    place_ref[...] = place
    unpack(place, got_ref, small_ref, decoded_ref, active_ref, 1)


def unpack_first_kernel(got_ref, small_ref, place_ref, decoded_ref, active_ref):
    unpack(place_ref[...], got_ref, small_ref, decoded_ref, active_ref, 0)


def vertical(frame):
    wide = frame.astype(f32)
    y = iota(wide.shape, 0) % H
    up = jnp.where(y == 0, 0.0, pltpu.roll(wide, 1, 0))
    down = jnp.where(y == H - 1, 0.0, pltpu.roll(wide, wide.shape[0] - 1, 0))
    return up.astype(bf16), frame, down.astype(bf16)


def steps(frame):
    wide = frame.astype(f32)
    up, here, down = vertical(frame)
    return (up.astype(f32) - wide).astype(bf16), here, (down.astype(f32) - wide).astype(bf16)


def patches(frame):
    pixels, channels = frame.shape
    nothing = jnp.zeros((H, channels), bf16)
    parts = []
    for shifted in vertical(frame):
        parts.append(jnp.concatenate([nothing, shifted[: pixels - H]], 0))
        parts.append(shifted)
        parts.append(jnp.concatenate([shifted[H:], nothing], 0))
    return jnp.concatenate(parts, 1)


def kept(keep_ref):
    return [[keep_ref[3 * f + back : 3 * f + back + 1, :1] for back in range(3)] for f in range(2)]


def local_conv_kernel(
    keep_ref, small_ref, first_ref, second_ref, decoded0_ref, decoded1_ref, here_ref, behind_ref,
    sum0_ref, sum1_ref,
):
    keep = kept(keep_ref)
    channels = sum0_ref.shape[1]
    sum1 = convolve(patches(second_ref[...]), here_ref[...])
    both = mm(
        patches(first_ref[...]), jnp.concatenate([here_ref[...], behind_ref[...]], 1)
    )
    bias = small_ref[2:3, :channels]
    sum0_ref[...] = both[:, :channels] + decoded0_ref[...].astype(f32) + bias
    base = decoded1_ref[...].astype(f32) + bias
    sum1_ref[...] = sum1 + base + keep[1][1] * both[:, channels:]


def second_residual_kernel(solo_ref, keep_ref, prior_ref, far_ref, sum_ref, out_ref):
    @pl.when(solo_ref[0] == 1)
    def _():
        out_ref[...] = sum_ref[...].astype(bf16)

    @pl.when(solo_ref[0] == 0)
    def _():
        far = kept(keep_ref)[1][2] * convolve(patches(prior_ref[...]), far_ref[...])
        out_ref[...] = (sum_ref[...] + far).astype(bf16)


def behind_kernel(solo_ref, keep_ref, prior_ref, behind_ref, sum_ref, out_ref):
    @pl.when(solo_ref[0] == 1)
    def _():
        out_ref[...] = sum_ref[...]

    @pl.when(solo_ref[0] == 0)
    def _():
        behind = convolve(patches(prior_ref[...]), behind_ref[...])
        out_ref[...] = sum_ref[...] + kept(keep_ref)[0][1] * behind


def first_residual_kernel(solo_ref, keep_ref, prior_ref, far_ref, sum_ref, out_ref):

    @pl.when(solo_ref[0] == 1)
    def _():
        out_ref[...] = sum_ref[...].astype(bf16)

    @pl.when(solo_ref[0] == 0)
    def _():
        far = kept(keep_ref)[0][2] * convolve(patches(prior_ref[...]), far_ref[...])
        out_ref[...] = (sum_ref[...] + far).astype(bf16)


def local_time_kernel(
    keep_ref, small_ref, first_ref, second_ref, time_ref, sum0_ref, sum1_ref
):
    keep = kept(keep_ref)
    bias = small_ref[3:4, : sum0_ref.shape[1]]
    sum0_ref[...] = mm(first_ref[...], time_ref[2]) + bias
    sum1_ref[...] = (
        mm(second_ref[...], time_ref[2]) + bias + keep[1][1] * mm(first_ref[...], time_ref[1])
    )


def upscale(temporal, frame, small_ref, folded_ref, made_ref, near, rows32, ready=()):
    pixels = H * W
    channels = near.shape[1] // 3
    outs = folded_ref.shape[3]
    both = temporal.astype(bf16)
    nothing = jnp.zeros((H, 3 * channels), bf16)
    bias = small_ref[4:5, :outs]
    blocks = 2 * outs // 128
    stride = pixels + 2 * H
    for half in range(2):
        base = H + half * stride
        near[base - H : base] = nothing
        near[base + pixels : base + pixels + H] = nothing
        shown = both[:, half * channels : (half + 1) * channels]
        for t, part in enumerate(steps(shown)):
            near[base : base + pixels, t * channels : (t + 1) * channels] = part
    for half in range(2):
        products = []
        for q in range(2):
            for t in range(3):
                windows = [
                    near[
                        half * stride + (q + side) * H : half * stride + (q + side) * H + pixels,
                        t * channels : (t + 1) * channels,
                    ]
                    for side in range(2)
                ]
                products.append(mm(jnp.concatenate(windows, 1), folded_ref[q, t]))
        for p in range(2):
            pair = jnp.concatenate(
                [products[3 * q + 1] + bias + products[3 * q + 2 * p] for q in range(2)], 1
            )
            for x in range(W):
                for block in range(blocks):
                    rows32[half, x * blocks + block, pl.ds(p, H, stride=2)] = pair[
                        x * H : (x + 1) * H, block * 128 : (block + 1) * 128
                    ]
        for block in range(W * blocks):
            made_ref[2 * frame + half, :, block * 128 : (block + 1) * 128] = rows32[
                half, block
            ].astype(bf16)
        for copy in ready[half : half + 1]:
            copy.start()


def early_up_kernel(
    solo_ref, small_ref, sum0_ref, sum1_ref, folded_ref, out_hbm, made_ref, near, rows32, left
):
    @pl.when(solo_ref[0] == 1)
    def _():
        copies = [
            pltpu.make_async_copy(made_ref.at[e], out_hbm.at[e], left.at[e]) for e in range(4)
        ]
        for f, sum_ref in ((1, sum1_ref), (0, sum0_ref)):
            ready = copies[2 * f : 2 * f + 2]
            upscale(sum_ref[...], f, small_ref, folded_ref, made_ref, near, rows32, ready)
        for copy in copies:
            copy.wait()


def second_up_kernel(
    solo_ref, keep_ref, small_ref, prior_ref, time_ref, sum_ref, folded_ref, made_ref, near, rows32
):
    @pl.when(solo_ref[0] == 0)
    def _():
        temporal = sum_ref[...] + kept(keep_ref)[1][2] * mm(prior_ref[...], time_ref[0])
        upscale(temporal, 0, small_ref, folded_ref, made_ref, near, rows32)


def first_up_kernel(
    solo_ref, keep_ref, small_ref, before_ref, prior_ref, time_ref, sum_ref, folded_ref,
    later_ref, early_hbm, out_hbm,
    made_ref, near, rows32, left,
):
    @pl.when(solo_ref[0] == 0)
    def _():
        later = pltpu.make_async_copy(later_ref, out_hbm.at[2:4], left.at[0])
        later.start()
        seen = [keep_ref[row : row + 1, :1].astype(bf16) for row in (2, 1)]
        pair = jnp.concatenate([before_ref[...] * seen[0], prior_ref[...] * seen[1]], 1)
        both = time_ref[:2].reshape(pair.shape[1], time_ref.shape[2])
        temporal = sum_ref[...] + mm(pair, both)
        copies = [
            pltpu.make_async_copy(made_ref.at[e], out_hbm.at[e], left.at[1 + e]) for e in range(2)
        ]
        upscale(temporal, 0, small_ref, folded_ref, made_ref, near, rows32, copies)
        for copy in copies:
            copy.wait()
        later.wait()


def keeps(counts_ref, position_ref):
    first = position_ref[0] * 2
    starts = [jnp.int32(0), jnp.int32(0)]
    end = jnp.int32(0)
    for video in range(counts_ref.shape[0]):
        end = end + counts_ref[video]
        starts = [jnp.where(end <= first + f, end, starts[f]) for f in range(2)]
    return [
        [(first + f - back >= starts[f]).astype(f32) for back in range(3)] for f in range(2)
    ]


def halves(taps):
    return (taps[0], taps[1] + taps[2]), (taps[0] + taps[1], taps[2])


def prepare_kernel(
    counts_ref, position_ref, gain_ref, shift_ref, res_bias_ref, time_bias_ref, up_bias_ref,
    up_hbm, taps_hbm,
    folded_hbm, small_ref, keep_ref, here_ref, behind_hbm, far_hbm, solo_ref,
    up_ref, folded_ref, behind_ref, far_ref, arrived, left,
):
    copies = [
        pltpu.make_async_copy(up_hbm, up_ref, arrived.at[0]),
        pltpu.make_async_copy(taps_hbm.at[2], here_ref, arrived.at[1]),
        pltpu.make_async_copy(taps_hbm.at[1], behind_ref, arrived.at[2]),
        pltpu.make_async_copy(taps_hbm.at[0], far_ref, arrived.at[3]),
    ]
    for copy in copies:
        copy.start()
    small_ref[...] = jnp.zeros_like(small_ref)
    for i, ref in enumerate((gain_ref, shift_ref, res_bias_ref, time_bias_ref, up_bias_ref)):
        small_ref[i : i + 1, : ref.shape[1]] = ref[...]
    keep = keeps(counts_ref, position_ref)
    solo_ref[0] = (keep[0][1] == 0.0).astype(jnp.int32)
    row = iota(keep_ref.shape, 0)
    seen = jnp.zeros(keep_ref.shape, f32)
    for f in range(2):
        for back in range(3):
            seen = jnp.where(row == 3 * f + back, keep[f][back], seen)
    keep_ref[...] = seen
    copies[0].wait()
    channels = up_ref.shape[3]
    rows = [[up_ref[a, b].astype(f32) for b in range(3)] for a in range(3)]
    rows[1] = [rows[0][b] + rows[1][b] + rows[2][b] for b in range(3)]
    for t in range(3):
        columns = halves(rows[t])
        for q in range(2):
            for side in range(2):
                folded_ref[q, t, side * channels : (side + 1) * channels] = columns[q][
                    side
                ].T.astype(bf16)
    for copy in copies[1:]:
        copy.wait()
    sent = [
        pltpu.make_async_copy(behind_ref, behind_hbm, left.at[0]),
        pltpu.make_async_copy(far_ref, far_hbm, left.at[1]),
        pltpu.make_async_copy(folded_ref, folded_hbm, left.at[2]),
    ]
    for copy in sent:
        copy.start()
    for copy in sent:
        copy.wait()


def on_device(
    latent,
    owner,
    frame_counts,
    norm_gain,
    norm_shift,
    res_kernel,
    res_bias,
    time_kernel,
    time_bias,
    up_kernel,
    up_bias,
):
    peers = lax.axis_size("tm")
    position = lax.axis_index("tm").astype(jnp.int32).reshape(1)
    tokens, channels = latent.shape
    capacity = 2 * tokens // peers
    pixels = H * W
    wide = time_kernel.shape[-1]
    outs = up_kernel.shape[-1]

    packed = pl.pallas_call(
        functools.partial(pack_kernel, peers=peers, capacity=capacity),
        out_shape=jax.ShapeDtypeStruct((peers * capacity, channels), bf16),
        in_specs=[HB, HB],
        out_specs=HB,
        scratch_shapes=[
            pltpu.VMEM((1, tokens), jnp.int32),
            pltpu.VMEM((tokens, channels + 128), bf16),
            pltpu.VMEM((peers * capacity, channels), bf16),
            pltpu.SemaphoreType.DMA((2,)),
            pltpu.SemaphoreType.DMA((4,)),
        ],
        compiler_params=pltpu.CompilerParams(vmem_limit_bytes=16 * MIB),
        name="pack",
    )(in_hbm(owner.reshape(1, tokens)), in_hbm(latent))
    packed, up_kernel = lax.optimization_barrier((packed, up_kernel))
    received = lax.all_to_all(packed, "tm", split_axis=0, concat_axis=0, tiled=True)
    res_kernel = res_kernel.reshape(3, 9 * channels, channels)
    one_tap = (9 * channels, channels)
    res_kernel = in_hbm(res_kernel)
    folded, small, keep, here, behind, far, solo = pl.pallas_call(
        prepare_kernel,
        out_shape=[
            pltpu.HBM((2, 3, 2 * channels, outs), bf16),
            pltpu.VMEM((8, wide), f32),
            pltpu.VMEM((8, 128), f32),
            pltpu.VMEM(one_tap, bf16),
            pltpu.HBM(one_tap, bf16),
            pltpu.HBM(one_tap, bf16),
            pltpu.SMEM((1,), jnp.int32),
        ],
        in_specs=[SM] * 2 + [VM] * 5 + [HB] * 2,
        out_specs=[HB] + [VM] * 3 + [HB] * 2 + [SM],
        scratch_shapes=[
            pltpu.VMEM((3, 3, outs, channels), bf16),
            pltpu.VMEM((2, 3, 2 * channels, outs), bf16),
            pltpu.VMEM(one_tap, bf16),
            pltpu.VMEM(one_tap, bf16),
            pltpu.SemaphoreType.DMA((4,)),
            pltpu.SemaphoreType.DMA((3,)),
        ],
        compiler_params=pltpu.CompilerParams(vmem_limit_bytes=20 * MIB),
        cost_estimate=pl.CostEstimate(
            flops=0, bytes_accessed=2 * res_kernel.size * 2, transcendentals=0
        ),
        name="prepare",
    )(
        frame_counts,
        position,
        norm_gain.reshape(1, channels),
        norm_shift.reshape(1, channels),
        res_bias.reshape(1, channels),
        time_bias.reshape(1, wide),
        up_bias.reshape(1, outs),
        in_hbm(jnp.swapaxes(up_kernel, 2, 3)),
        res_kernel,
    )

    def call(body, name, outputs, arguments, scratch=(), share=1.0, **more):
        out_specs = more.pop("out_specs", [VM] * len(outputs))
        in_specs = more.pop("in_specs", [VM] * len(arguments))
        return pl.pallas_call(
            body,
            out_shape=outputs,
            in_specs=in_specs,
            out_specs=out_specs,
            scratch_shapes=scratch,
            compiler_params=pltpu.CompilerParams(vmem_limit_bytes=12 * MIB),
            cost_estimate=pl.CostEstimate(
                flops=int(share * tap), bytes_accessed=0, transcendentals=0
            ),
            name=name,
            **more,
        )(*arguments)

    vm = in_vmem
    frame16 = pltpu.VMEM((pixels, channels), bf16)
    frame32 = pltpu.VMEM((pixels, channels), f32)
    tap = 2 * pixels * 9 * channels * channels
    sem = pltpu.SemaphoreType.DMA
    small, keep, received = vm(small), vm(keep), vm(received)
    decoded1, active1, place = call(
        functools.partial(unpack_second_kernel, peers=peers, capacity=capacity),
        "unpack_second",
        [frame16] * 2 + [pltpu.VMEM((1, peers * capacity), jnp.int32)],
        [received, small],
        share=3,
    )
    prior1 = from_behind(active1, "tm")
    decoded0, active0 = call(
        unpack_first_kernel, "unpack_first", [frame16] * 2, [received, small, vm(place)], share=0
    )
    prior0 = from_behind(active0, "tm")
    behind, far = vm(behind), vm(far)
    sum0, sum1 = call(
        local_conv_kernel,
        "local_conv",
        [frame32] * 2,
        [
            keep, small, vm(active0), vm(active1), vm(decoded0), vm(decoded1), vm(here), behind,
        ],
        share=3,
    )
    prior1 = vm(prior1)
    (second,) = call(
        second_residual_kernel,
        "second_residual",
        [frame16],
        [solo, keep, prior1, far, vm(sum1)],
        in_specs=[SM] + [VM] * 4,
        share=1,
    )
    prior_second = from_behind(second, "tm")
    (sum0,) = call(
        behind_kernel,
        "behind",
        [frame32],
        [solo, keep, prior1, behind, vm(sum0)],
        in_specs=[SM] + [VM] * 4,
        share=1,
    )
    (first,) = call(
        first_residual_kernel,
        "first_residual",
        [frame16],
        [solo, keep, vm(prior0), far, vm(sum0)],
        in_specs=[SM] + [VM] * 4,
        share=1,
    )
    prior_first = from_behind(first, "tm")
    times = vm(time_kernel)
    time0, time1 = call(
        local_time_kernel,
        "local_time",
        [pltpu.VMEM((pixels, wide), f32)] * 2,
        [keep, small, vm(first), vm(second), times],
        share=0.4,
    )
    frames = 2 * tokens // pixels
    shape = (frames, 2 * H, 2 * W * outs)
    up_scratch = [
        pltpu.VMEM((2 * pixels + 4 * H, 3 * channels), bf16),
        pltpu.VMEM((2, 2 * W * outs // 128, 2 * H, 128), f32),
    ]
    folded, prior_second = vm(folded), vm(prior_second)
    time0, time1 = vm(time0), vm(time1)
    half_shape = (frames // 2,) + shape[1:]
    (early,) = call(
        early_up_kernel,
        "early_up",
        [jax.ShapeDtypeStruct(shape, bf16)],
        [solo, small, time0, time1, folded],
        [pltpu.VMEM(shape, bf16)] + up_scratch + [sem((4,))],
        share=2,
        in_specs=[SM] + [VM] * 4,
        out_specs=[HB],
    )
    (later,) = call(
        second_up_kernel,
        "second_up",
        [pltpu.VMEM(half_shape, bf16)],
        [solo, keep, small, prior_second, times, time1, folded],
        up_scratch,
        share=6,
        in_specs=[SM] + [VM] * 6,
    )
    (made,) = call(
        first_up_kernel,
        "first_up",
        [jax.ShapeDtypeStruct(shape, bf16)],
        [
            solo, keep, small, vm(prior_first), prior_second, times, time0, folded, vm(later),
            early,
        ],
        [pltpu.VMEM(half_shape, bf16)] + up_scratch + [sem((3,))],
        share=6,
        in_specs=[SM] + [VM] * 8 + [pl.BlockSpec(memory_space=pl.ANY)],
        out_specs=[HB],
        input_output_aliases={9: 0},
    )
    return made


def solution(mesh):
    placed = (
        P(("groups", "tm"), None),
        P(("groups", "tm")),
        P("groups"),
        P(),
        P(),
        P(),
        P(),
        P(),
        P(),
        P(),
        P(),
    )
    return jax.shard_map(
        on_device,
        mesh=mesh,
        in_specs=placed,
        out_specs=P(("groups", "tm"), None, None),
        check_vma=False,
    )
```
